32 devices in a mesh: parts: 2 (over x), sub: 16 (over z, y, core).
Axes of the slice: x: 2, y: 2, z: 4, core: 2. Of those that a mesh axis runs over, the one named last changes fastest.
Arguments:
- right_side: float32 [32768, 256], P(('parts', 'sub')), parts along dimension 0, may hold values from -6 to 6
- face_weight: float32 [64, 512], P(('parts', 'sub')), parts along dimension 0, may hold values from 0.2 to 0.8
- schur: bfloat16 [65536, 1024], P(('parts', 'sub')), parts along dimension 0, as said below
- neumann: bfloat16 [65536, 1024], P(('parts', 'sub')), parts along dimension 0
- constraint: bfloat16 [2048, 512], P(('parts', 'sub')), parts along dimension 0, may hold values from -0.25 to 0.25
- coarse_inverse: bfloat16 [2048, 1024], P(('parts', 'sub')), parts along dimension 0
Outputs:
- solution: float32 [32768, 256], P(('parts', 'sub')), parts along dimension 0
- residual: float32 [32768, 256], P(('parts', 'sub')), parts along dimension 0
The draws below stay inside these ranges and needn't reach their ends.
There are 2 independent parts, one for each index of `parts`. The reference program is written for one: setup_inputs(seed, part) draws one part's arguments, and reference() takes and returns one part's arrays. A program takes and returns all parts, laid end to end along the dimension named above; each array names one. Nothing has to cross between parts.
Inputs may be any that keep to these rules, and one draw needn't show every extreme that they name: schur, neumann and coarse_inverse are symmetric, and each block schur_j, neumann_j and the whole coarse_inverse is positive definite.
All inputs are finite; a program needn't handle non-finite values.
Results may differ from the reference program's by a relative error of at most 0.0091.
Values may be sent and summed in bfloat16 or wider, within the bound.
No kernel may reach another device: no remote copies, remote signals or barrier semaphores. Data moves between devices by JAX's collectives and lax.ppermute only.
A program may use at most 64 MiB of HBM per device.

```python
import math
import jax
import jax.numpy as jnp
from jax import lax

NF = 512
NCF = 32
R = 256
ITERS = 2
NI = 1024
SUBS = 32
NCO = 1024


def spd_block(key, matrix_order):
    first_key, second_key = jax.random.split(key)
    entries = jax.random.normal(first_key, (matrix_order, matrix_order), jnp.float32)
    diagonal = jax.random.uniform(second_key, (matrix_order,), jnp.float32, 1.0, 3.0)
    symmetric = (entries + entries.T) / (2.0 * math.sqrt(2.0 * matrix_order))
    return jnp.diag(diagonal) + 0.9 * symmetric


def spd_stack(key, salt):
    keys = jax.random.split(jax.random.fold_in(key, salt), SUBS)
    blocks = lax.map(lambda block_key: spd_block(block_key, NI), keys)
    return blocks.reshape(SUBS * NI, NI).astype(jnp.bfloat16)


def draw_schur(key, part):
    return spd_stack(key, 11)


def draw_neumann(key, part):
    return spd_stack(key, 23)


def draw_coarse_inverse(key, part):
    return spd_block(jax.random.fold_in(key, 37), NCO).astype(jnp.bfloat16)


def levels(rng, dims, shards, smallest, high):
    loudness = 1.0
    for dim, blocks in shards:
        steps = jax.random.uniform(jax.random.fold_in(jax.random.fold_in(rng, 6), dim), (blocks,), jnp.float32, smallest / len(shards), high / len(shards))
        loudness = loudness * jnp.repeat(jnp.exp(steps), dims[dim] // blocks).reshape((-1,) + (1,) * (len(dims) - 1 - dim))
    return loudness


def gaussian(own_key, dims, deviation, limit, cuts=(), dtype=jnp.bfloat16):
    array = jax.random.normal(own_key, dims, jnp.float32) * deviation
    if len(cuts) > 0:
        array = levels(own_key, dims, cuts, -0.22, 0.18) * array
    return jnp.clip(array, min=-limit, max=limit).astype(dtype)


def setup_inputs(seed: int = 0, part: int = 0) -> dict:
    key_list = jax.random.split(jax.random.key(seed), 7)
    own_keys = jax.random.split(jax.random.fold_in(key_list[6], part), 7)
    return {
        "right_side": gaussian(own_keys[0], (SUBS * NF, R), 1.0, 6.0, ((0, 16),), jnp.float32),
        "face_weight": jnp.clip(0.2 + 0.6 * jax.random.uniform(own_keys[1], (SUBS, NF), jnp.float32) ** levels(own_keys[1], (SUBS, NF), ((0, 16),), -0.2, 0.2), 0.2, 0.8),
        "schur": draw_schur(jax.random.fold_in(jax.random.fold_in(key_list[6], part), 71), part),
        "neumann": draw_neumann(jax.random.fold_in(jax.random.fold_in(key_list[6], part), 71), part),
        "constraint": gaussian(own_keys[4], (SUBS * NCF, NF), NF ** -0.5, 0.25, ((0, 16),)),
        "coarse_inverse": draw_coarse_inverse(jax.random.fold_in(jax.random.fold_in(key_list[6], part), 71), part),
    }


def couple(matrices, left_part, right_part):
    stacked = jnp.concatenate([left_part, right_part], axis=1)
    return lax.map(lambda operands: jnp.dot(operands[0], operands[1], preferred_element_type=jnp.float32), (matrices, stacked))


def schur_apply(blocks, vector):
    rounded = vector.astype(jnp.bfloat16)
    output = couple(blocks, jnp.roll(rounded, 1, axis=0), rounded)
    return output[:, NF:] + jnp.roll(output[:, :NF], -1, axis=0)


def neumann_apply(blocks, weights, vector):
    right_part = (weights * vector).astype(jnp.bfloat16)
    left_source = ((1.0 - weights) * vector).astype(jnp.bfloat16)
    output = couple(blocks, jnp.roll(left_source, 1, axis=0), right_part)
    return weights * output[:, NF:] + (1.0 - weights) * jnp.roll(output[:, :NF], -1, axis=0)


def precondition(neumann_blocks, weights, rows_constraint, coarse_inverse, vector):
    local_part = neumann_apply(neumann_blocks, weights, vector)
    rounded = vector.astype(jnp.bfloat16)
    coarse_input = jnp.einsum("jqf,jfr->jqr", rows_constraint.astype(jnp.float32), rounded.astype(jnp.float32)).astype(jnp.bfloat16)
    coarse_solution = jnp.dot(coarse_inverse, coarse_input.reshape(NCO, R), preferred_element_type=jnp.float32).astype(jnp.bfloat16)
    coarse_solution = coarse_solution.reshape(SUBS, NCF, R)
    correction = jnp.einsum("jqf,jqr->jfr", rows_constraint.astype(jnp.float32), coarse_solution.astype(jnp.float32))
    return local_part + correction


def reference(right_side, face_weight, schur, neumann, constraint, coarse_inverse):
    schur_blocks = schur.reshape(SUBS, NI, NI)
    neumann_blocks = neumann.reshape(SUBS, NI, NI)
    rows_constraint = constraint.reshape(SUBS, NCF, NF)
    weights = face_weight.reshape(SUBS, NF, 1)
    residual = right_side.reshape(SUBS, NF, R)
    solution = jnp.zeros_like(residual)
    precond = precondition(neumann_blocks, weights, rows_constraint, coarse_inverse, residual)
    direction = precond
    norm_now = jnp.sum(residual * precond, axis=(0, 1))
    for iteration in range(ITERS):
        product_image = schur_apply(schur_blocks, direction)
        step_size = norm_now / jnp.sum(direction * product_image, axis=(0, 1))
        solution = solution + step_size * direction
        residual = residual - step_size * product_image
        if iteration + 1 < ITERS:
            precond = precondition(neumann_blocks, weights, rows_constraint, coarse_inverse, residual)
            norm_next = jnp.sum(residual * precond, axis=(0, 1))
            direction = precond + (norm_next / norm_now) * direction
            norm_now = norm_next
    return solution.reshape(SUBS * NF, R), residual.reshape(SUBS * NF, R)
```

```python
import jax
import jax.numpy as jnp
from jax import lax
from jax.sharding import PartitionSpec as P

AXIS = "sub"
BF16 = jnp.bfloat16
F32 = jnp.float32


def shifted(block, distance):
    n = lax.axis_size(AXIS)
    return lax.ppermute(block, AXIS, [((i - distance) % n, i) for i in range(n)])


def partner_block(block):
    n = lax.axis_size(AXIS)
    return lax.ppermute(block, AXIS, [(i, i ^ 1) for i in range(n)])


def gather_relative(block):
    n = lax.axis_size(AXIS)
    if n % 2:
        return jnp.concatenate([block] + [shifted(block, k) for k in range(1, n)], axis=0)
    same = jnp.concatenate([block] + [shifted(block, 2 * k) for k in range(1, n // 2)], axis=0)
    return jnp.concatenate([same, partner_block(same)], axis=0)


def relative_columns(rows):
    n = lax.axis_size(AXIS)
    me = lax.axis_index(AXIS)
    count, width = rows.shape[0], rows.shape[1] // n
    group = 1 if n % 2 else 2
    pairs = rows.reshape(count, n // group, group, width)[:, ::-1]
    first = n // group - 1 - me // group
    doubled = jnp.concatenate([pairs, pairs], axis=1)
    turned = lax.dynamic_slice_in_dim(doubled, first, n // group, axis=1)
    if group == 2:
        turned = jnp.where(me % 2 == 0, turned, turned[:, :, ::-1])
    return turned.transpose(0, 2, 1, 3).reshape(count, n * width)


def sum_all(block):
    n = lax.axis_size(AXIS)
    total = block
    for k in range(1, n):
        total = total + shifted(block, k)
    return total


def dot(a, b):
    return jnp.dot(a, b, preferred_element_type=F32)


def split_dot(a, b):
    high = lax.reduce_precision(b, 8, 7)
    return dot(a, high.astype(BF16)) + dot(a, (b - high).astype(BF16))


def combine(first, second, back, forward):
    faces = [first[0] + forward]
    for j in range(1, len(first)):
        faces.append(second[j - 1] + first[j])
    faces.append(second[-1] + back)
    return faces


def exchange(first, second):
    back = shifted(first[0].astype(BF16), -1).astype(F32)
    forward = shifted(second[-1].astype(BF16), 1).astype(F32)
    return combine(first, second, back, forward)


def shards(right_side, face_weight, schur, neumann, constraint, coarse_inverse):
    subs, nf = face_weight.shape
    ni = 2 * nf
    ncf = constraint.shape[0] // subs
    columns = right_side.shape[1]
    schur_blocks = [schur[j * ni : (j + 1) * ni] for j in range(subs)]
    neumann_blocks = [neumann[j * ni : (j + 1) * ni] for j in range(subs)]
    load = [right_side[j * nf : (j + 1) * nf] for j in range(subs)]
    own_rows = [constraint[j * ncf : (j + 1) * ncf] for j in range(subs)]

    coarse = jnp.concatenate([dot(own_rows[j], load[j].astype(BF16)) for j in range(subs)], axis=0).astype(BF16)
    weight = [face_weight[j].reshape(nf, 1) for j in range(subs)]
    halo_source = shifted(((1.0 - weight[-1]) * load[-1]).astype(BF16), 1)
    coarse_all = gather_relative(coarse)
    weight = [shifted(face_weight[-1:], 1).reshape(nf, 1)] + weight
    rows = [shifted(own_rows[-1], 1)] + own_rows
    inverse = relative_columns(jnp.concatenate([shifted(coarse_inverse[-ncf:], 1), coarse_inverse], axis=0))

    def neumann_halves(left, right):
        first, second = [], []
        for j in range(subs):
            product = dot(neumann_blocks[j], jnp.concatenate([left[j], right[j]], axis=0))
            first.append((1.0 - weight[j]) * product[:nf])
            second.append(weight[j + 1] * product[nf:])
        return first, second

    def add_coarse(faces, coarse_all):
        x = dot(inverse, coarse_all)
        return [face + split_dot(rows[j].T, x[j * ncf : (j + 1) * ncf]) for j, face in enumerate(faces)]

    def schur_halves(faces):
        first, second = [], []
        for j in range(subs):
            product = split_dot(schur_blocks[j], jnp.concatenate([faces[j], faces[j + 1]], axis=0))
            first.append(product[:nf])
            second.append(product[nf:])
        return first, second

    def energy(faces, first, second):
        total = 0.0
        for j in range(subs):
            total = total + jnp.sum(faces[j] * first[j], axis=0) + jnp.sum(faces[j + 1] * second[j], axis=0)
        return total

    def inner(a, b):
        return sum(jnp.sum(x * y, axis=0) for x, y in zip(a, b))

    left = [halo_source] + [((1.0 - weight[j + 1]) * load[j]).astype(BF16) for j in range(subs - 1)]
    right = [(weight[j + 1] * load[j]).astype(BF16) for j in range(subs)]
    z = add_coarse(exchange(*neumann_halves(left, right)), coarse_all)
    first, second = schur_halves(z)
    load_z, z_image = inner(load, z[1:]), energy(z, first, second)
    coarse_back = shifted(split_dot(rows[0], first[0]), -1)
    parts = [split_dot(rows[j], second[j - 1] + first[j]) for j in range(1, subs)]
    parts.append(split_dot(rows[subs], second[-1]) + coarse_back)
    coarse_all = gather_relative(jnp.concatenate(parts, axis=0).astype(BF16))
    image = exchange(first, second)
    left = [((1.0 - weight[j]) * image[j]).astype(BF16) for j in range(subs)]
    right = [(weight[j + 1] * image[j + 1]).astype(BF16) for j in range(subs)]
    y = add_coarse(exchange(*neumann_halves(left, right)), coarse_all)
    first, second = schur_halves(y)
    image_y, y_image = inner(image[1:], y[1:]), energy(y, first, second)
    a, b, c, d = sum_all(jnp.stack([load_z, z_image, image_y, y_image], axis=0))
    image_y_faces = exchange(first, second)[1:]

    step = a / b
    grow = step * (c / b)
    next_step = (grow - 1.0) / ((d - c * (c / b)) * (step / b))
    s = step + next_step * grow
    t = step * next_step
    solution = jnp.concatenate([s * z[j + 1] - t * y[j + 1] for j in range(subs)], axis=0)
    residual = jnp.concatenate([load[j] - s * image[j + 1] + t * image_y_faces[j] for j in range(subs)], axis=0)
    return solution, residual


def solution(mesh):
    specs = P(("parts", AXIS), None)
    return jax.shard_map(shards, mesh=mesh, in_specs=(specs,) * 6, out_specs=(specs, specs), check_vma=False)
```

```python
import jax
import jax.numpy as jnp
from jax import lax
from jax.sharding import PartitionSpec as P

AXIS = "sub"
BF16 = jnp.bfloat16
F32 = jnp.float32


def shifted(block, distance):
    n = lax.axis_size(AXIS)
    return lax.ppermute(block, AXIS, [((i - distance) % n, i) for i in range(n)])


def from_all(block):
    n = lax.axis_size(AXIS)
    return lax.all_to_all(jnp.broadcast_to(block[None], (n,) + block.shape), AXIS, 0, 0)


def exact_parts(x):
    high = lax.reduce_precision(x, 8, 7)
    middle = lax.reduce_precision(x - high, 8, 7)
    return [part.astype(BF16) for part in (high, middle, x - high - middle)]


def halo(load, weight, rows, inverse):
    columns = load.shape[1]
    pieces = [load]
    for array in [rows, inverse] + exact_parts(weight):
        pieces += [array[:, k : k + columns] for k in range(0, array.shape[1], columns)]
    heights = [piece.shape[0] for piece in pieces]
    got = shifted(jnp.concatenate(pieces, axis=0), 1)
    parts, at = [], 0
    for height in heights:
        parts.append(got[at : at + height])
        at += height
    results, at = [], 1
    for array in [rows, inverse, weight, weight, weight]:
        count = array.shape[1] // columns
        results.append(jnp.concatenate(parts[at : at + count], axis=1))
        at += count
    return parts[0], results[0], results[1], sum(part.astype(F32) for part in results[2:])


def dot(a, b):
    return jnp.dot(a, b, preferred_element_type=F32)


def split_dot(a, b):
    high = lax.reduce_precision(b, 8, 7)
    return dot(a, high.astype(BF16)) + dot(a, (b - high).astype(BF16))


def combine(first, second, back, forward):
    faces = [first[0] + forward]
    for j in range(1, len(first)):
        faces.append(second[j - 1] + first[j])
    faces.append(second[-1] + back)
    return faces


def exchange(first, second):
    back = shifted(first[0].astype(BF16), -1).astype(F32)
    forward = shifted(second[-1].astype(BF16), 1).astype(F32)
    return combine(first, second, back, forward)


def shards(right_side, face_weight, schur, neumann, constraint, coarse_inverse):
    subs, nf = face_weight.shape
    ni = 2 * nf
    ncf = constraint.shape[0] // subs
    columns = right_side.shape[1]
    schur_blocks = [schur[j * ni : (j + 1) * ni] for j in range(subs)]
    neumann_blocks = [neumann[j * ni : (j + 1) * ni] for j in range(subs)]
    load = [right_side[j * nf : (j + 1) * nf] for j in range(subs)]
    own_rows = [constraint[j * ncf : (j + 1) * ncf] for j in range(subs)]

    coarse = jnp.concatenate([dot(own_rows[j], load[j].astype(BF16)) for j in range(subs)], axis=0).astype(BF16)
    coarse_all = from_all(coarse).reshape(-1, columns)
    weight = [face_weight[j].reshape(nf, 1) for j in range(subs)]
    halo_source, halo_rows, halo_inverse, halo_weight = halo(
        ((1.0 - weight[-1]) * load[-1]).astype(BF16), face_weight[-1:], own_rows[-1], coarse_inverse[-ncf:]
    )
    weight = [halo_weight.reshape(nf, 1)] + weight
    rows = [halo_rows] + own_rows
    inverse = jnp.concatenate([halo_inverse, coarse_inverse], axis=0)

    def neumann_halves(left, right):
        first, second = [], []
        for j in range(subs):
            product = dot(neumann_blocks[j], jnp.concatenate([left[j], right[j]], axis=0))
            first.append((1.0 - weight[j]) * product[:nf])
            second.append(weight[j + 1] * product[nf:])
        return first, second

    def add_coarse(faces, coarse_all):
        x = dot(inverse, coarse_all)
        return [face + split_dot(rows[j].T, x[j * ncf : (j + 1) * ncf]) for j, face in enumerate(faces)]

    def schur_halves(faces):
        first, second = [], []
        for j in range(subs):
            product = split_dot(schur_blocks[j], jnp.concatenate([faces[j], faces[j + 1]], axis=0))
            first.append(product[:nf])
            second.append(product[nf:])
        return first, second

    def energy(faces, first, second):
        total = 0.0
        for j in range(subs):
            total = total + jnp.sum(faces[j] * first[j], axis=0) + jnp.sum(faces[j + 1] * second[j], axis=0)
        return total

    def inner(a, b):
        return sum(jnp.sum(x * y, axis=0) for x, y in zip(a, b))

    left = [halo_source] + [((1.0 - weight[j + 1]) * load[j]).astype(BF16) for j in range(subs - 1)]
    right = [(weight[j + 1] * load[j]).astype(BF16) for j in range(subs)]
    z = add_coarse(exchange(*neumann_halves(left, right)), coarse_all)
    first, second = schur_halves(z)
    load_z, z_image = inner(load, z[1:]), energy(z, first, second)
    coarse_back = shifted(split_dot(rows[0], first[0]), -1)
    parts = [split_dot(rows[j], second[j - 1] + first[j]) for j in range(1, subs)]
    parts.append(split_dot(rows[subs], second[-1]) + coarse_back)
    coarse_all = from_all(jnp.concatenate(parts, axis=0).astype(BF16)).reshape(-1, columns)
    image = exchange(first, second)
    left = [((1.0 - weight[j]) * image[j]).astype(BF16) for j in range(subs)]
    right = [(weight[j + 1] * image[j + 1]).astype(BF16) for j in range(subs)]
    y = add_coarse(exchange(*neumann_halves(left, right)), coarse_all)
    first, second = schur_halves(y)
    image_y, y_image = inner(image[1:], y[1:]), energy(y, first, second)
    a, b, c, d = jnp.sum(from_all(jnp.stack([load_z, z_image, image_y, y_image], axis=0)), axis=0)
    image_y_faces = exchange(first, second)[1:]

    step = a / b
    grow = step * (c / b)
    next_step = (grow - 1.0) / ((d - c * (c / b)) * (step / b))
    s = step + next_step * grow
    t = step * next_step
    solution = jnp.concatenate([s * z[j + 1] - t * y[j + 1] for j in range(subs)], axis=0)
    residual = jnp.concatenate([load[j] - s * image[j + 1] + t * image_y_faces[j] for j in range(subs)], axis=0)
    return solution, residual


def solution(mesh):
    specs = P(("parts", AXIS), None)
    return jax.shard_map(shards, mesh=mesh, in_specs=(specs,) * 6, out_specs=(specs, specs), check_vma=False)
```

```python
import functools

import jax
import jax.numpy as jnp
from jax import lax
from jax.experimental import pallas as pl
from jax.experimental.pallas import tpu as pltpu
from jax.sharding import PartitionSpec as P

AXIS = "sub"
BF16 = jnp.bfloat16
F32 = jnp.float32
LANES = 128
VMEM_BYTES = 48 * 2**20


def shifted(block, distance):
    n = lax.axis_size(AXIS)
    return lax.ppermute(block, AXIS, [((i - distance) % n, i) for i in range(n)])


def from_all(copies):
    return lax.all_to_all(copies, AXIS, 0, 0)


def dot(a, b):
    return jnp.dot(a, b, preferred_element_type=F32)


def dot_nt(a, b):
    return lax.dot_general(a, b, (((1,), (1,)), ((), ())), preferred_element_type=F32)


def dot_tn(a, b):
    return lax.dot_general(a, b, (((0,), (0,)), ((), ())), preferred_element_type=F32)


def split(x):
    high = x.astype(BF16)
    return high, (x - high.astype(F32)).astype(BF16)


def split_dot(a, b, contract=dot):
    high, low = split(b)
    if isinstance(a, tuple):
        return contract(a[0], high) + contract(a[0], low) + contract(a[1], high)
    return contract(a, high) + contract(a, low)


def column_sum(x):
    return jnp.sum(x, axis=0, keepdims=True)


def rows_of(ref, index, count):
    return ref[index * count : (index + 1) * count]


def stage(kernel, shapes, *operands):
    out = [jax.ShapeDtypeStruct(shape, dtype) for shape, dtype in shapes]
    params = pltpu.CompilerParams(vmem_limit_bytes=VMEM_BYTES)
    return pl.pallas_call(kernel, out_shape=out, compiler_params=params, name=kernel.func.__name__)(*operands)


def prepare(subs, load, weight, weight_rows, rows, inverse, copies, coarse, message):
    nf, columns = load.shape[0] // subs, load.shape[1]
    ncf = rows.shape[0] // subs
    for j in range(subs):
        coarse[j * ncf : (j + 1) * ncf] = dot(rows_of(rows, j, ncf), rows_of(load, j, nf).astype(BF16))
    rounded = coarse[...].astype(BF16)
    for k in range(copies.shape[0]):
        copies[k] = rounded
    last = slice((subs - 1) * nf, subs * nf)
    message[:nf] = ((1.0 - weight[last]) * load[last]).astype(BF16)
    at = nf
    for array in (rows, inverse):
        for k in range(0, array.shape[1], columns):
            message[at : at + ncf] = array[(subs - 1) * ncf :, k : k + columns]
            at += ncf
    message[at:] = weight_rows[...]


def neumann_products(subs, nf, left, right, weight, neumann, part, back, forward):
    previous = None
    for j in range(subs):
        product = dot(rows_of(neumann, j, 2 * nf), jnp.concatenate([left[j], right[j]], axis=0))
        first, second = product[:nf], product[nf:]
        if j == 0:
            part[:nf] = first
            back[...] = first.astype(BF16)
        else:
            own = weight(j)
            part[j * nf : (j + 1) * nf] = own * previous + (1.0 - own) * first
        previous = second
    part[subs * nf :] = previous
    forward[...] = previous.astype(BF16)


def neumann_load(subs, load, weight, halo_left, neumann, part, back, forward):
    nf = load.shape[0] // subs
    own = lambda e: rows_of(weight, e - 1, nf)
    left = [halo_left[...]] + [((1.0 - own(j)) * rows_of(load, j - 1, nf)).astype(BF16) for j in range(1, subs)]
    right = [(own(j + 1) * rows_of(load, j, nf)).astype(BF16) for j in range(subs)]
    neumann_products(subs, nf, left, right, own, neumann, part, back, forward)


def neumann_image(subs, part_in, from_next, from_previous, weight, neumann, image, part, back, forward):
    nf = part_in.shape[0] // (subs + 1)
    faces = [rows_of(part_in, e, nf) for e in range(subs + 1)]
    faces[0] = faces[0] + from_previous[...].astype(F32)
    faces[subs] = faces[subs] + from_next[...].astype(F32)
    for e in range(1, subs + 1):
        image[(e - 1) * nf : e * nf] = faces[e]
    own = lambda e: rows_of(weight, e, nf)
    left = [((1.0 - own(j)) * faces[j]).astype(BF16) for j in range(subs)]
    right = [(own(j + 1) * faces[j + 1]).astype(BF16) for j in range(subs)]
    neumann_products(subs, nf, left, right, own, neumann, part, back, forward)


def schur_products(subs, nf, other, part, from_next, from_previous, weight, schur, local, product, quadratic):
    own = lambda e: rows_of(weight, e, nf)
    local[:nf] = (1.0 - own(0)) * part[:nf] + own(0) * from_previous[...].astype(F32)
    for e in range(1, subs):
        local[e * nf : (e + 1) * nf] = rows_of(part, e, nf)
    local[subs * nf :] = own(subs) * part[subs * nf :] + (1.0 - own(subs)) * from_next[...].astype(F32)
    columns = local.shape[1]
    energy, previous = 0.0, None
    for j in range(subs):
        vector = local[j * nf : (j + 2) * nf]
        both = dot(rows_of(schur, j, 2 * nf), jnp.concatenate(split(vector), axis=1))
        result = both[:, :columns] + both[:, columns:]
        energy = energy + column_sum(vector * result)
        first = result[:nf]
        product[j * nf : (j + 1) * nf] = first if j == 0 else previous + first
        previous = result[nf:]
    product[subs * nf :] = previous
    quadratic[0:1] = energy
    quadratic[1:2] = column_sum(other[...] * local[nf:])


def schur_load(
    subs, load, part, from_next, from_previous, weight, schur, rows,
    local, product, quadratic, basis_high, basis_low, base, gram, message,
):
    nf = part.shape[0] // (subs + 1)
    ncf = rows.shape[0] // (subs + 1)
    schur_products(subs, nf, load, part, from_next, from_previous, weight, schur, local, product, quadratic)
    gram[...] = jnp.zeros_like(gram)
    for j in range(subs):
        matrix = rows_of(schur, j, 2 * nf)
        left, right = rows_of(rows, j, ncf), rows_of(rows, j + 1, ncf)
        basis = jnp.concatenate([dot(left, matrix[:nf]), dot(right, matrix[nf:])], axis=0)
        pair = split(basis)
        here = slice(2 * j * ncf, 2 * (j + 1) * ncf)
        basis_high[here], basis_low[here] = pair
        base[here] = split_dot(pair, local[j * nf : (j + 2) * nf])
        for side, block in ((0, left), (1, right)):
            half = slice(side * nf, (side + 1) * nf)
            gram[here, side * ncf : (side + 1) * ncf] = dot_nt(pair[0][:, half], block) + dot_nt(pair[1][:, half], block)
    message[:, : base.shape[1]] = base[:ncf]
    message[:, base.shape[1] :] = gram[:ncf]


def coarse_products(subs, ncf, x, base, gram):
    results, energy = [], 0.0
    for j in range(subs):
        here = slice(2 * j * ncf, 2 * (j + 1) * ncf)
        pair = jnp.concatenate([x[j], x[j + 1]], axis=0)
        change = split_dot(split(gram[here, : 2 * ncf]), pair)
        energy = energy + column_sum(pair * (2.0 * base[here] + change))
        results.append(base[here] + change)
    return results, energy


def add_basis(subs, nf, ncf, x, basis_high, basis_low, product):
    faces = [rows_of(product, e, nf) for e in range(subs + 1)]
    for j in range(subs):
        here = slice(2 * j * ncf, 2 * (j + 1) * ncf)
        pair = jnp.concatenate([x[j], x[j + 1]], axis=0)
        change = split_dot((basis_high[here], basis_low[here]), pair, dot_tn)
        faces[j] = faces[j] + change[:nf]
        faces[j + 1] = faces[j + 1] + change[nf:]
    return faces


def coarse_load(
    subs, coarse_all, inverse, halo_inverse, next_inverse, from_next, coarse, base, gram, quadratic, basis_high, basis_low, product,
    copies, image_coarse, solution, part, back, forward, sums,
):
    ncf = inverse.shape[0] // subs
    nf = product.shape[0] // (subs + 1)
    columns = coarse.shape[1]
    everything = coarse_all[...]
    own = dot(inverse[...], everything)
    x = [dot(halo_inverse[...], everything)] + [own[j * ncf : (j + 1) * ncf] for j in range(subs)]
    beyond = dot(next_inverse[...], everything)
    results, energy = coarse_products(subs, ncf, x, base, gram)
    for e in range(1, subs):
        image_coarse[(e - 1) * ncf : e * ncf] = results[e - 1][ncf:] + results[e][:ncf]
    share = from_next[:, :columns] + split_dot(
        split(from_next[:, columns : columns + 2 * ncf]), jnp.concatenate([x[subs], beyond], axis=0)
    )
    image_coarse[(subs - 1) * ncf :] = results[subs - 1][ncf:] + share
    rounded = image_coarse[...].astype(BF16)
    for k in range(copies.shape[0]):
        copies[k] = rounded
    for e in range(subs + 1):
        solution[e * ncf : (e + 1) * ncf] = x[e]
    sums[0:1] = quadratic[1:2] + column_sum(coarse[...] * own)
    sums[1:2] = quadratic[0:1] + energy
    faces = add_basis(subs, nf, ncf, x, basis_high, basis_low, product)
    for e in range(subs + 1):
        part[e * nf : (e + 1) * nf] = faces[e]
    back[...] = faces[0].astype(BF16)
    forward[...] = faces[subs].astype(BF16)


def schur_image(
    subs, image, part, from_next, from_previous, weight, schur, basis_high, basis_low, local, product, quadratic, base
):
    nf = part.shape[0] // (subs + 1)
    ncf = basis_high.shape[0] // (2 * subs)
    schur_products(subs, nf, image, part, from_next, from_previous, weight, schur, local, product, quadratic)
    for j in range(subs):
        here = slice(2 * j * ncf, 2 * (j + 1) * ncf)
        base[here] = split_dot((basis_high[here], basis_low[here]), local[j * nf : (j + 2) * nf])


def coarse_image(
    subs, coarse_all, inverse, halo_inverse, coarse, base, gram, quadratic, basis_high, basis_low, product, sums,
    copies, solution, part, back,
):
    ncf = inverse.shape[0] // subs
    nf = product.shape[0] // (subs + 1)
    everything = coarse_all[...]
    own = dot(inverse[...], everything)
    x = [dot(halo_inverse[...], everything)] + [own[j * ncf : (j + 1) * ncf] for j in range(subs)]
    _, energy = coarse_products(subs, ncf, x, base, gram)
    third = quadratic[1:2] + column_sum(coarse[...] * own)
    fourth = quadratic[0:1] + energy
    for k in range(copies.shape[0]):
        copies[k, 0:2] = sums[0:2]
        copies[k, 2:3] = third
        copies[k, 3:4] = fourth
    solution[...] = own
    faces = add_basis(subs, nf, ncf, x, basis_high, basis_low, product)
    for e in range(1, subs + 1):
        part[(e - 1) * nf : e * nf] = faces[e]
    back[...] = faces[0].astype(BF16)


def combine(subs, sums, load, z_local, z_coarse, y_local, y_coarse, rows, image, part, from_next, solution, residual):
    nf = load.shape[0] // subs
    ncf = rows.shape[0] // (subs + 1)
    total = sums[0]
    for k in range(1, sums.shape[0]):
        total = total + sums[k]
    a, b, c, d = (total[k : k + 1] for k in range(4))
    step = a / b
    grow = step * (c / b)
    next_step = (grow - 1.0) / ((d - c * (c / b)) * (step / b))
    s = step + next_step * grow
    t = step * next_step
    for j in range(subs):
        here, beside = slice(j * nf, (j + 1) * nf), slice((j + 1) * nf, (j + 2) * nf)
        block = rows_of(rows, j + 1, ncf)
        x = s * rows_of(z_coarse, j + 1, ncf) - t * rows_of(y_coarse, j, ncf)
        solution[here] = s * z_local[beside] - t * y_local[beside] + split_dot(block, x, dot_tn)
        last = part[here]
        if j == subs - 1:
            last = last + from_next[...].astype(F32)
        residual[here] = load[here] - s * image[here] + t * last


def exact_parts(x):
    high = lax.reduce_precision(x, 8, 7)
    middle = lax.reduce_precision(x - high, 8, 7)
    return [part.astype(BF16) for part in (high, middle, x - high - middle)]


def shards(right_side, face_weight, schur, neumann, constraint, coarse_inverse):
    subs, nf = face_weight.shape
    ncf = constraint.shape[0] // subs
    nco = coarse_inverse.shape[1]
    columns = right_side.shape[1]
    n = lax.axis_size(AXIS)
    bind = lambda kernel: functools.partial(kernel, subs)
    face, faces, own = (nf, columns), ((subs + 1) * nf, columns), (subs * nf, columns)
    coarse_own, basis = (subs * ncf, columns), (2 * subs * ncf, 2 * nf)
    copies = ((n,) + coarse_own, BF16)

    weight = face_weight.reshape(subs * nf, 1)
    pieces = jnp.concatenate([part.reshape(-1, columns) for part in exact_parts(face_weight[-1:])], axis=0)
    count = pieces.shape[0]
    padded = -(-count // 16) * 16
    weight_rows = jnp.pad(pieces, ((0, padded - count), (0, 0)))
    row_count, inverse_count = ncf * nf // columns, ncf * nco // columns
    message_rows = nf + row_count + inverse_count + padded
    coarse_copies, coarse, message = stage(
        bind(prepare), [copies, (coarse_own, F32), ((message_rows, columns), BF16)],
        right_side, weight, weight_rows, constraint, coarse_inverse,
    )
    got = shifted(message, 1)
    coarse_all = from_all(coarse_copies).reshape(nco, columns)
    next_inverse = shifted(coarse_inverse[:ncf], -1)

    def unfolded(start, stop):
        return jnp.concatenate([got[k : k + ncf] for k in range(start, stop, ncf)], axis=1)

    halo_left = got[:nf]
    rows = jnp.concatenate([unfolded(nf, nf + row_count), constraint], axis=0)
    halo_inverse = unfolded(nf + row_count, nf + row_count + inverse_count)
    third = count // 3
    got_weight = got[nf + row_count + inverse_count :].astype(F32)
    halo_weight = sum(got_weight[k * third : (k + 1) * third] for k in range(3)).reshape(nf, 1)
    weight_all = jnp.concatenate([halo_weight, weight], axis=0)

    halves = [(face, BF16), (face, BF16)]
    part, back, forward = stage(bind(neumann_load), [(faces, F32)] + halves, right_side, weight, halo_left, neumann)
    back, forward = shifted(back, -1), shifted(forward, 1)
    local, product, quadratic, basis_high, basis_low, base, gram, message = stage(
        bind(schur_load),
        [(faces, F32), (faces, F32), ((8, columns), F32), (basis, BF16), (basis, BF16), ((basis[0], columns), F32),
         ((basis[0], LANES), F32), ((ncf, columns + LANES), F32)],
        right_side, part, back, forward, weight_all, schur, rows,
    )
    from_next = shifted(message, -1)
    coarse_copies, coarse, z_coarse, part, back, forward, sums = stage(
        bind(coarse_load),
        [copies, (coarse_own, F32), (((subs + 1) * ncf, columns), F32), (faces, F32)] + halves + [((8, columns), F32)],
        coarse_all, coarse_inverse, halo_inverse, next_inverse, from_next, coarse, base, gram, quadratic,
        basis_high, basis_low, product,
    )
    back, forward = shifted(back, -1), shifted(forward, 1)
    coarse_all = from_all(coarse_copies).reshape(nco, columns)
    image, part, back, forward = stage(
        bind(neumann_image), [(own, F32), (faces, F32)] + halves, part, back, forward, weight_all, neumann
    )
    back, forward = shifted(back, -1), shifted(forward, 1)
    y_local, product, quadratic, base = stage(
        bind(schur_image), [(faces, F32), (faces, F32), ((8, columns), F32), ((basis[0], columns), F32)],
        image, part, back, forward, weight_all, schur, basis_high, basis_low,
    )
    sum_copies, y_coarse, part, back = stage(
        bind(coarse_image), [((n, 4, columns), F32), (coarse_own, F32), (own, F32), (face, BF16)],
        coarse_all, coarse_inverse, halo_inverse, coarse, base, gram, quadratic, basis_high, basis_low, product, sums,
    )
    sums = from_all(sum_copies)
    back = shifted(back, -1)
    return stage(
        bind(combine), [(own, F32), (own, F32)],
        sums, right_side, local, z_coarse, y_local, y_coarse, rows, image, part, back,
    )


def solution(mesh):
    specs = P(("parts", AXIS), None)
    return jax.shard_map(shards, mesh=mesh, in_specs=(specs,) * 6, out_specs=(specs, specs), check_vma=False)
```

```python
import functools

import jax
import jax.numpy as jnp
from jax import lax
from jax.experimental import pallas as pl
from jax.experimental.pallas import tpu as pltpu
from jax.sharding import PartitionSpec as P

AXIS = "sub"
BF16 = jnp.bfloat16
F32 = jnp.float32
LANES = 128
VMEM_BYTES = 20 * 2**20


def shifted(block, distance):
    n = lax.axis_size(AXIS)
    return lax.ppermute(block, AXIS, [((i - distance) % n, i) for i in range(n)])


def crossed(block, bit):
    return lax.ppermute(block, AXIS, [(i, i ^ bit) for i in range(lax.axis_size(AXIS))])


def bits():
    return [1 << k for k in reversed(range(lax.axis_size(AXIS).bit_length() - 1))]


def gather_halves(block):
    for bit in bits()[:-1]:
        block = jnp.concatenate([block, crossed(block, bit)], axis=0)
    return block, crossed(block, 1)


def half_order():
    order = [0]
    for bit in bits()[:-1]:
        order += [place ^ bit for place in order]
    return order


def sum_all(block):
    for bit in bits():
        block = block + crossed(block, bit)
    return block


def dot(a, b):
    return jnp.dot(a, b, preferred_element_type=F32)


def dot_nt(a, b):
    return lax.dot_general(a, b, (((1,), (1,)), ((), ())), preferred_element_type=F32)


def dot_tn(a, b):
    return lax.dot_general(a, b, (((0,), (0,)), ((), ())), preferred_element_type=F32)


def split(x):
    high = x.astype(BF16)
    return high, (x - high.astype(F32)).astype(BF16)


def split_dot(a, b, contract=dot):
    high, low = split(b)
    if isinstance(a, tuple):
        return contract(a[0], high) + contract(a[0], low) + contract(a[1], high)
    return contract(a, high) + contract(a, low)


def column_sum(x):
    return jnp.sum(x, axis=0, keepdims=True)


def rows_of(ref, index, count):
    return ref[index * count : (index + 1) * count]


def column_of(row):
    return jnp.broadcast_to(row, (8, row.shape[1])).T[:, :1]


def parts_of(row):
    high = row.astype(BF16).astype(F32)
    middle = (row - high).astype(BF16).astype(F32)
    return high, middle, row - high - middle


class Halo:
    def __init__(self, nf, ncf, nco, columns):
        self.nf, self.ncf, self.columns = nf, ncf, columns
        self.folds = nf // columns
        self.at_rows = nf
        self.at_inverse = nf + ncf * self.folds
        self.at_weight = self.at_inverse + ncf * (nco // columns)
        self.weight_count = -(-3 * self.folds // 16) * 16
        self.height = self.at_weight + self.weight_count

    def load(self, message):
        return message[: self.nf]

    def pieces(self, message, start, stop):
        return [message[k : k + self.ncf] for k in range(start, stop, self.ncf)]

    def rows(self, message):
        return jnp.concatenate(self.pieces(message, self.at_rows, self.at_inverse), axis=1)

    def inverse(self, message):
        return jnp.concatenate(self.pieces(message, self.at_inverse, self.at_weight), axis=1)

    def weight(self, message):
        got = message[self.at_weight : self.height].astype(F32)
        f = self.folds
        row = [sum(got[k * f + i : k * f + i + 1] for k in range(3)) for i in range(f)]
        return jnp.concatenate([column_of(piece) for piece in row], axis=0)


def all_rows(halo, message, rows):
    ncf = halo.ncf
    return [halo.rows(message)] + [rows_of(rows, j, ncf) for j in range(rows.shape[0] // ncf)]


def all_weights(halo, message, weight):
    return [halo.weight(message)] + [column_of(weight[j : j + 1]) for j in range(weight.shape[0])]


def stage(kernel, shapes, *operands, scratch=()):
    out = [jax.ShapeDtypeStruct(shape, dtype) for shape, dtype in shapes]
    params = pltpu.CompilerParams(vmem_limit_bytes=VMEM_BYTES)
    call = pl.pallas_call(
        kernel, out_shape=out, scratch_shapes=list(scratch), compiler_params=params, name=kernel.func.__name__
    )
    return call(*operands)


def prepare(halo, load, weight, rows, inverse, coarse_rounded, coarse, message, pieces):
    subs, nf = weight.shape
    ncf, columns, folds = halo.ncf, halo.columns, halo.folds
    for j in range(subs):
        coarse[j * ncf : (j + 1) * ncf] = dot(rows_of(rows, j, ncf), rows_of(load, j, nf).astype(BF16))
    coarse_rounded[...] = coarse[...].astype(BF16)
    last = weight[subs - 1 : subs]
    message[:nf] = ((1.0 - column_of(last)) * load[(subs - 1) * nf :]).astype(BF16)
    for array, at in ((rows, halo.at_rows), (inverse, halo.at_inverse)):
        for k in range(array.shape[1] // columns):
            message[at + k * ncf : at + (k + 1) * ncf] = array[(subs - 1) * ncf :, k * columns : (k + 1) * columns]
    pieces[...] = jnp.zeros_like(pieces)
    for k, part in enumerate(parts_of(last)):
        for i in range(folds):
            pieces[k * folds + i : k * folds + i + 1] = part[:, i * columns : (i + 1) * columns]
    message[halo.at_weight :] = pieces[...].astype(BF16)


def neumann_products(left, right, weights, neumann, part, back, forward):
    subs, nf = len(left), left[0].shape[0]
    previous = None
    for j in range(subs):
        product = dot(rows_of(neumann, j, 2 * nf), jnp.concatenate([left[j], right[j]], axis=0))
        first, second = product[:nf], product[nf:]
        if j == 0:
            part[:nf] = first
            back[...] = first.astype(BF16)
        else:
            part[j * nf : (j + 1) * nf] = weights[j] * previous + (1.0 - weights[j]) * first
        previous = second
    part[subs * nf :] = previous
    forward[...] = previous.astype(BF16)


def neumann_load(halo, load, weight, message, neumann, part, back, forward):
    subs, nf = weight.shape
    weights = [None] + [column_of(weight[j : j + 1]) for j in range(subs)]
    left = [halo.load(message)]
    left += [((1.0 - weights[j]) * rows_of(load, j - 1, nf)).astype(BF16) for j in range(1, subs)]
    right = [(weights[j + 1] * rows_of(load, j, nf)).astype(BF16) for j in range(subs)]
    neumann_products(left, right, weights, neumann, part, back, forward)


def neumann_image(halo, part_in, from_next, from_previous, weight, message, neumann, image, part, back, forward):
    subs, nf = weight.shape
    weights = all_weights(halo, message, weight)
    faces = [rows_of(part_in, e, nf) for e in range(subs + 1)]
    faces[0] = faces[0] + from_previous[...].astype(F32)
    faces[subs] = faces[subs] + from_next[...].astype(F32)
    for e in range(1, subs + 1):
        image[(e - 1) * nf : e * nf] = faces[e]
    left = [((1.0 - weights[j]) * faces[j]).astype(BF16) for j in range(subs)]
    right = [(weights[j + 1] * faces[j + 1]).astype(BF16) for j in range(subs)]
    neumann_products(left, right, weights, neumann, part, back, forward)


def static_basis(halo, schur, message, rows, basis_high, basis_low, turned_high, turned_low, gram):
    ncf, nf = halo.ncf, halo.nf
    blocks = all_rows(halo, message, rows)
    gram[...] = jnp.zeros_like(gram)
    for j in range(len(blocks) - 1):
        matrix, pair = rows_of(schur, j, 2 * nf), blocks[j : j + 2]
        basis = jnp.concatenate([dot_nt(matrix[:, k * nf : (k + 1) * nf], pair[k]) for k in range(2)], axis=1)
        long, wide = slice(2 * j * nf, 2 * (j + 1) * nf), slice(2 * j * ncf, 2 * (j + 1) * ncf)
        basis_high[long], basis_low[long] = split(basis)
        turned = split(basis.T)
        turned_high[wide], turned_low[wide] = turned
        for k in range(2):
            half = slice(k * nf, (k + 1) * nf)
            gram[wide, k * ncf : (k + 1) * ncf] = dot_nt(turned[0][:, half], pair[k]) + dot_nt(turned[1][:, half], pair[k])


def schur_products(
    halo, other, part, from_next, from_previous, weight, message, schur, turned_high, turned_low,
    local, product, quadratic, base,
):
    subs, nf = weight.shape
    ncf, columns = halo.ncf, halo.columns
    weights = all_weights(halo, message, weight)
    local[:nf] = (1.0 - weights[0]) * part[:nf] + weights[0] * from_previous[...].astype(F32)
    for e in range(1, subs):
        local[e * nf : (e + 1) * nf] = rows_of(part, e, nf)
    local[subs * nf :] = weights[subs] * part[subs * nf :] + (1.0 - weights[subs]) * from_next[...].astype(F32)
    energy, previous = 0.0, None
    for j in range(subs):
        vector = local[j * nf : (j + 2) * nf]
        high, low = split(vector)
        both = dot(rows_of(schur, j, 2 * nf), jnp.concatenate([high, low], axis=1))
        result = both[:, :columns] + both[:, columns:]
        energy = energy + column_sum(vector * result)
        first = result[:nf]
        product[j * nf : (j + 1) * nf] = first if j == 0 else previous + first
        previous = result[nf:]
        here = slice(2 * j * ncf, 2 * (j + 1) * ncf)
        base[here] = dot(turned_high[here], high) + dot(turned_high[here], low) + dot(turned_low[here], high)
    product[subs * nf :] = previous
    quadratic[0:1] = energy
    quadratic[1:2] = column_sum(other[...] * local[nf:])


def schur_load(*refs):
    *refs, gram, local, product, quadratic, base, share = refs
    schur_products(*refs, local, product, quadratic, base)
    ncf, columns = share.shape[0], base.shape[1]
    share[:, :columns] = base[:ncf]
    share[:, columns:] = gram[:ncf]


def schur_image(*refs):
    schur_products(*refs)


def coarse_solve(halo, half, crossed_half, inverses, gathered):
    me = lax.axis_index(AXIS)
    order = half_order()
    count = half.shape[0] // len(order)
    for flip, blocks in ((0, half), (1, crossed_half)):
        for k, place in enumerate(order):
            start = pl.multiple_of((me ^ (place ^ flip)) * count, count)
            gathered[pl.ds(start, count)] = rows_of(blocks, k, count)
    everything = gathered[...]
    return [dot(inverse, everything) for inverse in inverses]


def coarse_products(ncf, x, base, gram):
    results, energy = [], 0.0
    for j in range(len(x) - 1):
        here = slice(2 * j * ncf, 2 * (j + 1) * ncf)
        pair = jnp.concatenate([x[j], x[j + 1]], axis=0)
        change = split_dot(split(gram[here, : 2 * ncf]), pair)
        energy = energy + column_sum(pair * (2.0 * base[here] + change))
        results.append(base[here] + change)
    return results, energy


def add_basis(nf, x, basis_high, basis_low, product):
    faces = [rows_of(product, e, nf) for e in range(len(x))]
    for j in range(len(x) - 1):
        here = slice(2 * j * nf, 2 * (j + 1) * nf)
        pair = jnp.concatenate([x[j], x[j + 1]], axis=0)
        change = split_dot((basis_high[here], basis_low[here]), pair)
        faces[j] = faces[j] + change[:nf]
        faces[j + 1] = faces[j + 1] + change[nf:]
    return faces


def coarse_load(
    halo, half, crossed_half, inverse, message, next_inverse, share, coarse, base, gram, quadratic, basis_high, basis_low, product,
    coarse_rounded, image_coarse, solution, part, back, forward, sums, gathered,
):
    ncf, nf, columns = halo.ncf, halo.nf, halo.columns
    subs = inverse.shape[0] // ncf
    first, own, beyond = coarse_solve(
        halo, half, crossed_half, (halo.inverse(message), inverse[...], next_inverse[...]), gathered
    )
    x = [first] + [own[j * ncf : (j + 1) * ncf] for j in range(subs)]
    results, energy = coarse_products(ncf, x, base, gram)
    for e in range(1, subs):
        image_coarse[(e - 1) * ncf : e * ncf] = results[e - 1][ncf:] + results[e][:ncf]
    change = split_dot(split(share[:, columns : columns + 2 * ncf]), jnp.concatenate([x[subs], beyond], axis=0))
    image_coarse[(subs - 1) * ncf :] = results[subs - 1][ncf:] + share[:, :columns] + change
    coarse_rounded[...] = image_coarse[...].astype(BF16)
    solution[...] = own
    sums[0:1] = quadratic[1:2] + column_sum(coarse[...] * own)
    sums[1:2] = quadratic[0:1] + energy
    faces = add_basis(nf, x, basis_high, basis_low, product)
    for e in range(subs + 1):
        part[e * nf : (e + 1) * nf] = faces[e]
    back[...] = faces[0].astype(BF16)
    forward[...] = faces[subs].astype(BF16)


def coarse_image(
    halo, half, crossed_half, inverse, message, coarse, base, gram, quadratic, basis_high, basis_low, product, sums_in,
    sums, solution, part, back, gathered,
):
    ncf, nf = halo.ncf, halo.nf
    subs = inverse.shape[0] // ncf
    first, own = coarse_solve(halo, half, crossed_half, (halo.inverse(message), inverse[...]), gathered)
    x = [first] + [own[j * ncf : (j + 1) * ncf] for j in range(subs)]
    _, energy = coarse_products(ncf, x, base, gram)
    sums[0:2] = sums_in[0:2]
    sums[2:3] = quadratic[1:2] + column_sum(coarse[...] * own)
    sums[3:4] = quadratic[0:1] + energy
    solution[...] = own
    faces = add_basis(nf, x, basis_high, basis_low, product)
    for e in range(1, subs + 1):
        part[(e - 1) * nf : e * nf] = faces[e]
    back[...] = faces[0].astype(BF16)


def combine(halo, sums, load, z_local, z_coarse, y_local, y_coarse, rows, image, part, from_next, solution, residual):
    ncf, nf = halo.ncf, halo.nf
    subs = rows.shape[0] // ncf
    a, b, c, d = (sums[k : k + 1] for k in range(4))
    step = a / b
    grow = step * (c / b)
    next_step = (grow - 1.0) / ((d - c * (c / b)) * (step / b))
    s = step + next_step * grow
    t = step * next_step
    for j in range(subs):
        here, beside = slice(j * nf, (j + 1) * nf), slice((j + 1) * nf, (j + 2) * nf)
        x = s * rows_of(z_coarse, j, ncf) - t * rows_of(y_coarse, j, ncf)
        solution[here] = s * z_local[beside] - t * y_local[beside] + split_dot(rows_of(rows, j, ncf), x, dot_tn)
        last = part[here]
        if j == subs - 1:
            last = last + from_next[...].astype(F32)
        residual[here] = load[here] - s * image[here] + t * last


def shards(right_side, face_weight, schur, neumann, constraint, coarse_inverse):
    subs, nf = face_weight.shape
    ncf = constraint.shape[0] // subs
    nco = coarse_inverse.shape[1]
    columns = right_side.shape[1]
    halo = Halo(nf, ncf, nco, columns)
    bind = lambda kernel: functools.partial(kernel, halo)
    faces, own = ((subs + 1) * nf, columns), (subs * nf, columns)
    coarse_own, local_rows = (subs * ncf, columns), 2 * subs * ncf
    halves = [((nf, columns), BF16)] * 2
    products = [(faces, F32), (faces, F32), ((8, columns), F32), ((local_rows, columns), F32)]
    gathered = [pltpu.VMEM((nco, columns), BF16)]

    coarse_rounded, coarse, message = stage(
        bind(prepare), [(coarse_own, BF16), (coarse_own, F32), ((halo.height, columns), BF16)],
        right_side, face_weight, constraint, coarse_inverse, scratch=[pltpu.VMEM((halo.weight_count, columns), F32)],
    )
    message = shifted(message, 1)
    coarse_halves = gather_halves(coarse_rounded)
    next_inverse = shifted(coarse_inverse[:ncf], -1)

    part, back, forward = stage(
        bind(neumann_load), [(faces, F32)] + halves, right_side, face_weight, message, neumann
    )
    back, forward = shifted(back, -1), shifted(forward, 1)
    long, wide = ((2 * subs * nf, 2 * ncf), BF16), ((local_rows, 2 * nf), BF16)
    basis_high, basis_low, turned_high, turned_low, gram = stage(
        bind(static_basis), [long, long, wide, wide, ((local_rows, LANES), F32)], schur, message, constraint
    )
    local, product, quadratic, base, share = stage(
        bind(schur_load), products + [((ncf, columns + LANES), F32)],
        right_side, part, back, forward, face_weight, message, schur, turned_high, turned_low, gram,
    )
    share = shifted(share, -1)
    coarse_rounded, coarse, z_coarse, part, back, forward, sums = stage(
        bind(coarse_load),
        [(coarse_own, BF16), (coarse_own, F32), (coarse_own, F32), (faces, F32)] + halves + [((8, columns), F32)],
        *coarse_halves, coarse_inverse, message, next_inverse, share, coarse, base, gram, quadratic,
        basis_high, basis_low, product, scratch=gathered,
    )
    coarse_halves = gather_halves(coarse_rounded)
    back, forward = shifted(back, -1), shifted(forward, 1)
    image, part, back, forward = stage(
        bind(neumann_image), [(own, F32), (faces, F32)] + halves, part, back, forward, face_weight, message, neumann
    )
    back, forward = shifted(back, -1), shifted(forward, 1)
    y_local, product, quadratic, base = stage(
        bind(schur_image), products,
        image, part, back, forward, face_weight, message, schur, turned_high, turned_low,
    )
    sums, y_coarse, part, back = stage(
        bind(coarse_image), [((4, columns), F32), (coarse_own, F32), (own, F32), ((nf, columns), BF16)],
        *coarse_halves, coarse_inverse, message, coarse, base, gram, quadratic, basis_high, basis_low, product, sums,
        scratch=gathered,
    )
    sums = sum_all(sums)
    back = shifted(back, -1)
    return stage(
        bind(combine), [(own, F32), (own, F32)],
        sums, right_side, local, z_coarse, y_local, y_coarse, constraint, image, part, back,
    )


def solution(mesh):
    specs = P(("parts", AXIS), None)
    return jax.shard_map(shards, mesh=mesh, in_specs=(specs,) * 6, out_specs=(specs, specs), check_vma=False)
```

```python
import functools

import jax
import jax.numpy as jnp
from jax import lax
from jax.experimental import pallas as pl
from jax.experimental.pallas import tpu as pltpu
from jax.sharding import PartitionSpec as P

AXIS = "sub"
BF16 = jnp.bfloat16
F32 = jnp.float32
LANES = 128
VMEM_BYTES = 20 * 2**20


def shifted(block, distance):
    n = lax.axis_size(AXIS)
    return lax.ppermute(block, AXIS, [((i - distance) % n, i) for i in range(n)])


def crossed(block, bit):
    return lax.ppermute(block, AXIS, [(i, i ^ bit) for i in range(lax.axis_size(AXIS))])


def bits():
    return [1 << k for k in reversed(range(lax.axis_size(AXIS).bit_length() - 1))]


def gather_halves(block):
    for bit in bits()[:-1]:
        block = jnp.concatenate([block, crossed(block, bit)], axis=0)
    return block, crossed(block, 1)


def half_order():
    order = [0]
    for bit in bits()[:-1]:
        order += [place ^ bit for place in order]
    return order


def dot(a, b):
    return jnp.dot(a, b, preferred_element_type=F32)


def dot_nt(a, b):
    return lax.dot_general(a, b, (((1,), (1,)), ((), ())), preferred_element_type=F32)


def dot_tn(a, b):
    return lax.dot_general(a, b, (((0,), (0,)), ((), ())), preferred_element_type=F32)


def split(x):
    high = x.astype(BF16)
    return high, (x - high.astype(F32)).astype(BF16)


def split_dot(a, b, contract=dot):
    high, low = split(b)
    if isinstance(a, tuple):
        return contract(a[0], high) + contract(a[0], low) + contract(a[1], high)
    return contract(a, high) + contract(a, low)


def column_sum(x):
    return jnp.sum(x, axis=0, keepdims=True)


def rows_of(ref, index, count):
    return ref[index * count : (index + 1) * count]


def column_of(row):
    return jnp.broadcast_to(row, (8, row.shape[1])).T[:, :1]


def parts_of(row):
    high = row.astype(BF16).astype(F32)
    middle = (row - high).astype(BF16).astype(F32)
    return high, middle, row - high - middle


class Halo:
    def __init__(self, nf, ncf, nco, columns):
        self.nf, self.ncf, self.columns = nf, ncf, columns
        self.folds = nf // columns
        self.inverse_folds = nco // columns
        self.first_height = nf + ncf * self.folds
        self.at_weight = nf + ncf * self.inverse_folds
        self.weight_count = -(-3 * self.folds // 16) * 16
        self.second_height = self.at_weight + self.weight_count

    def unfolded(self, message, folds):
        start, ncf = self.nf, self.ncf
        return jnp.concatenate([message[start + k * ncf : start + (k + 1) * ncf] for k in range(folds)], axis=1)

    def fold(self, message, block, folds):
        start, ncf, columns = self.nf, self.ncf, self.columns
        for k in range(folds):
            message[start + k * ncf : start + (k + 1) * ncf] = block[:, k * columns : (k + 1) * columns]

    def product(self, message):
        return message[: self.nf].astype(F32)

    def rows(self, message):
        return self.unfolded(message, self.folds)

    def inverse(self, message):
        return self.unfolded(message, self.inverse_folds)

    def weight(self, message):
        got = message[self.at_weight : self.second_height].astype(F32)
        f = self.folds
        row = [sum(got[k * f + i : k * f + i + 1] for k in range(3)) for i in range(f)]
        return jnp.concatenate([column_of(piece) for piece in row], axis=0)


def all_rows(halo, message, rows):
    ncf = halo.ncf
    return [halo.rows(message)] + [rows_of(rows, j, ncf) for j in range(rows.shape[0] // ncf)]


def all_weights(halo, message, weight):
    return [halo.weight(message)] + [column_of(weight[j : j + 1]) for j in range(weight.shape[0])]


def stage(kernel, shapes, *operands, scratch=(), fetched=0):
    out = [jax.ShapeDtypeStruct(shape, dtype) for shape, dtype in shapes]
    params = pltpu.CompilerParams(vmem_limit_bytes=VMEM_BYTES)
    spaces = [pltpu.HBM] * fetched + [pltpu.VMEM] * (len(operands) - fetched)
    call = pl.pallas_call(
        kernel,
        out_shape=out,
        in_specs=[pl.BlockSpec(memory_space=space) for space in spaces],
        scratch_shapes=list(scratch),
        compiler_params=params,
        name=kernel.func.__name__,
    )
    return call(*operands)


def prepare(halo, load, rows, weight, load_here, rows_here, weight_here, coarse_rounded, coarse, done):
    ncf, nf = halo.ncf, halo.nf
    subs = load.shape[0] // nf
    copies = [pltpu.make_async_copy(rows, rows_here, done.at[subs])]
    copies += [
        pltpu.make_async_copy(rows_of(load.at, j, nf), rows_of(load_here.at, j, nf), done.at[j]) for j in range(subs)
    ]
    copies.append(pltpu.make_async_copy(weight, weight_here, done.at[subs + 1]))
    for copy in copies:
        copy.start()
    copies[0].wait()
    for j in range(subs):
        copies[1 + j].wait()
        coarse[j * ncf : (j + 1) * ncf] = dot(rows_of(rows_here, j, ncf), rows_of(load_here, j, nf).astype(BF16))
    coarse_rounded[...] = coarse[...].astype(BF16)
    copies[-1].wait()


def first_message(halo, load, weight, rows, message):
    ncf, nf = halo.ncf, halo.nf
    message[:nf] = ((1.0 - column_of(weight[weight.shape[0] - 1 :])) * load[load.shape[0] - nf :]).astype(BF16)
    halo.fold(message, rows[rows.shape[0] - ncf :], halo.folds)


def fetch(halo, neumann, schur, inverse, neumann_here, schur_here, inverse_here, done):
    pairs = ((neumann, neumann_here), (schur, schur_here), (inverse, inverse_here))
    copies = [pltpu.make_async_copy(source, here, done.at[k]) for k, (source, here) in enumerate(pairs)]
    for copy in copies:
        copy.start()
    for copy in copies:
        copy.wait()


def neumann_products(left, right, weights, neumann, part, back, forward):
    subs, nf = len(left), left[0].shape[0]
    previous = None
    for j in range(subs):
        product = dot(rows_of(neumann, j, 2 * nf), jnp.concatenate([left[j], right[j]], axis=0))
        first, second = product[:nf], product[nf:]
        if j == 0:
            part[:nf] = first
            back[...] = first.astype(BF16)
        else:
            part[j * nf : (j + 1) * nf] = weights[j] * previous + (1.0 - weights[j]) * first
        previous = second
    part[subs * nf :] = previous
    forward[:nf] = previous.astype(BF16)


def neumann_load(halo, load, weight, message, neumann, inverse, part, back, forward, pieces):
    subs, nf = weight.shape
    ncf, columns, folds = halo.ncf, halo.columns, halo.folds
    halo.fold(forward, inverse[inverse.shape[0] - ncf :], halo.inverse_folds)
    pieces[...] = jnp.zeros_like(pieces)
    for k, values in enumerate(parts_of(weight[subs - 1 : subs])):
        for i in range(folds):
            pieces[k * folds + i : k * folds + i + 1] = values[:, i * columns : (i + 1) * columns]
    forward[halo.at_weight :] = pieces[...].astype(BF16)
    weights = [None] + [column_of(weight[j : j + 1]) for j in range(subs)]
    left = [message[:nf]]
    left += [((1.0 - weights[j]) * rows_of(load, j - 1, nf)).astype(BF16) for j in range(1, subs)]
    right = [(weights[j + 1] * rows_of(load, j, nf)).astype(BF16) for j in range(subs)]
    neumann_products(left, right, weights, neumann, part, back, forward)


def neumann_image(halo, part_in, from_next, from_previous, weight, message, neumann, image, part, back, forward):
    subs, nf = weight.shape
    weights = all_weights(halo, message, weight)
    faces = [rows_of(part_in, e, nf) for e in range(subs + 1)]
    faces[0] = faces[0] + from_previous[...].astype(F32)
    faces[subs] = faces[subs] + from_next[...].astype(F32)
    for e in range(1, subs + 1):
        image[(e - 1) * nf : e * nf] = faces[e]
    left = [((1.0 - weights[j]) * faces[j]).astype(BF16) for j in range(subs)]
    right = [(weights[j + 1] * faces[j + 1]).astype(BF16) for j in range(subs)]
    neumann_products(left, right, weights, neumann, part, back, forward)


def static_basis(halo, schur, message, rows, basis_high, basis_low, turned_high, turned_low, gram):
    ncf, nf = halo.ncf, halo.nf
    blocks = all_rows(halo, message, rows)
    gram[...] = jnp.zeros_like(gram)
    for j in range(len(blocks) - 1):
        matrix, pair = rows_of(schur, j, 2 * nf), blocks[j : j + 2]
        basis = jnp.concatenate([dot_nt(matrix[:, k * nf : (k + 1) * nf], pair[k]) for k in range(2)], axis=1)
        long, wide = slice(2 * j * nf, 2 * (j + 1) * nf), slice(2 * j * ncf, 2 * (j + 1) * ncf)
        basis_high[long], basis_low[long] = split(basis)
        turned = split(basis.T)
        turned_high[wide], turned_low[wide] = turned
        for k in range(2):
            half = slice(k * nf, (k + 1) * nf)
            gram[wide, k * ncf : (k + 1) * ncf] = dot_nt(turned[0][:, half], pair[k]) + dot_nt(turned[1][:, half], pair[k])


def schur_products(
    halo, other, part, from_next, from_previous, weight, message, schur, turned_high, turned_low,
    local, product, quadratic, base,
):
    subs, nf = weight.shape
    ncf, columns = halo.ncf, halo.columns
    weights = all_weights(halo, message, weight)
    local[:nf] = (1.0 - weights[0]) * part[:nf] + weights[0] * halo.product(from_previous)
    for e in range(1, subs):
        local[e * nf : (e + 1) * nf] = rows_of(part, e, nf)
    local[subs * nf :] = weights[subs] * part[subs * nf :] + (1.0 - weights[subs]) * from_next[...].astype(F32)
    energy, previous = 0.0, None
    for j in range(subs):
        vector = local[j * nf : (j + 2) * nf]
        high, low = split(vector)
        both = dot(rows_of(schur, j, 2 * nf), jnp.concatenate([high, low], axis=1))
        result = both[:, :columns] + both[:, columns:]
        energy = energy + column_sum(vector * result)
        first = result[:nf]
        product[j * nf : (j + 1) * nf] = first if j == 0 else previous + first
        previous = result[nf:]
        here = slice(2 * j * ncf, 2 * (j + 1) * ncf)
        base[here] = dot(turned_high[here], high) + dot(turned_high[here], low) + dot(turned_low[here], high)
    product[subs * nf :] = previous
    quadratic[0:1] = energy
    quadratic[1:2] = column_sum(other[...] * local[nf:])


def schur_load(halo, load, part, from_next, from_previous, weight, schur, turned_high, turned_low, *outs):
    schur_products(
        halo, load, part, from_next, from_previous, weight, from_previous, schur, turned_high, turned_low, *outs
    )


def schur_image(halo, *refs):
    schur_products(halo, *refs)


def placed(half, crossed_half):
    me = lax.axis_index(AXIS)
    order = half_order()
    count = half.shape[0] // len(order)
    for flip, blocks in ((0, half), (1, crossed_half)):
        for k, place in enumerate(order):
            yield me ^ (place ^ flip), blocks, k * count, (k + 1) * count


def coarse_shares(ncf, results):
    shares = [results[0][:ncf]]
    for before, after in zip(results[:-1], results[1:]):
        shares.append(before[ncf:] + after[:ncf])
    return shares + [results[-1][ncf:]]


def coarse_products(ncf, x, base, gram):
    results, energy = [], 0.0
    for j in range(len(x) - 1):
        here = slice(2 * j * ncf, 2 * (j + 1) * ncf)
        pair = jnp.concatenate([x[j], x[j + 1]], axis=0)
        change = split_dot(split(gram[here, : 2 * ncf]), pair)
        energy = energy + column_sum(pair * (2.0 * base[here] + change))
        results.append(base[here] + change)
    return results, energy


def add_basis(nf, x, basis_high, basis_low, product):
    faces = [rows_of(product, e, nf) for e in range(len(x))]
    for j in range(len(x) - 1):
        here = slice(2 * j * nf, 2 * (j + 1) * nf)
        pair = jnp.concatenate([x[j], x[j + 1]], axis=0)
        change = split_dot((basis_high[here], basis_low[here]), pair)
        faces[j] = faces[j] + change[:nf]
        faces[j + 1] = faces[j + 1] + change[nf:]
    return faces


def coarse_load(
    halo, half, crossed_half, inverse, message, coarse, base, gram, quadratic, basis_high, basis_low, product,
    shares_rounded, shares, solution, part, back, forward, sums, gathered,
):
    ncf, nf = halo.ncf, halo.nf
    subs = inverse.shape[0] // ncf
    for place, blocks, start, stop in placed(half, crossed_half):
        gathered[pl.ds(pl.multiple_of(place * subs * ncf, subs * ncf), subs * ncf)] = blocks[start:stop]
    everything = gathered[...]
    own = dot(inverse[...], everything)
    x = [dot(halo.inverse(message), everything)] + [own[j * ncf : (j + 1) * ncf] for j in range(subs)]
    results, energy = coarse_products(ncf, x, base, gram)
    for e, share in enumerate(coarse_shares(ncf, results)):
        shares[e * ncf : (e + 1) * ncf] = share
    shares_rounded[...] = shares[...].astype(BF16)
    solution[...] = own
    sums[0:1] = quadratic[1:2] + column_sum(coarse[...] * own)
    sums[1:2] = quadratic[0:1] + energy
    faces = add_basis(nf, x, basis_high, basis_low, product)
    for e in range(subs + 1):
        part[e * nf : (e + 1) * nf] = faces[e]
    back[...] = faces[0].astype(BF16)
    forward[...] = faces[subs].astype(BF16)


def coarse_image(
    halo, half, crossed_half, inverse, message, shares, base, gram, quadratic, basis_high, basis_low, product, sums_in,
    sums, solution, part, back, gathered,
):
    ncf, nf = halo.ncf, halo.nf
    subs = inverse.shape[0] // ncf
    total = gathered.shape[0]
    for place, blocks, start, stop in placed(half, crossed_half):
        gathered[pl.ds(pl.multiple_of(place * subs * ncf, subs * ncf), subs * ncf)] = blocks[start + ncf : stop].astype(F32)
    for place, blocks, start, stop in placed(half, crossed_half):
        before = pl.multiple_of(lax.rem(place * subs * ncf + (total - ncf), total), ncf)
        gathered[pl.ds(before, ncf)] += blocks[start : start + ncf].astype(F32)
    everything = gathered[...]
    own = split_dot(inverse[...], everything)
    x = [split_dot(halo.inverse(message), everything)] + [own[j * ncf : (j + 1) * ncf] for j in range(subs)]
    _, energy = coarse_products(ncf, x, base, gram)
    sums[0:2] = sums_in[0:2]
    sums[2:3] = quadratic[1:2] + sum(column_sum(rows_of(shares, e, ncf) * x[e]) for e in range(subs + 1))
    sums[3:4] = quadratic[0:1] + energy
    solution[...] = own
    faces = add_basis(nf, x, basis_high, basis_low, product)
    for e in range(1, subs + 1):
        part[(e - 1) * nf : e * nf] = faces[e]
    back[...] = faces[0].astype(BF16)


def complete(halo, z_local, z_coarse, y_local, y_coarse, rows, z, y):
    ncf, nf = halo.ncf, halo.nf
    for j in range(rows.shape[0] // ncf):
        here, beside = slice(j * nf, (j + 1) * nf), slice((j + 1) * nf, (j + 2) * nf)
        for local, coarse, whole in ((z_local, z_coarse, z), (y_local, y_coarse, y)):
            whole[here] = local[beside] + split_dot(rows_of(rows, j, ncf), rows_of(coarse, j, ncf), dot_tn)


def combine(halo, sums, load, z, y, image, part, from_next, solution, residual):
    nf = halo.nf
    a, b, c, d = (sums[k : k + 1] for k in range(4))
    step = a / b
    grow = step * (c / b)
    next_step = (grow - 1.0) / ((d - c * (c / b)) * (step / b))
    s = step + next_step * grow
    t = step * next_step
    solution[...] = s * z[...] - t * y[...]
    last = load.shape[0] - nf
    residual[:last] = load[:last] - s * image[:last] + t * part[:last]
    residual[last:] = load[last:] - s * image[last:] + t * (part[last:] + from_next[...].astype(F32))


def shards(right_side, face_weight, schur, neumann, constraint, coarse_inverse):
    subs, nf = face_weight.shape
    ncf = constraint.shape[0] // subs
    nco = coarse_inverse.shape[1]
    columns = right_side.shape[1]
    halo = Halo(nf, ncf, nco, columns)
    bind = lambda kernel: functools.partial(kernel, halo)
    faces, own = ((subs + 1) * nf, columns), (subs * nf, columns)
    coarse_own, local_rows = (subs * ncf, columns), 2 * subs * ncf
    halves = [((nf, columns), BF16)] * 2
    products = [(faces, F32), (faces, F32), ((8, columns), F32), ((local_rows, columns), F32)]
    semaphores = lambda count: [pltpu.SemaphoreType.DMA((count,))]
    described = lambda array: (array.shape, array.dtype)

    load, rows, weight, coarse_rounded, coarse = stage(
        bind(prepare),
        [described(right_side), described(constraint), described(face_weight), (coarse_own, BF16), (coarse_own, F32)],
        right_side, constraint, face_weight, scratch=semaphores(subs + 2), fetched=3,
    )
    (first,) = stage(bind(first_message), [((halo.first_height, columns), BF16)], load, weight, rows)
    coarse_halves = gather_halves(coarse_rounded)
    tied, _ = lax.optimization_barrier(((neumann, schur, coarse_inverse), first))
    neumann, schur, inverse = stage(
        bind(fetch), [described(array) for array in tied], *tied, scratch=semaphores(3), fetched=3
    )
    first = shifted(first, 1)
    part, back, forward = stage(
        bind(neumann_load), [(faces, F32), ((nf, columns), BF16), ((halo.second_height, columns), BF16)],
        load, weight, first, neumann, inverse, scratch=[pltpu.VMEM((halo.weight_count, columns), F32)],
    )
    back, second = shifted(back, -1), shifted(forward, 1)
    long, wide = ((2 * subs * nf, 2 * ncf), BF16), ((local_rows, 2 * nf), BF16)
    basis_high, basis_low, turned_high, turned_low, gram = stage(
        bind(static_basis), [long, long, wide, wide, ((local_rows, LANES), F32)], schur, first, rows
    )
    z_local, product, quadratic, base = stage(
        bind(schur_load), products, load, part, back, second, weight, schur, turned_high, turned_low
    )
    share_rows = ((subs + 1) * ncf, columns)
    shares_rounded, shares, z_coarse, part, back, forward, sums = stage(
        bind(coarse_load),
        [(share_rows, BF16), (share_rows, F32), (coarse_own, F32), (faces, F32)] + halves + [((8, columns), F32)],
        *coarse_halves, inverse, second, coarse, base, gram, quadratic, basis_high, basis_low, product,
        scratch=[pltpu.VMEM((nco, columns), BF16)],
    )
    coarse_halves = gather_halves(shares_rounded)
    back, forward = shifted(back, -1), shifted(forward, 1)
    image, part, back, forward = stage(
        bind(neumann_image), [(own, F32), (faces, F32)] + halves, part, back, forward, weight, second, neumann
    )
    back, forward = shifted(back, -1), shifted(forward, 1)
    y_local, product, quadratic, base = stage(
        bind(schur_image), products, image, part, back, forward, weight, second, schur, turned_high, turned_low
    )
    sums, y_coarse, part, back = stage(
        bind(coarse_image), [((4, columns), F32), (coarse_own, F32), (own, F32), ((nf, columns), BF16)],
        *coarse_halves, inverse, second, shares, base, gram, quadratic, basis_high, basis_low, product, sums,
        scratch=[pltpu.VMEM((nco, columns), F32)],
    )
    steps = bits()
    for k, bit in enumerate(steps):
        sums = sums + crossed(sums, bit)
        if k + 1 == len(steps) // 2:
            sums, back = lax.optimization_barrier((sums, back))
            back = shifted(back, -1)
    z, y = stage(bind(complete), [(own, F32), (own, F32)], z_local, z_coarse, y_local, y_coarse, rows)
    return stage(bind(combine), [(own, F32), (own, F32)], sums, load, z, y, image, part, back)


def solution(mesh):
    specs = P(("parts", AXIS), None)
    return jax.shard_map(shards, mesh=mesh, in_specs=(specs,) * 6, out_specs=(specs, specs), check_vma=False)
```

```python
import functools

import jax
import jax.numpy as jnp
from jax import lax
from jax.experimental import pallas as pl
from jax.experimental.pallas import tpu as pltpu
from jax.sharding import PartitionSpec as P

AXIS = "sub"
BF16 = jnp.bfloat16
F32 = jnp.float32
LANES = 128
VMEM_BYTES = 20 * 2**20


def shifted(block, distance):
    n = lax.axis_size(AXIS)
    return lax.ppermute(block, AXIS, [((i - distance) % n, i) for i in range(n)])


def crossed(block, bit):
    return lax.ppermute(block, AXIS, [(i, i ^ bit) for i in range(lax.axis_size(AXIS))])


def groups():
    return [list(range(k, lax.axis_size(AXIS), 2)) for k in range(2)]


def from_group(copies):
    return lax.all_to_all(copies, AXIS, 0, 0, axis_index_groups=groups())


def dot(a, b):
    return jnp.dot(a, b, preferred_element_type=F32)


def dot_nt(a, b):
    return lax.dot_general(a, b, (((1,), (1,)), ((), ())), preferred_element_type=F32)


def dot_tn(a, b):
    return lax.dot_general(a, b, (((0,), (0,)), ((), ())), preferred_element_type=F32)


def split(x):
    high = x.astype(BF16)
    return high, (x - high.astype(F32)).astype(BF16)


def split_dot(a, b, contract=dot):
    high, low = split(b)
    if isinstance(a, tuple):
        return contract(a[0], high) + contract(a[0], low) + contract(a[1], high)
    return contract(a, high) + contract(a, low)


def column_sum(x):
    return jnp.sum(x, axis=0, keepdims=True)


def rows_of(ref, index, count):
    return ref[index * count : (index + 1) * count]


def column_of(row):
    return jnp.broadcast_to(row, (8, row.shape[1])).T[:, :1]


def parts_of(row):
    high = row.astype(BF16).astype(F32)
    middle = (row - high).astype(BF16).astype(F32)
    return high, middle, row - high - middle


class Halo:
    def __init__(self, nf, ncf, nco, columns):
        self.nf, self.ncf, self.columns = nf, ncf, columns
        self.folds = nf // columns
        self.inverse_folds = nco // columns
        self.first_height = nf + ncf * self.folds
        self.at_weight = nf + ncf * self.inverse_folds
        self.weight_count = -(-3 * self.folds // 16) * 16
        self.second_height = self.at_weight + self.weight_count

    def unfolded(self, message, folds):
        start, ncf = self.nf, self.ncf
        return jnp.concatenate([message[start + k * ncf : start + (k + 1) * ncf] for k in range(folds)], axis=1)

    def fold(self, message, block, folds):
        start, ncf, columns = self.nf, self.ncf, self.columns
        for k in range(folds):
            message[start + k * ncf : start + (k + 1) * ncf] = block[:, k * columns : (k + 1) * columns]

    def product(self, message):
        return message[: self.nf].astype(F32)

    def rows(self, message):
        return self.unfolded(message, self.folds)

    def inverse(self, message):
        return self.unfolded(message, self.inverse_folds)

    def weight(self, message):
        got = message[self.at_weight : self.second_height].astype(F32)
        f = self.folds
        row = [sum(got[k * f + i : k * f + i + 1] for k in range(3)) for i in range(f)]
        return jnp.concatenate([column_of(piece) for piece in row], axis=0)


def all_rows(halo, message, rows):
    ncf = halo.ncf
    return [halo.rows(message)] + [rows_of(rows, j, ncf) for j in range(rows.shape[0] // ncf)]


def all_weights(halo, message, weight):
    return [halo.weight(message)] + [column_of(weight[j : j + 1]) for j in range(weight.shape[0])]


def stage(kernel, shapes, *operands, scratch=(), fetched=0):
    out = [jax.ShapeDtypeStruct(shape, dtype) for shape, dtype in shapes]
    params = pltpu.CompilerParams(vmem_limit_bytes=VMEM_BYTES)
    spaces = [pltpu.HBM] * fetched + [pltpu.VMEM] * (len(operands) - fetched)
    call = pl.pallas_call(
        kernel,
        out_shape=out,
        in_specs=[pl.BlockSpec(memory_space=space) for space in spaces],
        scratch_shapes=list(scratch),
        compiler_params=params,
        name=kernel.func.__name__,
    )
    return call(*operands)


def prepare(halo, load, rows, weight, load_here, rows_here, weight_here, coarse, done):
    ncf, nf = halo.ncf, halo.nf
    subs = load.shape[0] // nf
    copies = [pltpu.make_async_copy(rows, rows_here, done.at[subs])]
    copies += [
        pltpu.make_async_copy(rows_of(load.at, j, nf), rows_of(load_here.at, j, nf), done.at[j]) for j in range(subs)
    ]
    copies.append(pltpu.make_async_copy(weight, weight_here, done.at[subs + 1]))
    for copy in copies:
        copy.start()
    copies[0].wait()
    for j in range(subs):
        copies[1 + j].wait()
        coarse[j * ncf : (j + 1) * ncf] = dot(rows_of(rows_here, j, ncf), rows_of(load_here, j, nf).astype(BF16))
    copies[-1].wait()


def first_message(halo, load, weight, rows, message):
    ncf, nf = halo.ncf, halo.nf
    message[:nf] = ((1.0 - column_of(weight[weight.shape[0] - 1 :])) * load[load.shape[0] - nf :]).astype(BF16)
    halo.fold(message, rows[rows.shape[0] - ncf :], halo.folds)


def fetch(halo, neumann, schur, inverse, neumann_here, schur_here, inverse_here, done):
    pairs = ((neumann, neumann_here), (schur, schur_here), (inverse, inverse_here))
    copies = [pltpu.make_async_copy(source, here, done.at[k]) for k, (source, here) in enumerate(pairs)]
    for copy in copies:
        copy.start()
    for copy in copies:
        copy.wait()


def neumann_products(left, right, weights, neumann, part, back, forward):
    subs, nf = len(left), left[0].shape[0]
    previous = None
    for j in range(subs):
        product = dot(rows_of(neumann, j, 2 * nf), jnp.concatenate([left[j], right[j]], axis=0))
        first, second = product[:nf], product[nf:]
        if j == 0:
            part[:nf] = first
            back[...] = first.astype(BF16)
        else:
            part[j * nf : (j + 1) * nf] = weights[j] * previous + (1.0 - weights[j]) * first
        previous = second
    part[subs * nf :] = previous
    forward[:nf] = previous.astype(BF16)


def neumann_load(halo, load, weight, message, neumann, inverse, part, back, forward, pieces):
    subs, nf = weight.shape
    ncf, columns, folds = halo.ncf, halo.columns, halo.folds
    halo.fold(forward, inverse[inverse.shape[0] - ncf :], halo.inverse_folds)
    pieces[...] = jnp.zeros_like(pieces)
    for k, values in enumerate(parts_of(weight[subs - 1 : subs])):
        for i in range(folds):
            pieces[k * folds + i : k * folds + i + 1] = values[:, i * columns : (i + 1) * columns]
    forward[halo.at_weight :] = pieces[...].astype(BF16)
    weights = [None] + [column_of(weight[j : j + 1]) for j in range(subs)]
    left = [message[:nf]]
    left += [((1.0 - weights[j]) * rows_of(load, j - 1, nf)).astype(BF16) for j in range(1, subs)]
    right = [(weights[j + 1] * rows_of(load, j, nf)).astype(BF16) for j in range(subs)]
    neumann_products(left, right, weights, neumann, part, back, forward)


def neumann_image(halo, part_in, from_next, from_previous, weight, message, neumann, image, part, back, forward):
    subs, nf = weight.shape
    weights = all_weights(halo, message, weight)
    faces = [rows_of(part_in, e, nf) for e in range(subs + 1)]
    faces[0] = faces[0] + from_previous[...].astype(F32)
    faces[subs] = faces[subs] + from_next[...].astype(F32)
    for e in range(1, subs + 1):
        image[(e - 1) * nf : e * nf] = faces[e]
    left = [((1.0 - weights[j]) * faces[j]).astype(BF16) for j in range(subs)]
    right = [(weights[j + 1] * faces[j + 1]).astype(BF16) for j in range(subs)]
    neumann_products(left, right, weights, neumann, part, back, forward)


def static_basis(halo, schur, message, rows, basis_high, basis_low, turned_high, turned_low, gram):
    ncf, nf = halo.ncf, halo.nf
    blocks = all_rows(halo, message, rows)
    gram[...] = jnp.zeros_like(gram)
    for j in range(len(blocks) - 1):
        matrix, pair = rows_of(schur, j, 2 * nf), blocks[j : j + 2]
        basis = jnp.concatenate([dot_nt(matrix[:, k * nf : (k + 1) * nf], pair[k]) for k in range(2)], axis=1)
        long, wide = slice(2 * j * nf, 2 * (j + 1) * nf), slice(2 * j * ncf, 2 * (j + 1) * ncf)
        basis_high[long], basis_low[long] = split(basis)
        turned = split(basis.T)
        turned_high[wide], turned_low[wide] = turned
        for k in range(2):
            half = slice(k * nf, (k + 1) * nf)
            gram[wide, k * ncf : (k + 1) * ncf] = dot_nt(turned[0][:, half], pair[k]) + dot_nt(turned[1][:, half], pair[k])


def schur_products(
    halo, other, part, from_next, from_previous, weight, message, schur, turned_high, turned_low,
    local, product, quadratic, base,
):
    subs, nf = weight.shape
    ncf, columns = halo.ncf, halo.columns
    weights = all_weights(halo, message, weight)
    local[:nf] = (1.0 - weights[0]) * part[:nf] + weights[0] * halo.product(from_previous)
    for e in range(1, subs):
        local[e * nf : (e + 1) * nf] = rows_of(part, e, nf)
    local[subs * nf :] = weights[subs] * part[subs * nf :] + (1.0 - weights[subs]) * from_next[...].astype(F32)
    energy, previous = 0.0, None
    for j in range(subs):
        vector = local[j * nf : (j + 2) * nf]
        high, low = split(vector)
        both = dot(rows_of(schur, j, 2 * nf), jnp.concatenate([high, low], axis=1))
        result = both[:, :columns] + both[:, columns:]
        energy = energy + column_sum(vector * result)
        first = result[:nf]
        product[j * nf : (j + 1) * nf] = first if j == 0 else previous + first
        previous = result[nf:]
        here = slice(2 * j * ncf, 2 * (j + 1) * ncf)
        base[here] = dot(turned_high[here], high) + dot(turned_high[here], low) + dot(turned_low[here], high)
    product[subs * nf :] = previous
    quadratic[0:1] = energy
    quadratic[1:2] = column_sum(other[...] * local[nf:])


def schur_load(halo, load, part, from_next, from_previous, weight, schur, turned_high, turned_low, *outs):
    schur_products(
        halo, load, part, from_next, from_previous, weight, from_previous, schur, turned_high, turned_low, *outs
    )


def schur_image(halo, *refs):
    schur_products(halo, *refs)


def placed(half, crossed_half):
    parity = lax.rem(lax.axis_index(AXIS), 2)
    for flip, blocks in ((0, half), (1, crossed_half)):
        for k in range(blocks.shape[0]):
            yield 2 * k + (parity ^ flip), blocks, k


def copy_out(halo, block, copies):
    rounded = block[...].astype(copies.dtype)
    for k in range(copies.shape[0]):
        copies[k] = rounded


def coarse_shares(ncf, results):
    shares = [results[0][:ncf]]
    for before, after in zip(results[:-1], results[1:]):
        shares.append(before[ncf:] + after[:ncf])
    return shares + [results[-1][ncf:]]


def coarse_products(ncf, x, base, gram):
    results, energy = [], 0.0
    for j in range(len(x) - 1):
        here = slice(2 * j * ncf, 2 * (j + 1) * ncf)
        pair = jnp.concatenate([x[j], x[j + 1]], axis=0)
        change = split_dot(split(gram[here, : 2 * ncf]), pair)
        energy = energy + column_sum(pair * (2.0 * base[here] + change))
        results.append(base[here] + change)
    return results, energy


def add_basis(nf, x, basis_high, basis_low, product):
    faces = [rows_of(product, e, nf) for e in range(len(x))]
    for j in range(len(x) - 1):
        here = slice(2 * j * nf, 2 * (j + 1) * nf)
        pair = jnp.concatenate([x[j], x[j + 1]], axis=0)
        change = split_dot((basis_high[here], basis_low[here]), pair)
        faces[j] = faces[j] + change[:nf]
        faces[j + 1] = faces[j + 1] + change[nf:]
    return faces


def coarse_load(
    halo, half, crossed_half, inverse, message, coarse, base, gram, quadratic, basis_high, basis_low, product,
    shares, solution, part, back, forward, sums, gathered,
):
    ncf, nf = halo.ncf, halo.nf
    subs = inverse.shape[0] // ncf
    for place, blocks, k in placed(half, crossed_half):
        gathered[pl.ds(pl.multiple_of(place * subs * ncf, subs * ncf), subs * ncf)] = blocks[k]
    everything = gathered[...]
    own = dot(inverse[...], everything)
    x = [dot(halo.inverse(message), everything)] + [own[j * ncf : (j + 1) * ncf] for j in range(subs)]
    results, energy = coarse_products(ncf, x, base, gram)
    for e, share in enumerate(coarse_shares(ncf, results)):
        shares[e * ncf : (e + 1) * ncf] = share
    solution[...] = own
    sums[0:1] = quadratic[1:2] + column_sum(coarse[...] * own)
    sums[1:2] = quadratic[0:1] + energy
    faces = add_basis(nf, x, basis_high, basis_low, product)
    for e in range(subs + 1):
        part[e * nf : (e + 1) * nf] = faces[e]
    back[...] = faces[0].astype(BF16)
    forward[...] = faces[subs].astype(BF16)


def coarse_image(
    halo, half, crossed_half, inverse, message, shares, base, gram, quadratic, basis_high, basis_low, product, sums_in,
    sums, solution, part, back, gathered,
):
    ncf, nf = halo.ncf, halo.nf
    subs = inverse.shape[0] // ncf
    total = gathered.shape[0]
    for place, blocks, k in placed(half, crossed_half):
        gathered[pl.ds(pl.multiple_of(place * subs * ncf, subs * ncf), subs * ncf)] = blocks[k, ncf:].astype(F32)
    for place, blocks, k in placed(half, crossed_half):
        before = pl.multiple_of(lax.rem(place * subs * ncf + (total - ncf), total), ncf)
        gathered[pl.ds(before, ncf)] += blocks[k, :ncf].astype(F32)
    everything = gathered[...]
    own = split_dot(inverse[...], everything)
    x = [split_dot(halo.inverse(message), everything)] + [own[j * ncf : (j + 1) * ncf] for j in range(subs)]
    _, energy = coarse_products(ncf, x, base, gram)
    third = quadratic[1:2] + sum(column_sum(rows_of(shares, e, ncf) * x[e]) for e in range(subs + 1))
    fourth = quadratic[0:1] + energy
    for k in range(sums.shape[0]):
        sums[k, 0:2] = sums_in[0:2]
        sums[k, 2:3] = third
        sums[k, 3:4] = fourth
    solution[...] = own
    faces = add_basis(nf, x, basis_high, basis_low, product)
    for e in range(1, subs + 1):
        part[(e - 1) * nf : e * nf] = faces[e]
    back[...] = faces[0].astype(BF16)


def complete(halo, z_local, z_coarse, y_local, y_coarse, rows, z, y):
    ncf, nf = halo.ncf, halo.nf
    for j in range(rows.shape[0] // ncf):
        here, beside = slice(j * nf, (j + 1) * nf), slice((j + 1) * nf, (j + 2) * nf)
        for local, coarse, whole in ((z_local, z_coarse, z), (y_local, y_coarse, y)):
            whole[here] = local[beside] + split_dot(rows_of(rows, j, ncf), rows_of(coarse, j, ncf), dot_tn)


def combine(halo, sums, crossed_sums, load, z, y, image, part, from_next, solution, residual):
    nf = halo.nf
    total = sums[...] + crossed_sums[...]
    a, b, c, d = (total[k : k + 1] for k in range(4))
    step = a / b
    grow = step * (c / b)
    next_step = (grow - 1.0) / ((d - c * (c / b)) * (step / b))
    s = step + next_step * grow
    t = step * next_step
    solution[...] = s * z[...] - t * y[...]
    last = load.shape[0] - nf
    residual[:last] = load[:last] - s * image[:last] + t * part[:last]
    residual[last:] = load[last:] - s * image[last:] + t * (part[last:] + from_next[...].astype(F32))


def shards(right_side, face_weight, schur, neumann, constraint, coarse_inverse):
    subs, nf = face_weight.shape
    ncf = constraint.shape[0] // subs
    nco = coarse_inverse.shape[1]
    columns = right_side.shape[1]
    halo = Halo(nf, ncf, nco, columns)
    bind = lambda kernel: functools.partial(kernel, halo)
    faces, own = ((subs + 1) * nf, columns), (subs * nf, columns)
    coarse_own, local_rows = (subs * ncf, columns), 2 * subs * ncf
    halves = [((nf, columns), BF16)] * 2
    products = [(faces, F32), (faces, F32), ((8, columns), F32), ((local_rows, columns), F32)]
    semaphores = lambda count: [pltpu.SemaphoreType.DMA((count,))]
    described = lambda array: (array.shape, array.dtype)

    group = lax.axis_size(AXIS) // 2

    def gather(block):
        shape = (group,) + block.shape
        (copies,) = stage(bind(copy_out), [(shape, BF16)], block)
        return from_group(copies)

    outside = [pltpu.with_memory_space_constraint(x, pltpu.HBM) for x in (right_side, constraint, face_weight)]
    load, rows, weight, coarse = stage(
        bind(prepare),
        [described(right_side), described(constraint), described(face_weight), (coarse_own, F32)],
        *outside, scratch=semaphores(subs + 2), fetched=3,
    )
    (first,) = stage(bind(first_message), [((halo.first_height, columns), BF16)], load, weight, rows)
    half = gather(coarse)
    outside = [pltpu.with_memory_space_constraint(x, pltpu.HBM) for x in (neumann, schur, coarse_inverse)]
    outside, _ = lax.optimization_barrier((outside, first))
    neumann, schur, inverse = stage(
        bind(fetch), [described(array) for array in outside], *outside, scratch=semaphores(3), fetched=3
    )
    first = shifted(first, 1)
    part, back, forward = stage(
        bind(neumann_load), [(faces, F32), ((nf, columns), BF16), ((halo.second_height, columns), BF16)],
        load, weight, first, neumann, inverse, scratch=[pltpu.VMEM((halo.weight_count, columns), F32)],
    )
    half, _ = lax.optimization_barrier((half, back))
    crossed_half = crossed(half, 1)
    back, second = shifted(back, -1), shifted(forward, 1)
    long, wide = ((2 * subs * nf, 2 * ncf), BF16), ((local_rows, 2 * nf), BF16)
    basis_high, basis_low, turned_high, turned_low, gram = stage(
        bind(static_basis), [long, long, wide, wide, ((local_rows, LANES), F32)], schur, first, rows
    )
    z_local, product, quadratic, base = stage(
        bind(schur_load), products, load, part, back, second, weight, schur, turned_high, turned_low
    )
    shares, z_coarse, part, back, forward, sums = stage(
        bind(coarse_load),
        [(((subs + 1) * ncf, columns), F32), (coarse_own, F32), (faces, F32)] + halves + [((8, columns), F32)],
        half, crossed_half, inverse, second, coarse, base, gram, quadratic, basis_high, basis_low, product,
        scratch=[pltpu.VMEM((nco, columns), BF16)],
    )
    back, forward = shifted(back, -1), shifted(forward, 1)
    half = gather(shares)
    image, part, back, forward = stage(
        bind(neumann_image), [(own, F32), (faces, F32)] + halves, part, back, forward, weight, second, neumann
    )
    half, _ = lax.optimization_barrier((half, back))
    crossed_half = crossed(half, 1)
    back, forward = shifted(back, -1), shifted(forward, 1)
    y_local, product, quadratic, base = stage(
        bind(schur_image), products, image, part, back, forward, weight, second, schur, turned_high, turned_low
    )
    sums, y_coarse, part, back = stage(
        bind(coarse_image), [((group, 4, columns), F32), (coarse_own, F32), (own, F32), ((nf, columns), BF16)],
        half, crossed_half, inverse, second, shares, base, gram, quadratic, basis_high, basis_low, product, sums,
        scratch=[pltpu.VMEM((nco, columns), F32)],
    )
    sums = jnp.sum(from_group(sums), axis=0)
    crossed_sums = crossed(sums, 1)
    back = shifted(back, -1)
    z, y = stage(bind(complete), [(own, F32), (own, F32)], z_local, z_coarse, y_local, y_coarse, rows)
    return stage(bind(combine), [(own, F32), (own, F32)], sums, crossed_sums, load, z, y, image, part, back)


def solution(mesh):
    specs = P(("parts", AXIS), None)
    return jax.shard_map(shards, mesh=mesh, in_specs=(specs,) * 6, out_specs=(specs, specs), check_vma=False)
```

```python
import functools

import jax
import jax.numpy as jnp
from jax import lax
from jax.experimental import pallas as pl
from jax.experimental.pallas import tpu as pltpu
from jax.sharding import PartitionSpec as P

AXIS = "sub"
BF16 = jnp.bfloat16
F32 = jnp.float32
LANES = 128
VMEM_BYTES = 20 * 2**20


def shifted(block, distance):
    n = lax.axis_size(AXIS)
    return lax.ppermute(block, AXIS, [((i - distance) % n, i) for i in range(n)])


def crossed(block, bit):
    return lax.ppermute(block, AXIS, [(i, i ^ bit) for i in range(lax.axis_size(AXIS))])


def bits():
    return [1 << k for k in reversed(range(lax.axis_size(AXIS).bit_length() - 1))]


def after(value, *others):
    return lax.optimization_barrier((value, others))[0]


def gather_half(block, steps, *others):
    for bit in steps:
        block = jnp.concatenate([block, after(crossed(block, bit), *others)], axis=0)
    return block


def half_order():
    order = [0]
    for bit in bits()[:-1]:
        order += [place ^ bit for place in order]
    return order


def dot(a, b):
    return jnp.dot(a, b, preferred_element_type=F32)


def dot_nt(a, b):
    return lax.dot_general(a, b, (((1,), (1,)), ((), ())), preferred_element_type=F32)


def dot_tn(a, b):
    return lax.dot_general(a, b, (((0,), (0,)), ((), ())), preferred_element_type=F32)


def split(x):
    high = x.astype(BF16)
    return high, (x - high.astype(F32)).astype(BF16)


def split_dot(a, b, contract=dot):
    high, low = split(b)
    if isinstance(a, tuple):
        return contract(a[0], high) + contract(a[0], low) + contract(a[1], high)
    return contract(a, high) + contract(a, low)


def column_sum(x):
    return jnp.sum(x, axis=0, keepdims=True)


def rows_of(ref, index, count):
    return ref[index * count : (index + 1) * count]


def column_of(row):
    return jnp.broadcast_to(row, (8, row.shape[1])).T[:, :1]


def parts_of(row):
    high = row.astype(BF16).astype(F32)
    middle = (row - high).astype(BF16).astype(F32)
    return high, middle, row - high - middle


class Halo:
    def __init__(self, nf, ncf, nco, columns):
        self.nf, self.ncf, self.columns = nf, ncf, columns
        self.folds = nf // columns
        self.inverse_folds = nco // columns
        self.first_height = nf + ncf * self.folds
        self.at_weight = nf + ncf * self.inverse_folds
        self.weight_count = -(-3 * self.folds // 16) * 16
        self.second_height = self.at_weight + self.weight_count

    def unfolded(self, message, folds):
        start, ncf = self.nf, self.ncf
        return jnp.concatenate([message[start + k * ncf : start + (k + 1) * ncf] for k in range(folds)], axis=1)

    def fold(self, message, block, folds):
        start, ncf, columns = self.nf, self.ncf, self.columns
        for k in range(folds):
            message[start + k * ncf : start + (k + 1) * ncf] = block[:, k * columns : (k + 1) * columns]

    def product(self, message):
        return message[: self.nf].astype(F32)

    def rows(self, message):
        return self.unfolded(message, self.folds)

    def inverse(self, message):
        return self.unfolded(message, self.inverse_folds)

    def weight(self, message):
        got = message[self.at_weight : self.second_height].astype(F32)
        f = self.folds
        row = [sum(got[k * f + i : k * f + i + 1] for k in range(3)) for i in range(f)]
        return jnp.concatenate([column_of(piece) for piece in row], axis=0)


def all_rows(halo, message, rows):
    ncf = halo.ncf
    return [halo.rows(message)] + [rows_of(rows, j, ncf) for j in range(rows.shape[0] // ncf)]


def all_weights(halo, message, weight):
    return [halo.weight(message)] + [column_of(weight[j : j + 1]) for j in range(weight.shape[0])]


def stage(kernel, shapes, *operands, scratch=(), fetched=0):
    out = [jax.ShapeDtypeStruct(shape, dtype) for shape, dtype in shapes]
    params = pltpu.CompilerParams(vmem_limit_bytes=VMEM_BYTES)
    spaces = [pltpu.HBM] * fetched + [pltpu.VMEM] * (len(operands) - fetched)
    call = pl.pallas_call(
        kernel,
        out_shape=out,
        in_specs=[pl.BlockSpec(memory_space=space) for space in spaces],
        scratch_shapes=list(scratch),
        compiler_params=params,
        name=kernel.func.__name__,
    )
    return call(*operands)


def prepare(halo, load, rows, weight, load_here, rows_here, weight_here, coarse_rounded, coarse, done):
    ncf, nf = halo.ncf, halo.nf
    subs = load.shape[0] // nf
    copies = [pltpu.make_async_copy(rows, rows_here, done.at[subs])]
    copies += [
        pltpu.make_async_copy(rows_of(load.at, j, nf), rows_of(load_here.at, j, nf), done.at[j]) for j in range(subs)
    ]
    copies.append(pltpu.make_async_copy(weight, weight_here, done.at[subs + 1]))
    for copy in copies:
        copy.start()
    copies[0].wait()
    for j in range(subs):
        copies[1 + j].wait()
        coarse[j * ncf : (j + 1) * ncf] = dot(rows_of(rows_here, j, ncf), rows_of(load_here, j, nf).astype(BF16))
    coarse_rounded[...] = coarse[...].astype(BF16)
    copies[-1].wait()


def first_message(halo, load, weight, rows, message):
    ncf, nf = halo.ncf, halo.nf
    message[:nf] = ((1.0 - column_of(weight[weight.shape[0] - 1 :])) * load[load.shape[0] - nf :]).astype(BF16)
    halo.fold(message, rows[rows.shape[0] - ncf :], halo.folds)


def fetch(halo, neumann, schur, inverse, neumann_here, schur_here, inverse_here, done):
    pairs = ((neumann, neumann_here), (schur, schur_here), (inverse, inverse_here))
    copies = [pltpu.make_async_copy(source, here, done.at[k]) for k, (source, here) in enumerate(pairs)]
    for copy in copies:
        copy.start()
    for copy in copies:
        copy.wait()


def neumann_products(left, right, weights, neumann, part, back, forward):
    subs, nf = len(left), left[0].shape[0]
    previous = None
    for j in range(subs):
        product = dot(rows_of(neumann, j, 2 * nf), jnp.concatenate([left[j], right[j]], axis=0))
        first, second = product[:nf], product[nf:]
        if j == 0:
            part[:nf] = first
            back[...] = first.astype(BF16)
        else:
            part[j * nf : (j + 1) * nf] = weights[j] * previous + (1.0 - weights[j]) * first
        previous = second
    part[subs * nf :] = previous
    forward[:nf] = previous.astype(BF16)


def neumann_load(halo, load, weight, message, neumann, inverse, part, back, forward, pieces):
    subs, nf = weight.shape
    ncf, columns, folds = halo.ncf, halo.columns, halo.folds
    halo.fold(forward, inverse[inverse.shape[0] - ncf :], halo.inverse_folds)
    pieces[...] = jnp.zeros_like(pieces)
    for k, values in enumerate(parts_of(weight[subs - 1 : subs])):
        for i in range(folds):
            pieces[k * folds + i : k * folds + i + 1] = values[:, i * columns : (i + 1) * columns]
    forward[halo.at_weight :] = pieces[...].astype(BF16)
    weights = [None] + [column_of(weight[j : j + 1]) for j in range(subs)]
    left = [message[:nf]]
    left += [((1.0 - weights[j]) * rows_of(load, j - 1, nf)).astype(BF16) for j in range(1, subs)]
    right = [(weights[j + 1] * rows_of(load, j, nf)).astype(BF16) for j in range(subs)]
    neumann_products(left, right, weights, neumann, part, back, forward)


def neumann_image(halo, part_in, from_next, from_previous, weight, message, neumann, image, part, back, forward):
    subs, nf = weight.shape
    weights = all_weights(halo, message, weight)
    faces = [rows_of(part_in, e, nf) for e in range(subs + 1)]
    faces[0] = faces[0] + from_previous[...].astype(F32)
    faces[subs] = faces[subs] + from_next[...].astype(F32)
    for e in range(1, subs + 1):
        image[(e - 1) * nf : e * nf] = faces[e]
    left = [((1.0 - weights[j]) * faces[j]).astype(BF16) for j in range(subs)]
    right = [(weights[j + 1] * faces[j + 1]).astype(BF16) for j in range(subs)]
    neumann_products(left, right, weights, neumann, part, back, forward)


def static_basis(halo, schur, message, rows, basis_high, basis_low, turned_high, turned_low, gram):
    ncf, nf = halo.ncf, halo.nf
    blocks = all_rows(halo, message, rows)
    gram[...] = jnp.zeros_like(gram)
    for j in range(len(blocks) - 1):
        matrix, pair = rows_of(schur, j, 2 * nf), blocks[j : j + 2]
        basis = jnp.concatenate([dot_nt(matrix[:, k * nf : (k + 1) * nf], pair[k]) for k in range(2)], axis=1)
        long, wide = slice(2 * j * nf, 2 * (j + 1) * nf), slice(2 * j * ncf, 2 * (j + 1) * ncf)
        basis_high[long], basis_low[long] = split(basis)
        turned = split(basis.T)
        turned_high[wide], turned_low[wide] = turned
        for k in range(2):
            half = slice(k * nf, (k + 1) * nf)
            gram[wide, k * ncf : (k + 1) * ncf] = dot_nt(turned[0][:, half], pair[k]) + dot_nt(turned[1][:, half], pair[k])


def schur_products(
    halo, other, part, from_next, from_previous, weight, message, schur, turned_high, turned_low,
    local, product, quadratic, base,
):
    subs, nf = weight.shape
    ncf, columns = halo.ncf, halo.columns
    weights = all_weights(halo, message, weight)
    local[:nf] = (1.0 - weights[0]) * part[:nf] + weights[0] * halo.product(from_previous)
    for e in range(1, subs):
        local[e * nf : (e + 1) * nf] = rows_of(part, e, nf)
    local[subs * nf :] = weights[subs] * part[subs * nf :] + (1.0 - weights[subs]) * from_next[...].astype(F32)
    energy, previous = 0.0, None
    for j in range(subs):
        vector = local[j * nf : (j + 2) * nf]
        high, low = split(vector)
        both = dot(rows_of(schur, j, 2 * nf), jnp.concatenate([high, low], axis=1))
        result = both[:, :columns] + both[:, columns:]
        energy = energy + column_sum(vector * result)
        first = result[:nf]
        product[j * nf : (j + 1) * nf] = first if j == 0 else previous + first
        previous = result[nf:]
        here = slice(2 * j * ncf, 2 * (j + 1) * ncf)
        base[here] = dot(turned_high[here], high) + dot(turned_high[here], low) + dot(turned_low[here], high)
    product[subs * nf :] = previous
    quadratic[0:1] = energy
    quadratic[1:2] = column_sum(other[...] * local[nf:])


def schur_load(halo, load, part, from_next, from_previous, weight, schur, turned_high, turned_low, *outs):
    schur_products(
        halo, load, part, from_next, from_previous, weight, from_previous, schur, turned_high, turned_low, *outs
    )


def schur_image(halo, *refs):
    schur_products(halo, *refs)


def placed(half, crossed_half):
    me = lax.axis_index(AXIS)
    order = half_order()
    count = half.shape[0] // len(order)
    for flip, blocks in ((0, half), (1, crossed_half)):
        for k, place in enumerate(order):
            yield me ^ (place ^ flip), blocks, k * count, (k + 1) * count


def coarse_shares(ncf, results):
    shares = [results[0][:ncf]]
    for before, after in zip(results[:-1], results[1:]):
        shares.append(before[ncf:] + after[:ncf])
    return shares + [results[-1][ncf:]]


def coarse_products(ncf, x, base, gram):
    results, energy = [], 0.0
    for j in range(len(x) - 1):
        here = slice(2 * j * ncf, 2 * (j + 1) * ncf)
        pair = jnp.concatenate([x[j], x[j + 1]], axis=0)
        change = split_dot(split(gram[here, : 2 * ncf]), pair)
        energy = energy + column_sum(pair * (2.0 * base[here] + change))
        results.append(base[here] + change)
    return results, energy


def add_basis(nf, x, basis_high, basis_low, product):
    faces = [rows_of(product, e, nf) for e in range(len(x))]
    for j in range(len(x) - 1):
        here = slice(2 * j * nf, 2 * (j + 1) * nf)
        pair = jnp.concatenate([x[j], x[j + 1]], axis=0)
        change = split_dot((basis_high[here], basis_low[here]), pair)
        faces[j] = faces[j] + change[:nf]
        faces[j + 1] = faces[j + 1] + change[nf:]
    return faces


def coarse_load(
    halo, half, crossed_half, inverse, message, coarse, base, gram, quadratic, basis_high, basis_low, product,
    shares_rounded, shares, solution, part, back, forward, sums, gathered,
):
    ncf, nf = halo.ncf, halo.nf
    subs = inverse.shape[0] // ncf
    for place, blocks, start, stop in placed(half, crossed_half):
        gathered[pl.ds(pl.multiple_of(place * subs * ncf, subs * ncf), subs * ncf)] = blocks[start:stop]
    everything = gathered[...]
    own = dot(inverse[...], everything)
    x = [dot(halo.inverse(message), everything)] + [own[j * ncf : (j + 1) * ncf] for j in range(subs)]
    results, energy = coarse_products(ncf, x, base, gram)
    for e, share in enumerate(coarse_shares(ncf, results)):
        shares[e * ncf : (e + 1) * ncf] = share
    shares_rounded[...] = shares[...].astype(BF16)
    solution[...] = own
    sums[0:1] = quadratic[1:2] + column_sum(coarse[...] * own)
    sums[1:2] = quadratic[0:1] + energy
    faces = add_basis(nf, x, basis_high, basis_low, product)
    for e in range(subs + 1):
        part[e * nf : (e + 1) * nf] = faces[e]
    back[...] = faces[0].astype(BF16)
    forward[...] = faces[subs].astype(BF16)


def coarse_image(
    halo, half, crossed_half, inverse, message, shares, base, gram, quadratic, basis_high, basis_low, product, sums_in,
    sums, solution, part, back, gathered,
):
    ncf, nf = halo.ncf, halo.nf
    subs = inverse.shape[0] // ncf
    total = gathered.shape[0]
    for place, blocks, start, stop in placed(half, crossed_half):
        gathered[pl.ds(pl.multiple_of(place * subs * ncf, subs * ncf), subs * ncf)] = blocks[start + ncf : stop].astype(F32)
    for place, blocks, start, stop in placed(half, crossed_half):
        before = pl.multiple_of(lax.rem(place * subs * ncf + (total - ncf), total), ncf)
        gathered[pl.ds(before, ncf)] += blocks[start : start + ncf].astype(F32)
    everything = gathered[...]
    own = split_dot(inverse[...], everything)
    x = [split_dot(halo.inverse(message), everything)] + [own[j * ncf : (j + 1) * ncf] for j in range(subs)]
    _, energy = coarse_products(ncf, x, base, gram)
    sums[0:2] = sums_in[0:2]
    sums[2:3] = quadratic[1:2] + sum(column_sum(rows_of(shares, e, ncf) * x[e]) for e in range(subs + 1))
    sums[3:4] = quadratic[0:1] + energy
    solution[...] = own
    faces = add_basis(nf, x, basis_high, basis_low, product)
    for e in range(1, subs + 1):
        part[(e - 1) * nf : e * nf] = faces[e]
    back[...] = faces[0].astype(BF16)


def complete(halo, z_local, z_coarse, y_local, y_coarse, rows, z, y):
    ncf, nf = halo.ncf, halo.nf
    for j in range(rows.shape[0] // ncf):
        here, beside = slice(j * nf, (j + 1) * nf), slice((j + 1) * nf, (j + 2) * nf)
        for local, coarse, whole in ((z_local, z_coarse, z), (y_local, y_coarse, y)):
            whole[here] = local[beside] + split_dot(rows_of(rows, j, ncf), rows_of(coarse, j, ncf), dot_tn)


def combine(halo, sums, load, z, y, image, part, from_next, solution, residual):
    nf = halo.nf
    a, b, c, d = (sums[k : k + 1] for k in range(4))
    step = a / b
    grow = step * (c / b)
    next_step = (grow - 1.0) / ((d - c * (c / b)) * (step / b))
    s = step + next_step * grow
    t = step * next_step
    solution[...] = s * z[...] - t * y[...]
    last = load.shape[0] - nf
    residual[:last] = load[:last] - s * image[:last] + t * part[:last]
    residual[last:] = load[last:] - s * image[last:] + t * (part[last:] + from_next[...].astype(F32))


def shards(right_side, face_weight, schur, neumann, constraint, coarse_inverse):
    subs, nf = face_weight.shape
    ncf = constraint.shape[0] // subs
    nco = coarse_inverse.shape[1]
    columns = right_side.shape[1]
    halo = Halo(nf, ncf, nco, columns)
    bind = lambda kernel: functools.partial(kernel, halo)
    faces, own = ((subs + 1) * nf, columns), (subs * nf, columns)
    coarse_own, local_rows = (subs * ncf, columns), 2 * subs * ncf
    halves = [((nf, columns), BF16)] * 2
    products = [(faces, F32), (faces, F32), ((8, columns), F32), ((local_rows, columns), F32)]
    semaphores = lambda count: [pltpu.SemaphoreType.DMA((count,))]
    described = lambda array: (array.shape, array.dtype)
    outside = lambda array: pltpu.with_memory_space_constraint(array, pltpu.HBM)
    steps = bits()
    early, late = steps[:-2], steps[-2:-1]

    load, rows, weight, coarse_rounded, coarse = stage(
        bind(prepare),
        [described(right_side), described(constraint), described(face_weight), (coarse_own, BF16), (coarse_own, F32)],
        *map(outside, (right_side, constraint, face_weight)), scratch=semaphores(subs + 2), fetched=3,
    )
    (first,) = stage(bind(first_message), [((halo.first_height, columns), BF16)], load, weight, rows)
    half = gather_half(coarse_rounded, early[:1])
    tied = after(tuple(map(outside, (neumann, schur, coarse_inverse))), first)
    neumann, schur, inverse = stage(
        bind(fetch), [described(array) for array in tied], *tied, scratch=semaphores(3), fetched=3
    )
    first = after(shifted(first, 1), half)
    part, back, forward = stage(
        bind(neumann_load), [(faces, F32), ((nf, columns), BF16), ((halo.second_height, columns), BF16)],
        load, weight, first, neumann, inverse, scratch=[pltpu.VMEM((halo.weight_count, columns), F32)],
    )
    half = gather_half(half, early[1:], back)
    back, second = shifted(back, -1), shifted(forward, 1)
    long, wide = ((2 * subs * nf, 2 * ncf), BF16), ((local_rows, 2 * nf), BF16)
    basis_high, basis_low, turned_high, turned_low, gram = stage(
        bind(static_basis), [long, long, wide, wide, ((local_rows, LANES), F32)], schur, first, rows
    )
    half = gather_half(half, late, back, second, gram)
    crossed_half = crossed(half, 1)
    part = after(part, half)
    z_local, product, quadratic, base = stage(
        bind(schur_load), products, load, part, back, second, weight, schur, turned_high, turned_low
    )
    share_rows = ((subs + 1) * ncf, columns)
    shares_rounded, shares, z_coarse, part, back, forward, sums = stage(
        bind(coarse_load),
        [(share_rows, BF16), (share_rows, F32), (coarse_own, F32), (faces, F32)] + halves + [((8, columns), F32)],
        half, crossed_half, inverse, second, coarse, base, gram, quadratic, basis_high, basis_low, product,
        scratch=[pltpu.VMEM((nco, columns), BF16)],
    )
    half = gather_half(shares_rounded, early[:1])
    back, forward = shifted(back, -1), shifted(forward, 1)
    image, part, back, forward = stage(
        bind(neumann_image), [(own, F32), (faces, F32)] + halves, part, back, forward, weight, second, neumann
    )
    half = gather_half(half, early[1:], back)
    back, forward = shifted(back, -1), shifted(forward, 1)
    half = gather_half(half, late, back, forward)
    crossed_half = crossed(half, 1)
    part = after(part, half)
    y_local, product, quadratic, base = stage(
        bind(schur_image), products, image, part, back, forward, weight, second, schur, turned_high, turned_low
    )
    sums, y_coarse, part, back = stage(
        bind(coarse_image), [((4, columns), F32), (coarse_own, F32), (own, F32), ((nf, columns), BF16)],
        half, crossed_half, inverse, second, shares, base, gram, quadratic, basis_high, basis_low, product, sums,
        scratch=[pltpu.VMEM((nco, columns), F32)],
    )
    for bit in early:
        sums = sums + crossed(sums, bit)
    z, y = stage(bind(complete), [(own, F32), (own, F32)], z_local, z_coarse, after(y_local, sums), y_coarse, rows)
    for bit in steps[-2:]:
        sums = sums + crossed(sums, bit)
    back = shifted(after(back, y), -1)
    return stage(bind(combine), [(own, F32), (own, F32)], sums, load, z, y, image, part, back)


def solution(mesh):
    specs = P(("parts", AXIS), None)
    return jax.shard_map(shards, mesh=mesh, in_specs=(specs,) * 6, out_specs=(specs, specs), check_vma=False)
```

```python
import functools

import jax
import jax.numpy as jnp
from jax import lax
from jax.experimental import pallas as pl
from jax.experimental.pallas import tpu as pltpu
from jax.sharding import PartitionSpec as P

AXIS = "sub"
BF16 = jnp.bfloat16
F32 = jnp.float32
LANES = 128
VMEM_BYTES = 20 * 2**20


def shifted(block, distance):
    n = lax.axis_size(AXIS)
    return lax.ppermute(block, AXIS, [((i - distance) % n, i) for i in range(n)])


def crossed(block, bit):
    return lax.ppermute(block, AXIS, [(i, i ^ bit) for i in range(lax.axis_size(AXIS))])


def far_block(block):
    n = lax.axis_size(AXIS)
    return lax.ppermute(block, AXIS, [(i, (i + (1 if i % 2 else -1)) % n) for i in range(n)])


def bits():
    order = [1 << k for k in reversed(range(lax.axis_size(AXIS).bit_length() - 1))]
    return order[:-3] + order[-2:-1] + order[-3:-2] + order[-1:]


def after(value, *others):
    return lax.optimization_barrier((value, others))[0]


def gather_half(block, steps, *others):
    for bit in steps:
        block = jnp.concatenate([block, after(crossed(block, bit), *others)], axis=0)
    return block


def half_order():
    order = [0]
    for bit in bits()[:-1]:
        order += [place ^ bit for place in order]
    return order


def dot(a, b):
    return jnp.dot(a, b, preferred_element_type=F32)


def dot_nt(a, b):
    return lax.dot_general(a, b, (((1,), (1,)), ((), ())), preferred_element_type=F32)


def dot_tn(a, b):
    return lax.dot_general(a, b, (((0,), (0,)), ((), ())), preferred_element_type=F32)


def split(x):
    high = x.astype(BF16)
    return high, (x - high.astype(F32)).astype(BF16)


def split_dot(a, b, contract=dot):
    high, low = split(b)
    if isinstance(a, tuple):
        return contract(a[0], high) + contract(a[0], low) + contract(a[1], high)
    return contract(a, high) + contract(a, low)


def column_sum(x):
    return jnp.sum(x, axis=0, keepdims=True)


def rows_of(ref, index, count):
    return ref[index * count : (index + 1) * count]


def column_of(row):
    return jnp.broadcast_to(row, (8, row.shape[1])).T[:, :1]


def parts_of(row):
    high = row.astype(BF16).astype(F32)
    middle = (row - high).astype(BF16).astype(F32)
    return high, middle, row - high - middle


class Halo:
    def __init__(self, nf, ncf, nco, columns):
        self.nf, self.ncf, self.columns = nf, ncf, columns
        self.folds = nf // columns
        self.at_inverse = nf + ncf * self.folds
        self.at_weight = self.at_inverse + ncf * (nco // columns)
        self.weight_count = -(-3 * self.folds // 16) * 16
        self.height = self.at_weight + self.weight_count

    def unfolded(self, message, start, stop):
        return jnp.concatenate([message[k : k + self.ncf] for k in range(start, stop, self.ncf)], axis=1)

    def fold(self, message, block, start):
        ncf, columns = self.ncf, self.columns
        for k in range(block.shape[1] // columns):
            message[start + k * ncf : start + (k + 1) * ncf] = block[:, k * columns : (k + 1) * columns]

    def rows(self, message):
        return self.unfolded(message, self.nf, self.at_inverse)

    def inverse(self, message):
        return self.unfolded(message, self.at_inverse, self.at_weight)

    def weight(self, message):
        got = message[self.at_weight : self.height].astype(F32)
        f = self.folds
        row = [sum(got[k * f + i : k * f + i + 1] for k in range(3)) for i in range(f)]
        return jnp.concatenate([column_of(piece) for piece in row], axis=0)


def all_rows(halo, message, rows):
    ncf = halo.ncf
    return [halo.rows(message)] + [rows_of(rows, j, ncf) for j in range(rows.shape[0] // ncf)]


def is_odd():
    return lax.rem(lax.axis_index(AXIS), 2) == 1


def send(first, second, near, far):
    first, second, odd = first.astype(BF16), second.astype(BF16), is_odd()
    near[...] = jnp.where(odd, first, second)
    far[...] = jnp.where(odd, second, first)


def received(near, far):
    near, far, odd = near[...].astype(F32), far[...].astype(F32), is_odd()
    return jnp.where(odd, far, near), jnp.where(odd, near, far)


def all_weights(halo, message, weight):
    return [halo.weight(message)] + [column_of(weight[j : j + 1]) for j in range(weight.shape[0])]


def stage(kernel, shapes, *operands, scratch=(), fetched=0):
    out = [jax.ShapeDtypeStruct(shape, dtype) for shape, dtype in shapes]
    params = pltpu.CompilerParams(vmem_limit_bytes=VMEM_BYTES)
    spaces = [pltpu.HBM] * fetched + [pltpu.VMEM] * (len(operands) - fetched)
    call = pl.pallas_call(
        kernel,
        out_shape=out,
        in_specs=[pl.BlockSpec(memory_space=space) for space in spaces],
        scratch_shapes=list(scratch),
        compiler_params=params,
        name=kernel.func.__name__,
    )
    return call(*operands)


def prepare(
    halo, load, rows, weight, inverse, load_here, rows_here, weight_here, inverse_here, coarse_rounded, coarse, done
):
    ncf, nf = halo.ncf, halo.nf
    subs = load.shape[0] // nf
    copies = [pltpu.make_async_copy(rows, rows_here, done.at[subs])]
    copies += [
        pltpu.make_async_copy(rows_of(load.at, j, nf), rows_of(load_here.at, j, nf), done.at[j]) for j in range(subs)
    ]
    copies.append(pltpu.make_async_copy(weight, weight_here, done.at[subs + 1]))
    copies.append(pltpu.make_async_copy(inverse, inverse_here, done.at[subs + 2]))
    for copy in copies:
        copy.start()
    copies[0].wait()
    for j in range(subs):
        copies[1 + j].wait()
        coarse[j * ncf : (j + 1) * ncf] = dot(rows_of(rows_here, j, ncf), rows_of(load_here, j, nf).astype(BF16))
    coarse_rounded[...] = coarse[...].astype(BF16)
    copies[-2].wait()
    copies[-1].wait()


def halo_message(halo, load, weight, rows, inverse, message, pieces):
    ncf, nf, columns, folds = halo.ncf, halo.nf, halo.columns, halo.folds
    last = weight[weight.shape[0] - 1 :]
    message[:nf] = ((1.0 - column_of(last)) * load[load.shape[0] - nf :]).astype(BF16)
    halo.fold(message, rows[rows.shape[0] - ncf :], nf)
    halo.fold(message, inverse[inverse.shape[0] - ncf :], halo.at_inverse)
    pieces[...] = jnp.zeros_like(pieces)
    for k, values in enumerate(parts_of(last)):
        for i in range(folds):
            pieces[k * folds + i : k * folds + i + 1] = values[:, i * columns : (i + 1) * columns]
    message[halo.at_weight :] = pieces[...].astype(BF16)


def fetch(halo, neumann, schur, neumann_here, schur_here, done):
    pairs = ((neumann, neumann_here), (schur, schur_here))
    copies = [pltpu.make_async_copy(source, here, done.at[k]) for k, (source, here) in enumerate(pairs)]
    for copy in copies:
        copy.start()
    for copy in copies:
        copy.wait()


def neumann_products(left, right, weights, neumann, part, near, far):
    subs, nf = len(left), left[0].shape[0]
    previous = None
    for j in range(subs):
        product = dot(rows_of(neumann, j, 2 * nf), jnp.concatenate([left[j], right[j]], axis=0))
        first, second = product[:nf], product[nf:]
        if j == 0:
            part[:nf] = outer = first
        else:
            part[j * nf : (j + 1) * nf] = weights[j] * previous + (1.0 - weights[j]) * first
        previous = second
    part[subs * nf :] = previous
    send(outer, previous, near, far)


def neumann_load(halo, load, weight, message, neumann, part, near, far):
    subs, nf = weight.shape
    weights = [None] + [column_of(weight[j : j + 1]) for j in range(subs)]
    left = [message[:nf]]
    left += [((1.0 - weights[j]) * rows_of(load, j - 1, nf)).astype(BF16) for j in range(1, subs)]
    right = [(weights[j + 1] * rows_of(load, j, nf)).astype(BF16) for j in range(subs)]
    neumann_products(left, right, weights, neumann, part, near, far)


def neumann_image(halo, part_in, near_in, far_in, weight, message, neumann, image, part, near, far):
    subs, nf = weight.shape
    weights = all_weights(halo, message, weight)
    faces = [rows_of(part_in, e, nf) for e in range(subs + 1)]
    from_next, from_previous = received(near_in, far_in)
    faces[0] = faces[0] + from_previous
    faces[subs] = faces[subs] + from_next
    for e in range(1, subs + 1):
        image[(e - 1) * nf : e * nf] = faces[e]
    left = [((1.0 - weights[j]) * faces[j]).astype(BF16) for j in range(subs)]
    right = [(weights[j + 1] * faces[j + 1]).astype(BF16) for j in range(subs)]
    neumann_products(left, right, weights, neumann, part, near, far)


def static_basis(halo, schur, message, rows, basis_high, basis_low, turned_high, turned_low, gram):
    ncf, nf = halo.ncf, halo.nf
    blocks = all_rows(halo, message, rows)
    gram[...] = jnp.zeros_like(gram)
    for j in range(len(blocks) - 1):
        matrix, pair = rows_of(schur, j, 2 * nf), blocks[j : j + 2]
        basis = jnp.concatenate([dot_nt(matrix[:, k * nf : (k + 1) * nf], pair[k]) for k in range(2)], axis=1)
        long, wide = slice(2 * j * nf, 2 * (j + 1) * nf), slice(2 * j * ncf, 2 * (j + 1) * ncf)
        basis_high[long], basis_low[long] = split(basis)
        turned = split(basis.T)
        turned_high[wide], turned_low[wide] = turned
        for k in range(2):
            half = slice(k * nf, (k + 1) * nf)
            gram[wide, k * ncf : (k + 1) * ncf] = dot_nt(turned[0][:, half], pair[k]) + dot_nt(turned[1][:, half], pair[k])


def schur_products(
    halo, other, part, near, far, weight, message, schur, turned_high, turned_low, local, product, quadratic, base
):
    subs, nf = weight.shape
    ncf, columns = halo.ncf, halo.columns
    weights = all_weights(halo, message, weight)
    from_next, from_previous = received(near, far)
    local[:nf] = (1.0 - weights[0]) * part[:nf] + weights[0] * from_previous
    for e in range(1, subs):
        local[e * nf : (e + 1) * nf] = rows_of(part, e, nf)
    local[subs * nf :] = weights[subs] * part[subs * nf :] + (1.0 - weights[subs]) * from_next
    energy, previous = 0.0, None
    for j in range(subs):
        vector = local[j * nf : (j + 2) * nf]
        high, low = split(vector)
        both = dot(rows_of(schur, j, 2 * nf), jnp.concatenate([high, low], axis=1))
        result = both[:, :columns] + both[:, columns:]
        energy = energy + column_sum(vector * result)
        first = result[:nf]
        product[j * nf : (j + 1) * nf] = first if j == 0 else previous + first
        previous = result[nf:]
        here = slice(2 * j * ncf, 2 * (j + 1) * ncf)
        base[here] = dot(turned_high[here], high) + dot(turned_high[here], low) + dot(turned_low[here], high)
    product[subs * nf :] = previous
    quadratic[0:1] = energy
    quadratic[1:2] = column_sum(other[...] * local[nf:])


def placed(half, crossed_half):
    me = lax.axis_index(AXIS)
    order = half_order()
    count = half.shape[0] // len(order)
    for flip, blocks in ((0, half), (1, crossed_half)):
        for k, place in enumerate(order):
            yield me ^ (place ^ flip), blocks, k * count, (k + 1) * count


def coarse_shares(ncf, results):
    shares = [results[0][:ncf]]
    for before, after in zip(results[:-1], results[1:]):
        shares.append(before[ncf:] + after[:ncf])
    return shares + [results[-1][ncf:]]


def coarse_products(ncf, x, base, gram):
    results, energy = [], 0.0
    for j in range(len(x) - 1):
        here = slice(2 * j * ncf, 2 * (j + 1) * ncf)
        pair = jnp.concatenate([x[j], x[j + 1]], axis=0)
        change = split_dot(split(gram[here, : 2 * ncf]), pair)
        energy = energy + column_sum(pair * (2.0 * base[here] + change))
        results.append(base[here] + change)
    return results, energy


def add_basis(nf, x, basis_high, basis_low, product):
    faces = [rows_of(product, e, nf) for e in range(len(x))]
    for j in range(len(x) - 1):
        here = slice(2 * j * nf, 2 * (j + 1) * nf)
        pair = jnp.concatenate([x[j], x[j + 1]], axis=0)
        change = split_dot((basis_high[here], basis_low[here]), pair)
        faces[j] = faces[j] + change[:nf]
        faces[j + 1] = faces[j + 1] + change[nf:]
    return faces


def coarse_load(
    halo, half, crossed_half, inverse, message, coarse, base, gram, quadratic, basis_high, basis_low, product,
    shares_rounded, shares, solution, part, near, far, sums, gathered,
):
    ncf, nf = halo.ncf, halo.nf
    subs = inverse.shape[0] // ncf
    for place, blocks, start, stop in placed(half, crossed_half):
        gathered[pl.ds(pl.multiple_of(place * subs * ncf, subs * ncf), subs * ncf)] = blocks[start:stop]
    everything = gathered[...]
    own = dot(inverse[...], everything)
    x = [dot(halo.inverse(message), everything)] + [own[j * ncf : (j + 1) * ncf] for j in range(subs)]
    results, energy = coarse_products(ncf, x, base, gram)
    for e, share in enumerate(coarse_shares(ncf, results)):
        shares[e * ncf : (e + 1) * ncf] = share
    shares_rounded[...] = shares[...].astype(BF16)
    solution[...] = own
    sums[0:1] = quadratic[1:2] + column_sum(coarse[...] * own)
    sums[1:2] = quadratic[0:1] + energy
    faces = add_basis(nf, x, basis_high, basis_low, product)
    for e in range(subs + 1):
        part[e * nf : (e + 1) * nf] = faces[e]
    send(faces[0], faces[subs], near, far)


def coarse_image(
    halo, half, crossed_half, inverse, message, shares, base, gram, quadratic, basis_high, basis_low, product, sums_in,
    sums, solution, part, back, gathered,
):
    ncf, nf = halo.ncf, halo.nf
    subs = inverse.shape[0] // ncf
    total = gathered.shape[0]
    for place, blocks, start, stop in placed(half, crossed_half):
        gathered[pl.ds(pl.multiple_of(place * subs * ncf, subs * ncf), subs * ncf)] = blocks[start + ncf : stop].astype(F32)
    for place, blocks, start, stop in placed(half, crossed_half):
        before = pl.multiple_of(lax.rem(place * subs * ncf + (total - ncf), total), ncf)
        gathered[pl.ds(before, ncf)] += blocks[start : start + ncf].astype(F32)
    everything = gathered[...]
    own = split_dot(inverse[...], everything)
    x = [split_dot(halo.inverse(message), everything)] + [own[j * ncf : (j + 1) * ncf] for j in range(subs)]
    _, energy = coarse_products(ncf, x, base, gram)
    sums[0:2] = sums_in[0:2]
    sums[2:3] = quadratic[1:2] + sum(column_sum(rows_of(shares, e, ncf) * x[e]) for e in range(subs + 1))
    sums[3:4] = quadratic[0:1] + energy
    solution[...] = own
    faces = add_basis(nf, x, basis_high, basis_low, product)
    for e in range(1, subs + 1):
        part[(e - 1) * nf : e * nf] = faces[e]
    back[...] = faces[0].astype(BF16)


def complete(halo, z_local, z_coarse, y_local, y_coarse, rows, z, y):
    ncf, nf = halo.ncf, halo.nf
    for j in range(rows.shape[0] // ncf):
        here, beside = slice(j * nf, (j + 1) * nf), slice((j + 1) * nf, (j + 2) * nf)
        for local, coarse, whole in ((z_local, z_coarse, z), (y_local, y_coarse, y)):
            whole[here] = local[beside] + split_dot(rows_of(rows, j, ncf), rows_of(coarse, j, ncf), dot_tn)


def combine(halo, sums, load, z, y, image, part, from_next, solution, residual):
    nf = halo.nf
    a, b, c, d = (sums[k : k + 1] for k in range(4))
    step = a / b
    grow = step * (c / b)
    next_step = (grow - 1.0) / ((d - c * (c / b)) * (step / b))
    s = step + next_step * grow
    t = step * next_step
    solution[...] = s * z[...] - t * y[...]
    last = load.shape[0] - nf
    residual[:last] = load[:last] - s * image[:last] + t * part[:last]
    residual[last:] = load[last:] - s * image[last:] + t * (part[last:] + from_next[...].astype(F32))


def shards(right_side, face_weight, schur, neumann, constraint, coarse_inverse):
    subs, nf = face_weight.shape
    ncf = constraint.shape[0] // subs
    nco = coarse_inverse.shape[1]
    columns = right_side.shape[1]
    halo = Halo(nf, ncf, nco, columns)
    bind = lambda kernel: functools.partial(kernel, halo)
    faces, own = ((subs + 1) * nf, columns), (subs * nf, columns)
    coarse_own, local_rows = (subs * ncf, columns), 2 * subs * ncf
    halves = [((nf, columns), BF16)] * 2
    products = [(faces, F32), (faces, F32), ((8, columns), F32), ((local_rows, columns), F32)]
    semaphores = lambda count: [pltpu.SemaphoreType.DMA((count,))]
    described = lambda array: (array.shape, array.dtype)
    outside = lambda array: pltpu.with_memory_space_constraint(array, pltpu.HBM)
    steps = bits()
    early, late = steps[:-2], steps[-2:-1]

    load, rows, weight, inverse, coarse_rounded, coarse = stage(
        bind(prepare),
        [described(right_side), described(constraint), described(face_weight), described(coarse_inverse)]
        + [(coarse_own, BF16), (coarse_own, F32)],
        *map(outside, (right_side, constraint, face_weight, coarse_inverse)), scratch=semaphores(subs + 3), fetched=4,
    )
    (message,) = stage(
        bind(halo_message), [((halo.height, columns), BF16)], load, weight, rows, inverse,
        scratch=[pltpu.VMEM((halo.weight_count, columns), F32)],
    )
    half = gather_half(coarse_rounded, early[:1])
    tied = after(tuple(map(outside, (neumann, schur))), message, half)
    neumann, schur = stage(
        bind(fetch), [described(array) for array in tied], *tied, scratch=semaphores(2), fetched=2
    )
    half = gather_half(half, early[1:])
    message = after(shifted(message, 1), half)
    part, near, far = stage(
        bind(neumann_load), [(faces, F32)] + halves, load, weight, message, neumann
    )
    far, near = far_block(far), crossed(near, 1)
    long, wide = ((2 * subs * nf, 2 * ncf), BF16), ((local_rows, 2 * nf), BF16)
    basis_high, basis_low, turned_high, turned_low, gram = stage(
        bind(static_basis), [long, long, wide, wide, ((local_rows, LANES), F32)], schur, message, rows
    )
    half = gather_half(half, late, near, far, gram)
    crossed_half = crossed(half, 1)
    part = after(part, half)
    z_local, product, quadratic, base = stage(
        bind(schur_products), products, load, part, near, far, weight, message, schur, turned_high, turned_low
    )
    share_rows = ((subs + 1) * ncf, columns)
    shares_rounded, shares, z_coarse, part, near, far, sums = stage(
        bind(coarse_load),
        [(share_rows, BF16), (share_rows, F32), (coarse_own, F32), (faces, F32)] + halves + [((8, columns), F32)],
        half, crossed_half, inverse, message, coarse, base, gram, quadratic, basis_high, basis_low, product,
        scratch=[pltpu.VMEM((nco, columns), BF16)],
    )
    far, near = far_block(far), crossed(near, 1)
    half = gather_half(shares_rounded, early[:1])
    image, part, near, far = stage(
        bind(neumann_image), [(own, F32), (faces, F32)] + halves, part, near, far, weight, message, neumann
    )
    half = gather_half(half, early[1:], far)
    far, near = far_block(far), crossed(near, 1)
    half = gather_half(half, late, near, far)
    crossed_half = crossed(half, 1)
    part = after(part, half)
    y_local, product, quadratic, base = stage(
        bind(schur_products), products, image, part, near, far, weight, message, schur, turned_high, turned_low
    )
    sums, y_coarse, part, back = stage(
        bind(coarse_image), [((4, columns), F32), (coarse_own, F32), (own, F32), ((nf, columns), BF16)],
        half, crossed_half, inverse, message, shares, base, gram, quadratic, basis_high, basis_low, product, sums,
        scratch=[pltpu.VMEM((nco, columns), F32)],
    )
    for bit in early:
        sums = sums + crossed(sums, bit)
    z, y = stage(bind(complete), [(own, F32), (own, F32)], z_local, z_coarse, after(y_local, sums), y_coarse, rows)
    for bit in steps[-2:]:
        sums = sums + crossed(sums, bit)
    back = shifted(after(back, y), -1)
    return stage(bind(combine), [(own, F32), (own, F32)], sums, load, z, y, image, part, back)


def solution(mesh):
    specs = P(("parts", AXIS), None)
    return jax.shard_map(shards, mesh=mesh, in_specs=(specs,) * 6, out_specs=(specs, specs), check_vma=False)
```

```python
import functools

import jax
import jax.numpy as jnp
from jax import lax
from jax.experimental import pallas as pl
from jax.experimental.pallas import tpu as pltpu
from jax.sharding import PartitionSpec as P

AXIS = "sub"
BF16 = jnp.bfloat16
F32 = jnp.float32
LANES = 128
VMEM_BYTES = 20 * 2**20


def shifted(block, distance):
    n = lax.axis_size(AXIS)
    return lax.ppermute(block, AXIS, [((i - distance) % n, i) for i in range(n)])


def crossed(block, bit):
    return lax.ppermute(block, AXIS, [(i, i ^ bit) for i in range(lax.axis_size(AXIS))])


def far_block(block):
    n = lax.axis_size(AXIS)
    return lax.ppermute(block, AXIS, [(i, (i + (1 if i % 2 else -1)) % n) for i in range(n)])


def bits():
    order = [1 << k for k in reversed(range(lax.axis_size(AXIS).bit_length() - 1))]
    return order[:-3] + order[-2:-1] + order[-3:-2] + order[-1:]


def after(value, *others):
    return lax.optimization_barrier((value, others))[0]


def gather_half(block, steps, *others):
    for bit in steps:
        block = jnp.concatenate([block, after(crossed(block, bit), *others)], axis=0)
    return block


def half_order():
    order = [0]
    for bit in bits()[:-1]:
        order += [place ^ bit for place in order]
    return order


def dot(a, b):
    return jnp.dot(a, b, preferred_element_type=F32)


def dot_nt(a, b):
    return lax.dot_general(a, b, (((1,), (1,)), ((), ())), preferred_element_type=F32)


def dot_tn(a, b):
    return lax.dot_general(a, b, (((0,), (0,)), ((), ())), preferred_element_type=F32)


def split(x):
    high = x.astype(BF16)
    return high, (x - high.astype(F32)).astype(BF16)


def split_dot(a, b, contract=dot):
    high, low = split(b)
    if isinstance(a, tuple):
        return contract(a[0], high) + contract(a[0], low) + contract(a[1], high)
    return contract(a, high) + contract(a, low)


def column_sum(x):
    return jnp.sum(x, axis=0, keepdims=True)


def rows_of(ref, index, count):
    return ref[index * count : (index + 1) * count]


def column_of(row):
    return jnp.broadcast_to(row, (8, row.shape[1])).T[:, :1]


def parts_of(row):
    high = row.astype(BF16).astype(F32)
    middle = (row - high).astype(BF16).astype(F32)
    return high, middle, row - high - middle


class Halo:
    def __init__(self, nf, ncf, nco, columns):
        self.nf, self.ncf, self.columns = nf, ncf, columns
        self.folds = nf // columns
        self.at_inverse = nf + ncf * self.folds
        self.at_weight = self.at_inverse + ncf * (nco // columns)
        self.weight_count = -(-3 * self.folds // 16) * 16
        self.height = self.at_weight + self.weight_count

    def unfolded(self, message, start, stop):
        return jnp.concatenate([message[k : k + self.ncf] for k in range(start, stop, self.ncf)], axis=1)

    def fold(self, message, block, start):
        ncf, columns = self.ncf, self.columns
        for k in range(block.shape[1] // columns):
            message[start + k * ncf : start + (k + 1) * ncf] = block[:, k * columns : (k + 1) * columns]

    def rows(self, message):
        return self.unfolded(message, self.nf, self.at_inverse)

    def inverse(self, message):
        return self.unfolded(message, self.at_inverse, self.at_weight)

    def weight(self, message):
        got = message[self.at_weight : self.height].astype(F32)
        f = self.folds
        row = [sum(got[k * f + i : k * f + i + 1] for k in range(3)) for i in range(f)]
        return jnp.concatenate([column_of(piece) for piece in row], axis=0)


def all_rows(halo, message, rows):
    ncf = halo.ncf
    return [halo.rows(message)] + [rows_of(rows, j, ncf) for j in range(rows.shape[0] // ncf)]


def is_odd():
    return lax.rem(lax.axis_index(AXIS), 2) == 1


def send(first, second, near, far):
    first, second, odd = first.astype(BF16), second.astype(BF16), is_odd()
    near[...] = jnp.where(odd, first, second)
    far[...] = jnp.where(odd, second, first)


def received(near, far):
    near, far, odd = near[...].astype(F32), far[...].astype(F32), is_odd()
    return jnp.where(odd, far, near), jnp.where(odd, near, far)


def all_weights(halo, message, weight):
    return [halo.weight(message)] + [column_of(weight[j : j + 1]) for j in range(weight.shape[0])]


def stage(kernel, shapes, *operands, scratch=(), fetched=0):
    out = [jax.ShapeDtypeStruct(shape, dtype) for shape, dtype in shapes]
    params = pltpu.CompilerParams(vmem_limit_bytes=VMEM_BYTES)
    spaces = [pltpu.HBM] * fetched + [pltpu.VMEM] * (len(operands) - fetched)
    call = pl.pallas_call(
        kernel,
        out_shape=out,
        in_specs=[pl.BlockSpec(memory_space=space) for space in spaces],
        scratch_shapes=list(scratch),
        compiler_params=params,
        name=kernel.func.__name__,
    )
    return call(*operands)


def prepare(
    halo, load, rows, weight, inverse, load_here, rows_here, weight_here, inverse_here, coarse_rounded, coarse, done
):
    ncf, nf = halo.ncf, halo.nf
    subs = load.shape[0] // nf
    copies = [pltpu.make_async_copy(rows, rows_here, done.at[subs])]
    copies += [
        pltpu.make_async_copy(rows_of(load.at, j, nf), rows_of(load_here.at, j, nf), done.at[j]) for j in range(subs)
    ]
    copies.append(pltpu.make_async_copy(weight, weight_here, done.at[subs + 1]))
    copies.append(pltpu.make_async_copy(inverse, inverse_here, done.at[subs + 2]))
    for copy in copies:
        copy.start()
    copies[0].wait()
    for j in range(subs):
        copies[1 + j].wait()
        coarse[j * ncf : (j + 1) * ncf] = dot(rows_of(rows_here, j, ncf), rows_of(load_here, j, nf).astype(BF16))
    coarse_rounded[...] = coarse[...].astype(BF16)
    copies[-2].wait()
    copies[-1].wait()


def halo_message(halo, load, weight, rows, inverse, message, pieces):
    ncf, nf, columns, folds = halo.ncf, halo.nf, halo.columns, halo.folds
    last = weight[weight.shape[0] - 1 :]
    message[:nf] = ((1.0 - column_of(last)) * load[load.shape[0] - nf :]).astype(BF16)
    halo.fold(message, rows[rows.shape[0] - ncf :], nf)
    halo.fold(message, inverse[inverse.shape[0] - ncf :], halo.at_inverse)
    pieces[...] = jnp.zeros_like(pieces)
    for k, values in enumerate(parts_of(last)):
        for i in range(folds):
            pieces[k * folds + i : k * folds + i + 1] = values[:, i * columns : (i + 1) * columns]
    message[halo.at_weight :] = pieces[...].astype(BF16)


def fetch(halo, neumann, schur, neumann_here, schur_here, done):
    pairs = ((neumann, neumann_here), (schur, schur_here))
    copies = [pltpu.make_async_copy(source, here, done.at[k]) for k, (source, here) in enumerate(pairs)]
    for copy in copies:
        copy.start()
    for copy in copies:
        copy.wait()


def neumann_products(left, right, weights, neumann, part, near, far):
    subs, nf = len(left), left[0].shape[0]
    previous = None
    for j in range(subs):
        product = dot(rows_of(neumann, j, 2 * nf), jnp.concatenate([left[j], right[j]], axis=0))
        first, second = product[:nf], product[nf:]
        if j == 0:
            part[:nf] = outer = first
        else:
            part[j * nf : (j + 1) * nf] = weights[j] * previous + (1.0 - weights[j]) * first
        previous = second
    part[subs * nf :] = previous
    send(outer, previous, near, far)


def neumann_load(halo, load, weight, message, neumann, part, near, far):
    subs, nf = weight.shape
    weights = [None] + [column_of(weight[j : j + 1]) for j in range(subs)]
    left = [message[:nf]]
    left += [((1.0 - weights[j]) * rows_of(load, j - 1, nf)).astype(BF16) for j in range(1, subs)]
    right = [(weights[j + 1] * rows_of(load, j, nf)).astype(BF16) for j in range(subs)]
    neumann_products(left, right, weights, neumann, part, near, far)


def neumann_image(halo, part_in, near_in, far_in, weight, message, neumann, image, part, near, far):
    subs, nf = weight.shape
    weights = all_weights(halo, message, weight)
    faces = [rows_of(part_in, e, nf) for e in range(subs + 1)]
    from_next, from_previous = received(near_in, far_in)
    faces[0] = faces[0] + from_previous
    faces[subs] = faces[subs] + from_next
    for e in range(1, subs + 1):
        image[(e - 1) * nf : e * nf] = faces[e]
    left = [((1.0 - weights[j]) * faces[j]).astype(BF16) for j in range(subs)]
    right = [(weights[j + 1] * faces[j + 1]).astype(BF16) for j in range(subs)]
    neumann_products(left, right, weights, neumann, part, near, far)


def static_basis(halo, schur, message, rows, basis_high, basis_low, turned_high, turned_low, gram):
    ncf, nf = halo.ncf, halo.nf
    blocks = all_rows(halo, message, rows)
    gram[...] = jnp.zeros_like(gram)
    for j in range(len(blocks) - 1):
        matrix, pair = rows_of(schur, j, 2 * nf), blocks[j : j + 2]
        basis = jnp.concatenate([dot_nt(matrix[:, k * nf : (k + 1) * nf], pair[k]) for k in range(2)], axis=1)
        long, wide = slice(2 * j * nf, 2 * (j + 1) * nf), slice(2 * j * ncf, 2 * (j + 1) * ncf)
        basis_high[long], basis_low[long] = split(basis)
        turned = split(basis.T)
        turned_high[wide], turned_low[wide] = turned
        for k in range(2):
            half = slice(k * nf, (k + 1) * nf)
            gram[wide, k * ncf : (k + 1) * ncf] = dot_nt(turned[0][:, half], pair[k]) + dot_nt(turned[1][:, half], pair[k])


def complete_local(halo, part, near, far, weight, message, local):
    subs, nf = weight.shape
    weights = all_weights(halo, message, weight)
    from_next, from_previous = received(near, far)
    local[:nf] = (1.0 - weights[0]) * part[:nf] + weights[0] * from_previous
    for e in range(1, subs):
        local[e * nf : (e + 1) * nf] = rows_of(part, e, nf)
    local[subs * nf :] = weights[subs] * part[subs * nf :] + (1.0 - weights[subs]) * from_next


def project(halo, local, turned_high, turned_low, base):
    ncf, nf = halo.ncf, halo.nf
    for j in range(base.shape[0] // (2 * ncf)):
        here = slice(2 * j * ncf, 2 * (j + 1) * ncf)
        base[here] = split_dot((turned_high[here], turned_low[here]), local[j * nf : (j + 2) * nf])


def schur_faces(halo, local, schur):
    nf, columns = halo.nf, halo.columns
    faces, energy = [], 0.0
    for j in range(schur.shape[0] // (2 * nf)):
        vector = local[j * nf : (j + 2) * nf]
        both = dot(rows_of(schur, j, 2 * nf), jnp.concatenate(split(vector), axis=1))
        result = both[:, :columns] + both[:, columns:]
        energy = energy + column_sum(vector * result)
        faces[j:] = [result[:nf] if j == 0 else faces[j] + result[:nf], result[nf:]]
    return faces, energy


def schur_load(halo, local, schur, basis_high, basis_low, solution, sums_in, part, near, far, sums):
    ncf, nf = halo.ncf, halo.nf
    faces, energy = schur_faces(halo, local, schur)
    x = [rows_of(solution, e, ncf) for e in range(len(faces))]
    faces = add_basis(nf, x, basis_high, basis_low, faces)
    for e, face in enumerate(faces):
        part[e * nf : (e + 1) * nf] = face
    send(faces[0], faces[-1], near, far)
    sums[0:1] = sums_in[0:1]
    sums[1:2] = sums_in[1:2] + energy


def schur_image(
    halo, image, part, near, far, weight, message, schur, turned_high, turned_low, local, product, quadratic, base
):
    nf = halo.nf
    complete_local(halo, part, near, far, weight, message, local)
    project(halo, local, turned_high, turned_low, base)
    faces, energy = schur_faces(halo, local, schur)
    for e, face in enumerate(faces):
        product[e * nf : (e + 1) * nf] = face
    quadratic[0:1] = energy
    quadratic[1:2] = column_sum(image[...] * local[nf:])


def placed(half, crossed_half):
    me = lax.axis_index(AXIS)
    order = half_order()
    count = half.shape[0] // len(order)
    for flip, blocks in ((0, half), (1, crossed_half)):
        for k, place in enumerate(order):
            yield me ^ (place ^ flip), blocks, k * count, (k + 1) * count


def coarse_shares(ncf, results):
    shares = [results[0][:ncf]]
    for before, after in zip(results[:-1], results[1:]):
        shares.append(before[ncf:] + after[:ncf])
    return shares + [results[-1][ncf:]]


def coarse_products(ncf, x, base, gram):
    results, energy = [], 0.0
    for j in range(len(x) - 1):
        here = slice(2 * j * ncf, 2 * (j + 1) * ncf)
        pair = jnp.concatenate([x[j], x[j + 1]], axis=0)
        change = split_dot(split(gram[here, : 2 * ncf]), pair)
        energy = energy + column_sum(pair * (2.0 * base[here] + change))
        results.append(base[here] + change)
    return results, energy


def add_basis(nf, x, basis_high, basis_low, faces):
    faces = list(faces)
    for j in range(len(x) - 1):
        here = slice(2 * j * nf, 2 * (j + 1) * nf)
        pair = jnp.concatenate([x[j], x[j + 1]], axis=0)
        change = split_dot((basis_high[here], basis_low[here]), pair)
        faces[j] = faces[j] + change[:nf]
        faces[j + 1] = faces[j + 1] + change[nf:]
    return faces


def coarse_load(
    halo, load, part, near, far, weight, message, turned_high, turned_low, half, crossed_half, inverse, coarse, gram,
    local, shares_rounded, shares, solution, sums, base, gathered,
):
    ncf, nf = halo.ncf, halo.nf
    subs = weight.shape[0]
    complete_local(halo, part, near, far, weight, message, local)
    project(halo, local, turned_high, turned_low, base)
    for place, blocks, start, stop in placed(half, crossed_half):
        gathered[pl.ds(pl.multiple_of(place * subs * ncf, subs * ncf), subs * ncf)] = blocks[start:stop]
    everything = gathered[...]
    own = dot(inverse[...], everything)
    x = [dot(halo.inverse(message), everything)] + [own[j * ncf : (j + 1) * ncf] for j in range(subs)]
    results, energy = coarse_products(ncf, x, base, gram)
    for e, share in enumerate(coarse_shares(ncf, results)):
        shares[e * ncf : (e + 1) * ncf] = share
        solution[e * ncf : (e + 1) * ncf] = x[e]
    shares_rounded[...] = shares[...].astype(BF16)
    sums[0:1] = column_sum(load[...] * local[nf:]) + column_sum(coarse[...] * own)
    sums[1:2] = energy


def coarse_image(
    halo, half, crossed_half, inverse, message, shares, base, gram, quadratic, basis_high, basis_low, product, sums_in,
    sums, solution, part, back, gathered,
):
    ncf, nf = halo.ncf, halo.nf
    subs = inverse.shape[0] // ncf
    total = gathered.shape[0]
    for place, blocks, start, stop in placed(half, crossed_half):
        gathered[pl.ds(pl.multiple_of(place * subs * ncf, subs * ncf), subs * ncf)] = blocks[start + ncf : stop].astype(F32)
    for place, blocks, start, stop in placed(half, crossed_half):
        before = pl.multiple_of(lax.rem(place * subs * ncf + (total - ncf), total), ncf)
        gathered[pl.ds(before, ncf)] += blocks[start : start + ncf].astype(F32)
    everything = gathered[...]
    own = split_dot(inverse[...], everything)
    x = [split_dot(halo.inverse(message), everything)] + [own[j * ncf : (j + 1) * ncf] for j in range(subs)]
    _, energy = coarse_products(ncf, x, base, gram)
    sums[0:2] = sums_in[0:2]
    sums[2:3] = quadratic[1:2] + sum(column_sum(rows_of(shares, e, ncf) * x[e]) for e in range(subs + 1))
    sums[3:4] = quadratic[0:1] + energy
    solution[...] = own
    faces = add_basis(nf, x, basis_high, basis_low, [rows_of(product, e, nf) for e in range(subs + 1)])
    for e in range(1, subs + 1):
        part[(e - 1) * nf : e * nf] = faces[e]
    back[...] = faces[0].astype(BF16)


def complete(halo, z_local, z_coarse, y_local, y_coarse, rows, z, y):
    ncf, nf = halo.ncf, halo.nf
    for j in range(rows.shape[0] // ncf):
        here, beside = slice(j * nf, (j + 1) * nf), slice((j + 1) * nf, (j + 2) * nf)
        for local, coarse, whole in ((z_local, z_coarse[ncf:], z), (y_local, y_coarse[...], y)):
            whole[here] = local[beside] + split_dot(rows_of(rows, j, ncf), rows_of(coarse, j, ncf), dot_tn)


def combine(halo, sums, load, z, y, image, part, from_next, solution, residual):
    nf = halo.nf
    a, b, c, d = (sums[k : k + 1] for k in range(4))
    step = a / b
    grow = step * (c / b)
    next_step = (grow - 1.0) / ((d - c * (c / b)) * (step / b))
    s = step + next_step * grow
    t = step * next_step
    solution[...] = s * z[...] - t * y[...]
    last = load.shape[0] - nf
    residual[:last] = load[:last] - s * image[:last] + t * part[:last]
    residual[last:] = load[last:] - s * image[last:] + t * (part[last:] + from_next[...].astype(F32))


def shards(right_side, face_weight, schur, neumann, constraint, coarse_inverse):
    subs, nf = face_weight.shape
    ncf = constraint.shape[0] // subs
    nco = coarse_inverse.shape[1]
    columns = right_side.shape[1]
    halo = Halo(nf, ncf, nco, columns)
    bind = lambda kernel: functools.partial(kernel, halo)
    faces, own = ((subs + 1) * nf, columns), (subs * nf, columns)
    coarse_own, local_rows = (subs * ncf, columns), 2 * subs * ncf
    halves = [((nf, columns), BF16)] * 2
    products = [(faces, F32), (faces, F32), ((8, columns), F32), ((local_rows, columns), F32)]
    semaphores = lambda count: [pltpu.SemaphoreType.DMA((count,))]
    described = lambda array: (array.shape, array.dtype)
    outside = lambda array: pltpu.with_memory_space_constraint(array, pltpu.HBM)
    steps = bits()
    early, late = steps[:-2], steps[-2:-1]

    load, rows, weight, inverse, coarse_rounded, coarse = stage(
        bind(prepare),
        [described(right_side), described(constraint), described(face_weight), described(coarse_inverse)]
        + [(coarse_own, BF16), (coarse_own, F32)],
        *map(outside, (right_side, constraint, face_weight, coarse_inverse)), scratch=semaphores(subs + 3), fetched=4,
    )
    (message,) = stage(
        bind(halo_message), [((halo.height, columns), BF16)], load, weight, rows, inverse,
        scratch=[pltpu.VMEM((halo.weight_count, columns), F32)],
    )
    half = gather_half(coarse_rounded, early[:1])
    message = after(message, half)
    tied = after(tuple(map(outside, (neumann, schur))), message)
    neumann, schur = stage(
        bind(fetch), [described(array) for array in tied], *tied, scratch=semaphores(2), fetched=2
    )
    message = shifted(message, 1)
    half = gather_half(half, early[1:], neumann)
    part, near, far = stage(
        bind(neumann_load), [(faces, F32)] + halves, load, weight, message, neumann
    )
    far, near = far_block(far), crossed(near, 1)
    long, wide = ((2 * subs * nf, 2 * ncf), BF16), ((local_rows, 2 * nf), BF16)
    basis_high, basis_low, turned_high, turned_low, gram = stage(
        bind(static_basis), [long, long, wide, wide, ((local_rows, LANES), F32)], schur, after(message, part), rows
    )
    half = gather_half(half, late, gram)
    crossed_half = crossed(half, 1)
    share_rows, sum_rows = ((subs + 1) * ncf, columns), ((8, columns), F32)
    z_local, shares_rounded, shares, z_coarse, sums = stage(
        bind(coarse_load), [(faces, F32), (share_rows, BF16), (share_rows, F32), (share_rows, F32), sum_rows],
        load, part, near, far, weight, message, turned_high, turned_low, half, crossed_half, inverse, coarse, gram,
        scratch=[pltpu.VMEM((local_rows, columns), F32), pltpu.VMEM((nco, columns), BF16)],
    )
    part, near, far, sums = stage(
        bind(schur_load), [(faces, F32)] + halves + [sum_rows],
        z_local, schur, basis_high, basis_low, z_coarse, sums,
    )
    half = gather_half(shares_rounded, early[:1])
    near, far = after((near, far), half)
    far, near = far_block(far), crossed(near, 1)
    image, part, near, far = stage(
        bind(neumann_image), [(own, F32), (faces, F32)] + halves, part, near, far, weight, message, neumann
    )
    half = gather_half(half, early[1:], far)
    far, near = far_block(far), crossed(near, 1)
    half = gather_half(half, late, near, far)
    crossed_half = crossed(half, 1)
    part = after(part, half)
    y_local, product, quadratic, base = stage(
        bind(schur_image), products, image, part, near, far, weight, message, schur, turned_high, turned_low
    )
    sums, y_coarse, part, back = stage(
        bind(coarse_image), [((4, columns), F32), (coarse_own, F32), (own, F32), ((nf, columns), BF16)],
        half, crossed_half, inverse, message, shares, base, gram, quadratic, basis_high, basis_low, product, sums,
        scratch=[pltpu.VMEM((nco, columns), F32)],
    )
    z, y = stage(bind(complete), [(own, F32), (own, F32)], z_local, z_coarse, y_local, y_coarse, rows)
    for k, bit in enumerate(steps):
        sums = sums + after(crossed(sums, bit), y)
        if k == len(early) - 1:
            back = shifted(after(back, sums), -1)
    return stage(bind(combine), [(own, F32), (own, F32)], sums, load, z, y, image, part, back)


def solution(mesh):
    specs = P(("parts", AXIS), None)
    return jax.shard_map(shards, mesh=mesh, in_specs=(specs,) * 6, out_specs=(specs, specs), check_vma=False)
```

```python
import functools

import jax
import jax.numpy as jnp
from jax import lax
from jax.experimental import pallas as pl
from jax.experimental.pallas import tpu as pltpu
from jax.sharding import PartitionSpec as P

AXIS = "sub"
BF16 = jnp.bfloat16
F32 = jnp.float32
LANES = 128
VMEM_BYTES = 20 * 2**20


def shifted(block, distance):
    n = lax.axis_size(AXIS)
    return lax.ppermute(block, AXIS, [((i - distance) % n, i) for i in range(n)])


def crossed(block, bit):
    return lax.ppermute(block, AXIS, [(i, i ^ bit) for i in range(lax.axis_size(AXIS))])


def far_block(block):
    n = lax.axis_size(AXIS)
    return lax.ppermute(block, AXIS, [(i, (i + (1 if i % 2 else -1)) % n) for i in range(n)])


def bits():
    order = [1 << k for k in reversed(range(lax.axis_size(AXIS).bit_length() - 1))]
    return order[:-3] + order[-2:-1] + order[-3:-2] + order[-1:]


def after(value, *others):
    return lax.optimization_barrier((value, others))[0]


def gather_half(block, steps, *others):
    for bit in steps:
        block = jnp.concatenate([block, after(crossed(block, bit), *others)], axis=0)
    return block


def half_order():
    order = [0]
    for bit in bits()[:-1]:
        order += [place ^ bit for place in order]
    return order


def dot(a, b):
    return jnp.dot(a, b, preferred_element_type=F32)


def dot_nt(a, b):
    return lax.dot_general(a, b, (((1,), (1,)), ((), ())), preferred_element_type=F32)


def dot_tn(a, b):
    return lax.dot_general(a, b, (((0,), (0,)), ((), ())), preferred_element_type=F32)


def split(x):
    high = x.astype(BF16)
    return high, (x - high.astype(F32)).astype(BF16)


def split_dot(a, b, contract=dot):
    high, low = split(b)
    if isinstance(a, tuple):
        return contract(a[0], high) + contract(a[0], low) + contract(a[1], high)
    return contract(a, high) + contract(a, low)


def column_sum(x):
    return jnp.sum(x, axis=0, keepdims=True)


def rows_of(ref, index, count):
    return ref[index * count : (index + 1) * count]


def column_of(row):
    return jnp.broadcast_to(row, (8, row.shape[1])).T[:, :1]


def parts_of(row):
    high = row.astype(BF16).astype(F32)
    middle = (row - high).astype(BF16).astype(F32)
    return high, middle, row - high - middle


class Halo:
    def __init__(self, nf, ncf, nco, columns):
        self.nf, self.ncf, self.columns = nf, ncf, columns
        self.folds = nf // columns
        self.at_inverse = nf + ncf * self.folds
        self.at_weight = self.at_inverse + ncf * (nco // columns)
        self.weight_count = -(-3 * self.folds // 16) * 16
        self.height = self.at_weight + self.weight_count

    def unfolded(self, message, start, stop):
        return jnp.concatenate([message[k : k + self.ncf] for k in range(start, stop, self.ncf)], axis=1)

    def fold(self, message, block, start):
        ncf, columns = self.ncf, self.columns
        for k in range(block.shape[1] // columns):
            message[start + k * ncf : start + (k + 1) * ncf] = block[:, k * columns : (k + 1) * columns]

    def rows(self, message):
        return self.unfolded(message, self.nf, self.at_inverse)

    def inverse(self, message):
        return self.unfolded(message, self.at_inverse, self.at_weight)

    def weight(self, message):
        got = message[self.at_weight : self.height].astype(F32)
        f = self.folds
        row = [sum(got[k * f + i : k * f + i + 1] for k in range(3)) for i in range(f)]
        return jnp.concatenate([column_of(piece) for piece in row], axis=0)


def all_rows(halo, message, rows):
    ncf = halo.ncf
    return [halo.rows(message)] + [rows_of(rows, j, ncf) for j in range(rows.shape[0] // ncf)]


def is_odd():
    return lax.rem(lax.axis_index(AXIS), 2) == 1


def send(first, second, near, far):
    first, second, odd = first.astype(BF16), second.astype(BF16), is_odd()
    near[...] = jnp.where(odd, first, second)
    far[...] = jnp.where(odd, second, first)


def received(near, far):
    near, far, odd = near[...].astype(F32), far[...].astype(F32), is_odd()
    return jnp.where(odd, far, near), jnp.where(odd, near, far)


def all_weights(halo, message, weight):
    return [halo.weight(message)] + [column_of(weight[j : j + 1]) for j in range(weight.shape[0])]


def stage(kernel, shapes, *operands, scratch=(), fetched=0):
    out = [jax.ShapeDtypeStruct(shape, dtype) for shape, dtype in shapes]
    params = pltpu.CompilerParams(vmem_limit_bytes=VMEM_BYTES)
    spaces = [pltpu.HBM] * fetched + [pltpu.VMEM] * (len(operands) - fetched)
    call = pl.pallas_call(
        kernel,
        out_shape=out,
        in_specs=[pl.BlockSpec(memory_space=space) for space in spaces],
        scratch_shapes=list(scratch),
        compiler_params=params,
        name=kernel.func.__name__,
    )
    return call(*operands)


def prepare(
    halo, load, rows, weight, inverse, load_here, rows_here, weight_here, inverse_here, coarse_rounded, coarse, done
):
    ncf, nf = halo.ncf, halo.nf
    subs = load.shape[0] // nf
    copies = [pltpu.make_async_copy(rows, rows_here, done.at[subs])]
    copies += [
        pltpu.make_async_copy(rows_of(load.at, j, nf), rows_of(load_here.at, j, nf), done.at[j]) for j in range(subs)
    ]
    copies.append(pltpu.make_async_copy(weight, weight_here, done.at[subs + 1]))
    copies.append(pltpu.make_async_copy(inverse, inverse_here, done.at[subs + 2]))
    for copy in copies:
        copy.start()
    copies[0].wait()
    for j in range(subs):
        copies[1 + j].wait()
        coarse[j * ncf : (j + 1) * ncf] = dot(rows_of(rows_here, j, ncf), rows_of(load_here, j, nf).astype(BF16))
    coarse_rounded[...] = coarse[...].astype(BF16)
    copies[-2].wait()
    copies[-1].wait()


def halo_message(halo, load, weight, rows, inverse, message, pieces):
    ncf, nf, columns, folds = halo.ncf, halo.nf, halo.columns, halo.folds
    last = weight[weight.shape[0] - 1 :]
    message[:nf] = ((1.0 - column_of(last)) * load[load.shape[0] - nf :]).astype(BF16)
    halo.fold(message, rows[rows.shape[0] - ncf :], nf)
    halo.fold(message, inverse[inverse.shape[0] - ncf :], halo.at_inverse)
    pieces[...] = jnp.zeros_like(pieces)
    for k, values in enumerate(parts_of(last)):
        for i in range(folds):
            pieces[k * folds + i : k * folds + i + 1] = values[:, i * columns : (i + 1) * columns]
    message[halo.at_weight :] = pieces[...].astype(BF16)


def fetch(halo, neumann, schur, neumann_here, schur_here, done):
    pairs = ((neumann, neumann_here), (schur, schur_here))
    copies = [pltpu.make_async_copy(source, here, done.at[k]) for k, (source, here) in enumerate(pairs)]
    for copy in copies:
        copy.start()
    for copy in copies:
        copy.wait()


def neumann_products(left, right, weights, neumann, part, near, far):
    subs, nf = len(left), left[0].shape[0]
    previous = None
    for j in range(subs):
        product = dot(rows_of(neumann, j, 2 * nf), jnp.concatenate([left[j], right[j]], axis=0))
        first, second = product[:nf], product[nf:]
        if j == 0:
            part[:nf] = outer = first
        else:
            part[j * nf : (j + 1) * nf] = weights[j] * previous + (1.0 - weights[j]) * first
        previous = second
    part[subs * nf :] = previous
    send(outer, previous, near, far)


def neumann_load(halo, load, weight, message, neumann, part, near, far):
    subs, nf = weight.shape
    weights = [None] + [column_of(weight[j : j + 1]) for j in range(subs)]
    left = [message[:nf]]
    left += [((1.0 - weights[j]) * rows_of(load, j - 1, nf)).astype(BF16) for j in range(1, subs)]
    right = [(weights[j + 1] * rows_of(load, j, nf)).astype(BF16) for j in range(subs)]
    neumann_products(left, right, weights, neumann, part, near, far)


def neumann_image(halo, part_in, near_in, far_in, weight, message, neumann, image, part, near, far):
    subs, nf = weight.shape
    weights = all_weights(halo, message, weight)
    faces = [rows_of(part_in, e, nf) for e in range(subs + 1)]
    from_next, from_previous = received(near_in, far_in)
    faces[0] = faces[0] + from_previous
    faces[subs] = faces[subs] + from_next
    for e in range(1, subs + 1):
        image[(e - 1) * nf : e * nf] = faces[e]
    left = [((1.0 - weights[j]) * faces[j]).astype(BF16) for j in range(subs)]
    right = [(weights[j + 1] * faces[j + 1]).astype(BF16) for j in range(subs)]
    neumann_products(left, right, weights, neumann, part, near, far)


def static_basis(halo, schur, message, rows, basis_high, basis_low, turned_high, turned_low, gram):
    ncf, nf = halo.ncf, halo.nf
    blocks = all_rows(halo, message, rows)
    gram[...] = jnp.zeros_like(gram)
    for j in range(len(blocks) - 1):
        matrix, pair = rows_of(schur, j, 2 * nf), blocks[j : j + 2]
        basis = jnp.concatenate([dot_nt(matrix[:, k * nf : (k + 1) * nf], pair[k]) for k in range(2)], axis=1)
        long, wide = slice(2 * j * nf, 2 * (j + 1) * nf), slice(2 * j * ncf, 2 * (j + 1) * ncf)
        basis_high[long], basis_low[long] = split(basis)
        turned = split(basis.T)
        turned_high[wide], turned_low[wide] = turned
        for k in range(2):
            half = slice(k * nf, (k + 1) * nf)
            gram[wide, k * ncf : (k + 1) * ncf] = dot_nt(turned[0][:, half], pair[k]) + dot_nt(turned[1][:, half], pair[k])


def complete_local(halo, part, near, far, weight, message, local):
    subs, nf = weight.shape
    weights = all_weights(halo, message, weight)
    from_next, from_previous = received(near, far)
    local[:nf] = (1.0 - weights[0]) * part[:nf] + weights[0] * from_previous
    for e in range(1, subs):
        local[e * nf : (e + 1) * nf] = rows_of(part, e, nf)
    local[subs * nf :] = weights[subs] * part[subs * nf :] + (1.0 - weights[subs]) * from_next


def project(halo, local, turned_high, turned_low, base):
    ncf, nf = halo.ncf, halo.nf
    for j in range(base.shape[0] // (2 * ncf)):
        here = slice(2 * j * ncf, 2 * (j + 1) * ncf)
        base[here] = split_dot((turned_high[here], turned_low[here]), local[j * nf : (j + 2) * nf])


def schur_faces(halo, local, schur):
    nf, columns = halo.nf, halo.columns
    faces, energy = [], 0.0
    for j in range(schur.shape[0] // (2 * nf)):
        vector = local[j * nf : (j + 2) * nf]
        both = dot(rows_of(schur, j, 2 * nf), jnp.concatenate(split(vector), axis=1))
        result = both[:, :columns] + both[:, columns:]
        energy = energy + column_sum(vector * result)
        faces[j:] = [result[:nf] if j == 0 else faces[j] + result[:nf], result[nf:]]
    return faces, energy


def schur_load(halo, local, schur, basis_high, basis_low, solution, sums_in, part, near, far, sums):
    ncf, nf = halo.ncf, halo.nf
    faces, energy = schur_faces(halo, local, schur)
    x = [rows_of(solution, e, ncf) for e in range(len(faces))]
    faces = add_basis(nf, x, basis_high, basis_low, faces)
    for e, face in enumerate(faces):
        part[e * nf : (e + 1) * nf] = face
    send(faces[0], faces[-1], near, far)
    sums[0:1] = sums_in[0:1]
    sums[1:2] = sums_in[1:2] + energy


def schur_image(
    halo, image, part, near, far, weight, message, schur, turned_high, turned_low, local, product, quadratic, base
):
    nf = halo.nf
    complete_local(halo, part, near, far, weight, message, local)
    project(halo, local, turned_high, turned_low, base)
    faces, energy = schur_faces(halo, local, schur)
    for e, face in enumerate(faces):
        product[e * nf : (e + 1) * nf] = face
    quadratic[0:1] = energy
    quadratic[1:2] = column_sum(image[...] * local[nf:])


def placed(half, crossed_half):
    me = lax.axis_index(AXIS)
    order = half_order()
    count = half.shape[0] // len(order)
    for flip, blocks in ((0, half), (1, crossed_half)):
        for k, place in enumerate(order):
            yield me ^ (place ^ flip), blocks, k * count, (k + 1) * count


def coarse_shares(ncf, results):
    shares = [results[0][:ncf]]
    for before, after in zip(results[:-1], results[1:]):
        shares.append(before[ncf:] + after[:ncf])
    return shares + [results[-1][ncf:]]


def coarse_products(ncf, x, base, gram):
    results, energy = [], 0.0
    for j in range(len(x) - 1):
        here = slice(2 * j * ncf, 2 * (j + 1) * ncf)
        pair = jnp.concatenate([x[j], x[j + 1]], axis=0)
        change = split_dot(split(gram[here, : 2 * ncf]), pair)
        energy = energy + column_sum(pair * (2.0 * base[here] + change))
        results.append(base[here] + change)
    return results, energy


def add_basis(nf, x, basis_high, basis_low, faces):
    faces = list(faces)
    for j in range(len(x) - 1):
        here = slice(2 * j * nf, 2 * (j + 1) * nf)
        pair = jnp.concatenate([x[j], x[j + 1]], axis=0)
        change = split_dot((basis_high[here], basis_low[here]), pair)
        faces[j] = faces[j] + change[:nf]
        faces[j + 1] = faces[j + 1] + change[nf:]
    return faces


def coarse_load(
    halo, load, part, near, far, weight, message, turned_high, turned_low, half, crossed_half, inverse, coarse, gram,
    local, shares_rounded, shares, solution, sums, base, gathered,
):
    ncf, nf = halo.ncf, halo.nf
    subs = weight.shape[0]
    complete_local(halo, part, near, far, weight, message, local)
    project(halo, local, turned_high, turned_low, base)
    for place, blocks, start, stop in placed(half, crossed_half):
        gathered[pl.ds(pl.multiple_of(place * subs * ncf, subs * ncf), subs * ncf)] = blocks[start:stop]
    everything = gathered[...]
    own = dot(inverse[...], everything)
    x = [dot(halo.inverse(message), everything)] + [own[j * ncf : (j + 1) * ncf] for j in range(subs)]
    results, energy = coarse_products(ncf, x, base, gram)
    for e, share in enumerate(coarse_shares(ncf, results)):
        shares[e * ncf : (e + 1) * ncf] = share
        solution[e * ncf : (e + 1) * ncf] = x[e]
    shares_rounded[...] = shares[...].astype(BF16)
    sums[0:1] = column_sum(load[...] * local[nf:]) + column_sum(coarse[...] * own)
    sums[1:2] = energy


def coarse_image(
    halo, half, crossed_half, inverse, message, shares, base, gram, quadratic, basis_high, basis_low, product, sums_in,
    sums, solution, part, back, gathered,
):
    ncf, nf = halo.ncf, halo.nf
    subs = inverse.shape[0] // ncf
    total = gathered.shape[0]
    for place, blocks, start, stop in placed(half, crossed_half):
        gathered[pl.ds(pl.multiple_of(place * subs * ncf, subs * ncf), subs * ncf)] = blocks[start + ncf : stop].astype(F32)
    for place, blocks, start, stop in placed(half, crossed_half):
        before = pl.multiple_of(lax.rem(place * subs * ncf + (total - ncf), total), ncf)
        gathered[pl.ds(before, ncf)] += blocks[start : start + ncf].astype(F32)
    everything = gathered[...]
    own = split_dot(inverse[...], everything)
    x = [split_dot(halo.inverse(message), everything)] + [own[j * ncf : (j + 1) * ncf] for j in range(subs)]
    _, energy = coarse_products(ncf, x, base, gram)
    sums[0:2] = sums_in[0:2]
    sums[2:3] = quadratic[1:2] + sum(column_sum(rows_of(shares, e, ncf) * x[e]) for e in range(subs + 1))
    sums[3:4] = quadratic[0:1] + energy
    solution[...] = own
    faces = add_basis(nf, x, basis_high, basis_low, [rows_of(product, e, nf) for e in range(subs + 1)])
    for e in range(1, subs + 1):
        part[(e - 1) * nf : e * nf] = faces[e]
    back[...] = faces[0].astype(BF16)


def complete(halo, z_local, z_coarse, y_local, y_coarse, rows, z, y):
    ncf, nf = halo.ncf, halo.nf
    for j in range(rows.shape[0] // ncf):
        here, beside = slice(j * nf, (j + 1) * nf), slice((j + 1) * nf, (j + 2) * nf)
        for local, coarse, whole in ((z_local, z_coarse[ncf:], z), (y_local, y_coarse[...], y)):
            whole[here] = local[beside] + split_dot(rows_of(rows, j, ncf), rows_of(coarse, j, ncf), dot_tn)


def combine(halo, sums, load, z, y, image, part, from_next, solution, residual):
    nf = halo.nf
    a, b, c, d = (sums[k : k + 1] for k in range(4))
    step = a / b
    grow = step * (c / b)
    next_step = (grow - 1.0) / ((d - c * (c / b)) * (step / b))
    s = step + next_step * grow
    t = step * next_step
    solution[...] = s * z[...] - t * y[...]
    last = load.shape[0] - nf
    residual[:last] = load[:last] - s * image[:last] + t * part[:last]
    residual[last:] = load[last:] - s * image[last:] + t * (part[last:] + from_next[...].astype(F32))


def shards(right_side, face_weight, schur, neumann, constraint, coarse_inverse):
    subs, nf = face_weight.shape
    ncf = constraint.shape[0] // subs
    nco = coarse_inverse.shape[1]
    columns = right_side.shape[1]
    halo = Halo(nf, ncf, nco, columns)
    bind = lambda kernel: functools.partial(kernel, halo)
    faces, own = ((subs + 1) * nf, columns), (subs * nf, columns)
    coarse_own, local_rows = (subs * ncf, columns), 2 * subs * ncf
    halves = [((nf, columns), BF16)] * 2
    products = [(faces, F32), (faces, F32), ((8, columns), F32), ((local_rows, columns), F32)]
    semaphores = lambda count: [pltpu.SemaphoreType.DMA((count,))]
    described = lambda array: (array.shape, array.dtype)
    outside = lambda array: pltpu.with_memory_space_constraint(array, pltpu.HBM)
    steps = bits()
    early, late = steps[:-2], steps[-2:-1]

    load, rows, weight, inverse, coarse_rounded, coarse = stage(
        bind(prepare),
        [described(right_side), described(constraint), described(face_weight), described(coarse_inverse)]
        + [(coarse_own, BF16), (coarse_own, F32)],
        *map(outside, (right_side, constraint, face_weight, coarse_inverse)), scratch=semaphores(subs + 3), fetched=4,
    )
    (message,) = stage(
        bind(halo_message), [((halo.height, columns), BF16)], load, weight, rows, inverse,
        scratch=[pltpu.VMEM((halo.weight_count, columns), F32)],
    )
    half = gather_half(coarse_rounded, early[:1])
    message = after(message, half)
    tied = after(tuple(map(outside, (neumann, schur))), message)
    neumann, schur = stage(
        bind(fetch), [described(array) for array in tied], *tied, scratch=semaphores(2), fetched=2
    )
    message = shifted(message, 1)
    half = gather_half(half, early[1:], neumann)
    part, near, far = stage(
        bind(neumann_load), [(faces, F32)] + halves, load, weight, message, neumann
    )
    far, near = far_block(far), crossed(near, 1)
    long, wide = ((2 * subs * nf, 2 * ncf), BF16), ((local_rows, 2 * nf), BF16)
    basis_high, basis_low, turned_high, turned_low, gram = stage(
        bind(static_basis), [long, long, wide, wide, ((local_rows, LANES), F32)], schur, after(message, part), rows
    )
    half = gather_half(half, late, gram)
    crossed_half = crossed(half, 1)
    share_rows, sum_rows = ((subs + 1) * ncf, columns), ((8, columns), F32)
    z_local, shares_rounded, shares, z_coarse, sums = stage(
        bind(coarse_load), [(faces, F32), (share_rows, BF16), (share_rows, F32), (share_rows, F32), sum_rows],
        load, part, near, far, weight, message, turned_high, turned_low, half, crossed_half, inverse, coarse, gram,
        scratch=[pltpu.VMEM((local_rows, columns), F32), pltpu.VMEM((nco, columns), BF16)],
    )
    part, near, far, sums = stage(
        bind(schur_load), [(faces, F32)] + halves + [sum_rows],
        z_local, schur, basis_high, basis_low, z_coarse, sums,
    )
    half = gather_half(shares_rounded, early[:1], far)
    near, far = after((near, far), half)
    far, near = far_block(far), crossed(near, 1)
    half = gather_half(half, early[1:])
    part = after(part, half)
    image, part, near, far = stage(
        bind(neumann_image), [(own, F32), (faces, F32)] + halves, part, near, far, weight, message, neumann
    )
    far, near = far_block(far), crossed(near, 1)
    half = gather_half(half, late, near)
    crossed_half = crossed(half, 1)
    part = after(part, half)
    y_local, product, quadratic, base = stage(
        bind(schur_image), products, image, part, near, far, weight, message, schur, turned_high, turned_low
    )
    sums, y_coarse, part, back = stage(
        bind(coarse_image), [((4, columns), F32), (coarse_own, F32), (own, F32), ((nf, columns), BF16)],
        half, crossed_half, inverse, message, shares, base, gram, quadratic, basis_high, basis_low, product, sums,
        scratch=[pltpu.VMEM((nco, columns), F32)],
    )
    z, y = stage(bind(complete), [(own, F32), (own, F32)], z_local, z_coarse, y_local, y_coarse, rows)
    for k, bit in enumerate(steps):
        sums = sums + after(crossed(sums, bit), y)
        if k == len(steps) - 2:
            back = shifted(after(back, sums), -1)
    return stage(bind(combine), [(own, F32), (own, F32)], sums, load, z, y, image, part, back)


def solution(mesh):
    specs = P(("parts", AXIS), None)
    return jax.shard_map(shards, mesh=mesh, in_specs=(specs,) * 6, out_specs=(specs, specs), check_vma=False)
```

```python
import functools

import jax
import jax.numpy as jnp
from jax import lax
from jax.experimental import pallas as pl
from jax.experimental.pallas import tpu as pltpu
from jax.sharding import PartitionSpec as P

AXIS = "sub"
BF16 = jnp.bfloat16
F32 = jnp.float32
LANES = 128
VMEM_BYTES = 20 * 2**20


def shifted(block, distance):
    n = lax.axis_size(AXIS)
    return lax.ppermute(block, AXIS, [((i - distance) % n, i) for i in range(n)])


def crossed(block, bit):
    return lax.ppermute(block, AXIS, [(i, i ^ bit) for i in range(lax.axis_size(AXIS))])


def far_block(block):
    n = lax.axis_size(AXIS)
    return lax.ppermute(block, AXIS, [(i, (i + (1 if i % 2 else -1)) % n) for i in range(n)])


def bits():
    order = [1 << k for k in reversed(range(lax.axis_size(AXIS).bit_length() - 1))]
    return order[:-3] + order[-2:-1] + order[-3:-2] + order[-1:]


def after(value, *others):
    return lax.optimization_barrier((value, others))[0]


def gather_half(block, steps, *others):
    for bit in steps:
        block = jnp.concatenate([block, after(crossed(block, bit), *others)], axis=0)
    return block


def half_order():
    order = [0]
    for bit in bits()[:-1]:
        order += [place ^ bit for place in order]
    return order


def dot(a, b):
    return jnp.dot(a, b, preferred_element_type=F32)


def dot_nt(a, b):
    return lax.dot_general(a, b, (((1,), (1,)), ((), ())), preferred_element_type=F32)


def dot_tn(a, b):
    return lax.dot_general(a, b, (((0,), (0,)), ((), ())), preferred_element_type=F32)


def split(x):
    high = x.astype(BF16)
    return high, (x - high.astype(F32)).astype(BF16)


def split_dot(a, b, contract=dot):
    high, low = split(b)
    if isinstance(a, tuple):
        return contract(a[0], high) + contract(a[0], low) + contract(a[1], high)
    return contract(a, high) + contract(a, low)


def column_sum(x):
    return jnp.sum(x, axis=0, keepdims=True)


def rows_of(ref, index, count):
    return ref[index * count : (index + 1) * count]


def column_of(row):
    return jnp.broadcast_to(row, (8, row.shape[1])).T[:, :1]


def parts_of(row):
    high = row.astype(BF16).astype(F32)
    middle = (row - high).astype(BF16).astype(F32)
    return high, middle, row - high - middle


class Halo:
    def __init__(self, nf, ncf, nco, columns):
        self.nf, self.ncf, self.columns = nf, ncf, columns
        self.folds = nf // columns
        self.at_inverse = nf + ncf * self.folds
        self.at_weight = self.at_inverse + ncf * (nco // columns)
        self.weight_count = -(-3 * self.folds // 16) * 16
        self.height = self.at_weight + self.weight_count

    def unfolded(self, message, start, stop):
        return jnp.concatenate([message[k : k + self.ncf] for k in range(start, stop, self.ncf)], axis=1)

    def fold(self, message, block, start):
        ncf, columns = self.ncf, self.columns
        for k in range(block.shape[1] // columns):
            message[start + k * ncf : start + (k + 1) * ncf] = block[:, k * columns : (k + 1) * columns]

    def rows(self, message):
        return self.unfolded(message, self.nf, self.at_inverse)

    def inverse(self, message):
        return self.unfolded(message, self.at_inverse, self.at_weight)

    def weight(self, message):
        got = message[self.at_weight : self.height].astype(F32)
        f = self.folds
        row = [sum(got[k * f + i : k * f + i + 1] for k in range(3)) for i in range(f)]
        return jnp.concatenate([column_of(piece) for piece in row], axis=0)


def all_rows(halo, message, rows):
    ncf = halo.ncf
    return [halo.rows(message)] + [rows_of(rows, j, ncf) for j in range(rows.shape[0] // ncf)]


def is_odd():
    return lax.rem(lax.axis_index(AXIS), 2) == 1


def send(first, second, near, far):
    first, second, odd = first.astype(BF16), second.astype(BF16), is_odd()
    near[...] = jnp.where(odd, first, second)
    far[...] = jnp.where(odd, second, first)


def received(near, far):
    near, far, odd = near[...].astype(F32), far[...].astype(F32), is_odd()
    return jnp.where(odd, far, near), jnp.where(odd, near, far)


def all_weights(halo, message, weight):
    return [halo.weight(message)] + [column_of(weight[j : j + 1]) for j in range(weight.shape[0])]


def stage(kernel, shapes, *operands, scratch=(), fetched=0):
    out = [jax.ShapeDtypeStruct(shape, dtype) for shape, dtype in shapes]
    params = pltpu.CompilerParams(vmem_limit_bytes=VMEM_BYTES)
    spaces = [pltpu.HBM] * fetched + [pltpu.VMEM] * (len(operands) - fetched)
    call = pl.pallas_call(
        kernel,
        out_shape=out,
        in_specs=[pl.BlockSpec(memory_space=space) for space in spaces],
        scratch_shapes=list(scratch),
        compiler_params=params,
        name=kernel.func.__name__,
    )
    return call(*operands)


def prepare(
    halo, load, rows, weight, inverse, load_here, rows_here, weight_here, inverse_here, coarse_rounded, coarse, done
):
    ncf, nf = halo.ncf, halo.nf
    subs = load.shape[0] // nf
    copies = [pltpu.make_async_copy(rows, rows_here, done.at[subs])]
    copies += [
        pltpu.make_async_copy(rows_of(load.at, j, nf), rows_of(load_here.at, j, nf), done.at[j]) for j in range(subs)
    ]
    copies.append(pltpu.make_async_copy(weight, weight_here, done.at[subs + 1]))
    copies.append(pltpu.make_async_copy(inverse, inverse_here, done.at[subs + 2]))
    for copy in copies:
        copy.start()
    copies[0].wait()
    for j in range(subs):
        copies[1 + j].wait()
        coarse[j * ncf : (j + 1) * ncf] = dot(rows_of(rows_here, j, ncf), rows_of(load_here, j, nf).astype(BF16))
    coarse_rounded[...] = coarse[...].astype(BF16)
    copies[-2].wait()
    copies[-1].wait()


def halo_message(halo, load, weight, rows, inverse, message, pieces):
    ncf, nf, columns, folds = halo.ncf, halo.nf, halo.columns, halo.folds
    last = weight[weight.shape[0] - 1 :]
    message[:nf] = ((1.0 - column_of(last)) * load[load.shape[0] - nf :]).astype(BF16)
    halo.fold(message, rows[rows.shape[0] - ncf :], nf)
    halo.fold(message, inverse[inverse.shape[0] - ncf :], halo.at_inverse)
    pieces[...] = jnp.zeros_like(pieces)
    for k, values in enumerate(parts_of(last)):
        for i in range(folds):
            pieces[k * folds + i : k * folds + i + 1] = values[:, i * columns : (i + 1) * columns]
    message[halo.at_weight :] = pieces[...].astype(BF16)


def fetch(halo, neumann, schur, neumann_here, schur_here, done):
    pairs = ((neumann, neumann_here), (schur, schur_here))
    copies = [pltpu.make_async_copy(source, here, done.at[k]) for k, (source, here) in enumerate(pairs)]
    for copy in copies:
        copy.start()
    for copy in copies:
        copy.wait()


def neumann_products(left, right, weights, neumann, part, near, far):
    subs, nf = len(left), left[0].shape[0]
    previous = None
    for j in range(subs):
        product = dot(rows_of(neumann, j, 2 * nf), jnp.concatenate([left[j], right[j]], axis=0))
        first, second = product[:nf], product[nf:]
        if j == 0:
            part[:nf] = outer = first
        else:
            part[j * nf : (j + 1) * nf] = weights[j] * previous + (1.0 - weights[j]) * first
        previous = second
    part[subs * nf :] = previous
    send(outer, previous, near, far)


def neumann_load(halo, load, weight, message, neumann, part, near, far):
    subs, nf = weight.shape
    weights = [None] + [column_of(weight[j : j + 1]) for j in range(subs)]
    left = [message[:nf]]
    left += [((1.0 - weights[j]) * rows_of(load, j - 1, nf)).astype(BF16) for j in range(1, subs)]
    right = [(weights[j + 1] * rows_of(load, j, nf)).astype(BF16) for j in range(subs)]
    neumann_products(left, right, weights, neumann, part, near, far)


def neumann_image(halo, part_in, near_in, far_in, weight, message, neumann, image, part, near, far):
    subs, nf = weight.shape
    weights = all_weights(halo, message, weight)
    faces = [rows_of(part_in, e, nf) for e in range(subs + 1)]
    from_next, from_previous = received(near_in, far_in)
    faces[0] = faces[0] + from_previous
    faces[subs] = faces[subs] + from_next
    for e in range(1, subs + 1):
        image[(e - 1) * nf : e * nf] = faces[e]
    left = [((1.0 - weights[j]) * faces[j]).astype(BF16) for j in range(subs)]
    right = [(weights[j + 1] * faces[j + 1]).astype(BF16) for j in range(subs)]
    neumann_products(left, right, weights, neumann, part, near, far)


def static_basis(halo, schur, message, rows, basis_high, basis_low, turned_high, turned_low, gram):
    ncf, nf = halo.ncf, halo.nf
    blocks = all_rows(halo, message, rows)
    gram[...] = jnp.zeros_like(gram)
    for j in range(len(blocks) - 1):
        matrix, pair = rows_of(schur, j, 2 * nf), blocks[j : j + 2]
        basis = jnp.concatenate([dot_nt(matrix[:, k * nf : (k + 1) * nf], pair[k]) for k in range(2)], axis=1)
        long, wide = slice(2 * j * nf, 2 * (j + 1) * nf), slice(2 * j * ncf, 2 * (j + 1) * ncf)
        basis_high[long], basis_low[long] = split(basis)
        turned = split(basis.T)
        turned_high[wide], turned_low[wide] = turned
        for k in range(2):
            half = slice(k * nf, (k + 1) * nf)
            gram[wide, k * ncf : (k + 1) * ncf] = dot_nt(turned[0][:, half], pair[k]) + dot_nt(turned[1][:, half], pair[k])


def complete_local(halo, part, near, far, weight, message, local):
    subs, nf = weight.shape
    weights = all_weights(halo, message, weight)
    from_next, from_previous = received(near, far)
    local[:nf] = (1.0 - weights[0]) * part[:nf] + weights[0] * from_previous
    for e in range(1, subs):
        local[e * nf : (e + 1) * nf] = rows_of(part, e, nf)
    local[subs * nf :] = weights[subs] * part[subs * nf :] + (1.0 - weights[subs]) * from_next


def project(halo, local, turned_high, turned_low, base):
    ncf, nf = halo.ncf, halo.nf
    for j in range(base.shape[0] // (2 * ncf)):
        here = slice(2 * j * ncf, 2 * (j + 1) * ncf)
        base[here] = split_dot((turned_high[here], turned_low[here]), local[j * nf : (j + 2) * nf])


def schur_faces(halo, local, schur):
    nf, columns = halo.nf, halo.columns
    faces, energy = [], 0.0
    for j in range(schur.shape[0] // (2 * nf)):
        vector = local[j * nf : (j + 2) * nf]
        both = dot(rows_of(schur, j, 2 * nf), jnp.concatenate(split(vector), axis=1))
        result = both[:, :columns] + both[:, columns:]
        energy = energy + column_sum(vector * result)
        faces[j:] = [result[:nf] if j == 0 else faces[j] + result[:nf], result[nf:]]
    return faces, energy


def schur_load(halo, local, schur, basis_high, basis_low, solution, sums_in, part, near, far, sums):
    ncf, nf = halo.ncf, halo.nf
    faces, energy = schur_faces(halo, local, schur)
    x = [rows_of(solution, e, ncf) for e in range(len(faces))]
    faces = add_basis(nf, x, basis_high, basis_low, faces)
    for e, face in enumerate(faces):
        part[e * nf : (e + 1) * nf] = face
    send(faces[0], faces[-1], near, far)
    sums[0:1] = sums_in[0:1]
    sums[1:2] = sums_in[1:2] + energy


def schur_image(
    halo, image, part, near, far, weight, message, schur, turned_high, turned_low, local, product, quadratic, base
):
    nf = halo.nf
    complete_local(halo, part, near, far, weight, message, local)
    project(halo, local, turned_high, turned_low, base)
    faces, energy = schur_faces(halo, local, schur)
    for e, face in enumerate(faces):
        product[e * nf : (e + 1) * nf] = face
    quadratic[0:1] = energy
    quadratic[1:2] = column_sum(image[...] * local[nf:])


def placed(half, crossed_half):
    me = lax.axis_index(AXIS)
    order = half_order()
    count = half.shape[0] // len(order)
    for flip, blocks in ((0, half), (1, crossed_half)):
        for k, place in enumerate(order):
            yield me ^ (place ^ flip), blocks, k * count, (k + 1) * count


def coarse_shares(ncf, results):
    shares = [results[0][:ncf]]
    for before, after in zip(results[:-1], results[1:]):
        shares.append(before[ncf:] + after[:ncf])
    return shares + [results[-1][ncf:]]


def coarse_products(ncf, x, base, gram):
    results, energy = [], 0.0
    for j in range(len(x) - 1):
        here = slice(2 * j * ncf, 2 * (j + 1) * ncf)
        pair = jnp.concatenate([x[j], x[j + 1]], axis=0)
        change = split_dot(split(gram[here, : 2 * ncf]), pair)
        energy = energy + column_sum(pair * (2.0 * base[here] + change))
        results.append(base[here] + change)
    return results, energy


def add_basis(nf, x, basis_high, basis_low, faces):
    faces = list(faces)
    for j in range(len(x) - 1):
        here = slice(2 * j * nf, 2 * (j + 1) * nf)
        pair = jnp.concatenate([x[j], x[j + 1]], axis=0)
        change = split_dot((basis_high[here], basis_low[here]), pair)
        faces[j] = faces[j] + change[:nf]
        faces[j + 1] = faces[j + 1] + change[nf:]
    return faces


def coarse_load(
    halo, load, part, near, far, weight, message, turned_high, turned_low, half, crossed_half, inverse, coarse, gram,
    local, shares_rounded, shares, solution, sums, base, gathered,
):
    ncf, nf = halo.ncf, halo.nf
    subs = weight.shape[0]
    complete_local(halo, part, near, far, weight, message, local)
    project(halo, local, turned_high, turned_low, base)
    for place, blocks, start, stop in placed(half, crossed_half):
        gathered[pl.ds(pl.multiple_of(place * subs * ncf, subs * ncf), subs * ncf)] = blocks[start:stop]
    everything = gathered[...]
    own = dot(inverse[...], everything)
    x = [dot(halo.inverse(message), everything)] + [own[j * ncf : (j + 1) * ncf] for j in range(subs)]
    results, energy = coarse_products(ncf, x, base, gram)
    for e, share in enumerate(coarse_shares(ncf, results)):
        shares[e * ncf : (e + 1) * ncf] = share
        solution[e * ncf : (e + 1) * ncf] = x[e]
    shares_rounded[...] = shares[...].astype(BF16)
    sums[0:1] = column_sum(load[...] * local[nf:]) + column_sum(coarse[...] * own)
    sums[1:2] = energy


def coarse_image(
    halo, half, crossed_half, inverse, message, shares, base, gram, quadratic, basis_high, basis_low, product, sums_in,
    sums, solution, part, back, gathered,
):
    ncf, nf = halo.ncf, halo.nf
    subs = inverse.shape[0] // ncf
    total = gathered.shape[0]
    for place, blocks, start, stop in placed(half, crossed_half):
        gathered[pl.ds(pl.multiple_of(place * subs * ncf, subs * ncf), subs * ncf)] = blocks[start + ncf : stop].astype(F32)
    for place, blocks, start, stop in placed(half, crossed_half):
        before = pl.multiple_of(lax.rem(place * subs * ncf + (total - ncf), total), ncf)
        gathered[pl.ds(before, ncf)] += blocks[start : start + ncf].astype(F32)
    everything = gathered[...]
    own = split_dot(inverse[...], everything)
    x = [split_dot(halo.inverse(message), everything)] + [own[j * ncf : (j + 1) * ncf] for j in range(subs)]
    _, energy = coarse_products(ncf, x, base, gram)
    sums[0:2] = sums_in[0:2]
    sums[2:3] = quadratic[1:2] + sum(column_sum(rows_of(shares, e, ncf) * x[e]) for e in range(subs + 1))
    sums[3:4] = quadratic[0:1] + energy
    solution[...] = own
    faces = add_basis(nf, x, basis_high, basis_low, [rows_of(product, e, nf) for e in range(subs + 1)])
    for e in range(1, subs + 1):
        part[(e - 1) * nf : e * nf] = faces[e]
    back[...] = faces[0].astype(BF16)


def complete(halo, z_local, z_coarse, y_local, y_coarse, rows, z, y):
    ncf, nf = halo.ncf, halo.nf
    for j in range(rows.shape[0] // ncf):
        here, beside = slice(j * nf, (j + 1) * nf), slice((j + 1) * nf, (j + 2) * nf)
        for local, coarse, whole in ((z_local, z_coarse[ncf:], z), (y_local, y_coarse[...], y)):
            whole[here] = local[beside] + split_dot(rows_of(rows, j, ncf), rows_of(coarse, j, ncf), dot_tn)


def combine(halo, sums, load, z, y, image, part, from_next, solution, residual):
    nf = halo.nf
    a, b, c, d = (sums[k : k + 1] for k in range(4))
    step = a / b
    grow = step * (c / b)
    next_step = (grow - 1.0) / ((d - c * (c / b)) * (step / b))
    s = step + next_step * grow
    t = step * next_step
    solution[...] = s * z[...] - t * y[...]
    last = load.shape[0] - nf
    residual[:last] = load[:last] - s * image[:last] + t * part[:last]
    residual[last:] = load[last:] - s * image[last:] + t * (part[last:] + from_next[...].astype(F32))


def shards(right_side, face_weight, schur, neumann, constraint, coarse_inverse):
    subs, nf = face_weight.shape
    ncf = constraint.shape[0] // subs
    nco = coarse_inverse.shape[1]
    columns = right_side.shape[1]
    halo = Halo(nf, ncf, nco, columns)
    bind = lambda kernel: functools.partial(kernel, halo)
    faces, own = ((subs + 1) * nf, columns), (subs * nf, columns)
    coarse_own, local_rows = (subs * ncf, columns), 2 * subs * ncf
    halves = [((nf, columns), BF16)] * 2
    products = [(faces, F32), (faces, F32), ((8, columns), F32), ((local_rows, columns), F32)]
    semaphores = lambda count: [pltpu.SemaphoreType.DMA((count,))]
    described = lambda array: (array.shape, array.dtype)
    outside = lambda array: pltpu.with_memory_space_constraint(array, pltpu.HBM)
    steps = bits()
    early, late = steps[:-2], steps[-2:-1]

    load, rows, weight, inverse, coarse_rounded, coarse = stage(
        bind(prepare),
        [described(right_side), described(constraint), described(face_weight), described(coarse_inverse)]
        + [(coarse_own, BF16), (coarse_own, F32)],
        *map(outside, (right_side, constraint, face_weight, coarse_inverse)), scratch=semaphores(subs + 3), fetched=4,
    )
    (message,) = stage(
        bind(halo_message), [((halo.height, columns), BF16)], load, weight, rows, inverse,
        scratch=[pltpu.VMEM((halo.weight_count, columns), F32)],
    )
    half = gather_half(coarse_rounded, early[:1])
    message = after(message, half)
    tied = after(tuple(map(outside, (neumann, schur))), message)
    neumann, schur = stage(
        bind(fetch), [described(array) for array in tied], *tied, scratch=semaphores(2), fetched=2
    )
    message = shifted(message, 1)
    half = gather_half(half, early[1:], neumann)
    part, near, far = stage(
        bind(neumann_load), [(faces, F32)] + halves, load, weight, message, neumann
    )
    far, near = far_block(far), crossed(near, 1)
    long, wide = ((2 * subs * nf, 2 * ncf), BF16), ((local_rows, 2 * nf), BF16)
    basis_high, basis_low, turned_high, turned_low, gram = stage(
        bind(static_basis), [long, long, wide, wide, ((local_rows, LANES), F32)], schur, after(message, part), rows
    )
    half = gather_half(half, late, gram)
    crossed_half = crossed(half, 1)
    share_rows, sum_rows = ((subs + 1) * ncf, columns), ((8, columns), F32)
    z_local, shares_rounded, shares, z_coarse, sums = stage(
        bind(coarse_load), [(faces, F32), (share_rows, BF16), (share_rows, F32), (share_rows, F32), sum_rows],
        load, part, near, far, weight, message, turned_high, turned_low, half, crossed_half, inverse, coarse, gram,
        scratch=[pltpu.VMEM((local_rows, columns), F32), pltpu.VMEM((nco, columns), BF16)],
    )
    half = gather_half(shares_rounded, early[:1])
    part, near, far, sums = stage(
        bind(schur_load), [(faces, F32)] + halves + [sum_rows],
        after(z_local, half), schur, basis_high, basis_low, z_coarse, sums,
    )
    half = gather_half(half, early[1:], far)
    near, far = after((near, far), half)
    far, near = far_block(far), crossed(near, 1)
    half = gather_half(half, late)
    part = after(part, half)
    image, part, near, far = stage(
        bind(neumann_image), [(own, F32), (faces, F32)] + halves, part, near, far, weight, message, neumann
    )
    crossed_half = crossed(half, 1)
    far, near = far_block(far), crossed(near, 1)
    y_local, product, quadratic, base = stage(
        bind(schur_image), products, image, part, near, far, weight, message, schur, turned_high, turned_low
    )
    sums, y_coarse, part, back = stage(
        bind(coarse_image), [((4, columns), F32), (coarse_own, F32), (own, F32), ((nf, columns), BF16)],
        half, crossed_half, inverse, message, shares, base, gram, quadratic, basis_high, basis_low, product, sums,
        scratch=[pltpu.VMEM((nco, columns), F32)],
    )
    z, y = stage(bind(complete), [(own, F32), (own, F32)], z_local, z_coarse, y_local, y_coarse, rows)
    for k, bit in enumerate(steps):
        sums = sums + after(crossed(sums, bit), y)
        if k == len(early) - 1:
            back = shifted(after(back, sums), -1)
    return stage(bind(combine), [(own, F32), (own, F32)], sums, load, z, y, image, part, back)


def solution(mesh):
    specs = P(("parts", AXIS), None)
    return jax.shard_map(shards, mesh=mesh, in_specs=(specs,) * 6, out_specs=(specs, specs), check_vma=False)
```

```python
import functools

import jax
import jax.numpy as jnp
from jax import lax
from jax.experimental import pallas as pl
from jax.experimental.pallas import tpu as pltpu
from jax.sharding import PartitionSpec as P

AXIS = "sub"
BF16 = jnp.bfloat16
F32 = jnp.float32
LANES = 128
VMEM_BYTES = 20 * 2**20


def shifted(block, distance):
    n = lax.axis_size(AXIS)
    return lax.ppermute(block, AXIS, [((i - distance) % n, i) for i in range(n)])


def crossed(block, bit):
    return lax.ppermute(block, AXIS, [(i, i ^ bit) for i in range(lax.axis_size(AXIS))])


def far_block(block):
    n = lax.axis_size(AXIS)
    return lax.ppermute(block, AXIS, [(i, (i + (1 if i % 2 else -1)) % n) for i in range(n)])


def bits():
    order = [1 << k for k in reversed(range(lax.axis_size(AXIS).bit_length() - 1))]
    return order[:-3] + order[-2:-1] + order[-3:-2] + order[-1:]


def after(value, *others):
    return lax.optimization_barrier((value, others))[0]


def gather_half(block, steps, *others):
    for bit in steps:
        block = jnp.concatenate([block, after(crossed(block, bit), *others)], axis=0)
    return block


def half_order():
    order = [0]
    for bit in bits()[:-1]:
        order += [place ^ bit for place in order]
    return order


def dot(a, b):
    return jnp.dot(a, b, preferred_element_type=F32)


def dot_nt(a, b):
    return lax.dot_general(a, b, (((1,), (1,)), ((), ())), preferred_element_type=F32)


def dot_tn(a, b):
    return lax.dot_general(a, b, (((0,), (0,)), ((), ())), preferred_element_type=F32)


def split(x):
    high = x.astype(BF16)
    return high, (x - high.astype(F32)).astype(BF16)


def split_dot(a, b, contract=dot):
    high, low = split(b)
    if isinstance(a, tuple):
        return contract(a[0], high) + contract(a[0], low) + contract(a[1], high)
    return contract(a, high) + contract(a, low)


def column_sum(x):
    return jnp.sum(x, axis=0, keepdims=True)


def rows_of(ref, index, count):
    return ref[index * count : (index + 1) * count]


def column_of(row):
    return jnp.broadcast_to(row, (8, row.shape[1])).T[:, :1]


def parts_of(row):
    high = row.astype(BF16).astype(F32)
    middle = (row - high).astype(BF16).astype(F32)
    return high, middle, row - high - middle


class Halo:
    def __init__(self, nf, ncf, nco, columns):
        self.nf, self.ncf, self.columns = nf, ncf, columns
        self.folds = nf // columns
        self.at_inverse = nf + ncf * self.folds
        self.at_weight = self.at_inverse + ncf * (nco // columns)
        self.weight_count = -(-3 * self.folds // 16) * 16
        self.height = self.at_weight + self.weight_count

    def unfolded(self, message, start, stop):
        return jnp.concatenate([message[k : k + self.ncf] for k in range(start, stop, self.ncf)], axis=1)

    def fold(self, message, block, start):
        ncf, columns = self.ncf, self.columns
        for k in range(block.shape[1] // columns):
            message[start + k * ncf : start + (k + 1) * ncf] = block[:, k * columns : (k + 1) * columns]

    def rows(self, message):
        return self.unfolded(message, self.nf, self.at_inverse)

    def inverse(self, message):
        return self.unfolded(message, self.at_inverse, self.at_weight)

    def weight(self, message):
        got = message[self.at_weight : self.height].astype(F32)
        f = self.folds
        row = [sum(got[k * f + i : k * f + i + 1] for k in range(3)) for i in range(f)]
        return jnp.concatenate([column_of(piece) for piece in row], axis=0)


def all_rows(halo, message, rows):
    ncf = halo.ncf
    return [halo.rows(message)] + [rows_of(rows, j, ncf) for j in range(rows.shape[0] // ncf)]


def is_odd():
    return lax.rem(lax.axis_index(AXIS), 2) == 1


def send(first, second, near, far):
    first, second, odd = first.astype(BF16), second.astype(BF16), is_odd()
    near[...] = jnp.where(odd, first, second)
    far[...] = jnp.where(odd, second, first)


def received(near, far):
    near, far, odd = near[...].astype(F32), far[...].astype(F32), is_odd()
    return jnp.where(odd, far, near), jnp.where(odd, near, far)


def all_weights(halo, message, weight):
    return [halo.weight(message)] + [column_of(weight[j : j + 1]) for j in range(weight.shape[0])]


def stage(kernel, shapes, *operands, scratch=(), fetched=0):
    out = [jax.ShapeDtypeStruct(shape, dtype) for shape, dtype in shapes]
    params = pltpu.CompilerParams(vmem_limit_bytes=VMEM_BYTES)
    spaces = [pltpu.HBM] * fetched + [pltpu.VMEM] * (len(operands) - fetched)
    call = pl.pallas_call(
        kernel,
        out_shape=out,
        in_specs=[pl.BlockSpec(memory_space=space) for space in spaces],
        scratch_shapes=list(scratch),
        compiler_params=params,
        name=kernel.func.__name__,
    )
    return call(*operands)


def prepare(
    halo, load, rows, weight, inverse, load_here, rows_here, weight_here, inverse_here, coarse_rounded, coarse, done
):
    ncf, nf = halo.ncf, halo.nf
    subs = load.shape[0] // nf
    copies = [pltpu.make_async_copy(rows, rows_here, done.at[subs])]
    copies += [
        pltpu.make_async_copy(rows_of(load.at, j, nf), rows_of(load_here.at, j, nf), done.at[j]) for j in range(subs)
    ]
    copies.append(pltpu.make_async_copy(weight, weight_here, done.at[subs + 1]))
    copies.append(pltpu.make_async_copy(inverse, inverse_here, done.at[subs + 2]))
    for copy in copies:
        copy.start()
    copies[0].wait()
    for j in range(subs):
        copies[1 + j].wait()
        coarse[j * ncf : (j + 1) * ncf] = dot(rows_of(rows_here, j, ncf), rows_of(load_here, j, nf).astype(BF16))
    coarse_rounded[...] = coarse[...].astype(BF16)
    copies[-2].wait()
    copies[-1].wait()


def halo_message(halo, load, weight, rows, inverse, message, pieces):
    ncf, nf, columns, folds = halo.ncf, halo.nf, halo.columns, halo.folds
    last = weight[weight.shape[0] - 1 :]
    message[:nf] = ((1.0 - column_of(last)) * load[load.shape[0] - nf :]).astype(BF16)
    halo.fold(message, rows[rows.shape[0] - ncf :], nf)
    halo.fold(message, inverse[inverse.shape[0] - ncf :], halo.at_inverse)
    pieces[...] = jnp.zeros_like(pieces)
    for k, values in enumerate(parts_of(last)):
        for i in range(folds):
            pieces[k * folds + i : k * folds + i + 1] = values[:, i * columns : (i + 1) * columns]
    message[halo.at_weight :] = pieces[...].astype(BF16)


def fetch(halo, neumann, schur, neumann_here, schur_here, done):
    pairs = ((neumann, neumann_here), (schur, schur_here))
    copies = [pltpu.make_async_copy(source, here, done.at[k]) for k, (source, here) in enumerate(pairs)]
    for copy in copies:
        copy.start()
    for copy in copies:
        copy.wait()


def neumann_half(neumann, left, right, j, half, nf):
    start = (2 * j + half) * nf
    return dot(neumann[start : start + nf], jnp.concatenate([left[j](), right[j]()], axis=0))


def neumann_outer(left, right, neumann, outer, near, far):
    nf, last = near.shape[0], len(left) - 1
    first = neumann_half(neumann, left, right, 0, 0, nf)
    second = neumann_half(neumann, left, right, last, 1, nf)
    outer[:nf], outer[nf:] = first, second
    send(first, second, near, far)


def neumann_inner(left, right, weights, neumann, inner, nf):
    for j in range(1, len(left)):
        before = neumann_half(neumann, left, right, j - 1, 1, nf)
        after_it = neumann_half(neumann, left, right, j, 0, nf)
        inner[(j - 1) * nf : j * nf] = weights(j) * before + (1.0 - weights(j)) * after_it


def face_of(outer, inner, e, nf):
    if e == 0:
        return outer[:nf]
    if e * nf > inner.shape[0]:
        return outer[nf:]
    return inner[(e - 1) * nf : e * nf]


def load_sides(halo, load, weight, message):
    subs, nf = weight.shape
    own = lambda e: column_of(weight[e - 1 : e])
    left = [lambda: message[:nf]]
    left += [lambda j=j: ((1.0 - own(j)) * rows_of(load, j - 1, nf)).astype(BF16) for j in range(1, subs)]
    right = [lambda j=j: (own(j + 1) * rows_of(load, j, nf)).astype(BF16) for j in range(subs)]
    return left, right, own


def load_outer(halo, load, weight, message, neumann, outer, near, far):
    left, right, _ = load_sides(halo, load, weight, message)
    neumann_outer(left, right, neumann, outer, near, far)


def load_inner(halo, load, weight, message, neumann, inner):
    left, right, own = load_sides(halo, load, weight, message)
    neumann_inner(left, right, own, neumann, inner, halo.nf)


def image_sides(halo, outer, inner, near, far, weight, message):
    subs, nf = weight.shape
    own = lambda e: column_of(weight[e - 1 : e]) if e else halo.weight(message)
    from_next, from_previous = received(near, far)
    face = lambda e: face_of(outer, inner, e, nf) + (from_previous if e == 0 else from_next if e == subs else 0.0)
    left = [lambda j=j: ((1.0 - own(j)) * face(j)).astype(BF16) for j in range(subs)]
    right = [lambda j=j: (own(j + 1) * face(j + 1)).astype(BF16) for j in range(subs)]
    return left, right, own, face


def image_outer(halo, outer_in, inner_in, near_in, far_in, weight, message, neumann, outer, near, far):
    left, right, _, _ = image_sides(halo, outer_in, inner_in, near_in, far_in, weight, message)
    neumann_outer(left, right, neumann, outer, near, far)


def image_inner(halo, outer_in, inner_in, near_in, far_in, weight, message, neumann, image, inner):
    nf = halo.nf
    left, right, own, face = image_sides(halo, outer_in, inner_in, near_in, far_in, weight, message)
    for e in range(1, len(left) + 1):
        image[(e - 1) * nf : e * nf] = face(e)
    neumann_inner(left, right, own, neumann, inner, nf)


def static_basis(halo, schur, message, rows, basis_high, basis_low, turned_high, turned_low, gram):
    ncf, nf = halo.ncf, halo.nf
    blocks = all_rows(halo, message, rows)
    gram[...] = jnp.zeros_like(gram)
    for j in range(len(blocks) - 1):
        matrix, pair = rows_of(schur, j, 2 * nf), blocks[j : j + 2]
        basis = jnp.concatenate([dot_nt(matrix[:, k * nf : (k + 1) * nf], pair[k]) for k in range(2)], axis=1)
        long, wide = slice(2 * j * nf, 2 * (j + 1) * nf), slice(2 * j * ncf, 2 * (j + 1) * ncf)
        basis_high[long], basis_low[long] = split(basis)
        turned = split(basis.T)
        turned_high[wide], turned_low[wide] = turned
        for k in range(2):
            half = slice(k * nf, (k + 1) * nf)
            gram[wide, k * ncf : (k + 1) * ncf] = dot_nt(turned[0][:, half], pair[k]) + dot_nt(turned[1][:, half], pair[k])


def complete_local(halo, outer, inner, near, far, weight, message, local):
    subs, nf = weight.shape
    weights = all_weights(halo, message, weight)
    from_next, from_previous = received(near, far)
    local[:nf] = (1.0 - weights[0]) * outer[:nf] + weights[0] * from_previous
    for e in range(1, subs):
        local[e * nf : (e + 1) * nf] = face_of(outer, inner, e, nf)
    local[subs * nf :] = weights[subs] * outer[nf:] + (1.0 - weights[subs]) * from_next


def project(halo, local, turned_high, turned_low, base):
    ncf, nf = halo.ncf, halo.nf
    for j in range(base.shape[0] // (2 * ncf)):
        here = slice(2 * j * ncf, 2 * (j + 1) * ncf)
        base[here] = split_dot((turned_high[here], turned_low[here]), local[j * nf : (j + 2) * nf])


def schur_faces(halo, local, schur):
    nf, columns = halo.nf, halo.columns
    faces, energy = [], 0.0
    for j in range(schur.shape[0] // (2 * nf)):
        vector = local[j * nf : (j + 2) * nf]
        both = dot(rows_of(schur, j, 2 * nf), jnp.concatenate(split(vector), axis=1))
        result = both[:, :columns] + both[:, columns:]
        energy = energy + column_sum(vector * result)
        faces[j:] = [result[:nf] if j == 0 else faces[j] + result[:nf], result[nf:]]
    return faces, energy


def schur_half(halo, local, schur, j, half):
    nf, columns = halo.nf, halo.columns
    start = (2 * j + half) * nf
    both = dot(schur[start : start + nf], jnp.concatenate(split(local[j * nf : (j + 2) * nf]), axis=1))
    return both[:, :columns] + both[:, columns:]


def basis_half(halo, basis_high, basis_low, solution, j, half):
    ncf, nf = halo.ncf, halo.nf
    here = slice((2 * j + half) * nf, (2 * j + half + 1) * nf)
    return split_dot((basis_high[here], basis_low[here]), solution[j * ncf : (j + 2) * ncf])


def schur_outer(halo, local, schur, basis_high, basis_low, solution, sums_in, outer, near, far, sums):
    nf = halo.nf
    last = schur.shape[0] // (2 * nf) - 1
    energy = sums_in[1:2]
    for here, face, j, half in ((slice(0, nf), 0, 0, 0), (slice(nf, 2 * nf), last + 1, last, 1)):
        outer[here] = basis_half(halo, basis_high, basis_low, solution, j, half)
        result = schur_half(halo, local, schur, j, half)
        energy = energy + column_sum(local[face * nf : (face + 1) * nf] * result)
        outer[here] += result
    send(outer[:nf], outer[nf:], near, far)
    sums[0:1] = sums_in[0:1]
    sums[1:2] = energy


def schur_inner(halo, local, schur, basis_high, basis_low, solution, inner, energies):
    nf = halo.nf
    for j in range(1, schur.shape[0] // (2 * nf)):
        here = slice((j - 1) * nf, j * nf)
        inner[here] = basis_half(halo, basis_high, basis_low, solution, j - 1, 1)
        inner[here] += basis_half(halo, basis_high, basis_low, solution, j, 0)
        result = schur_half(halo, local, schur, j - 1, 1)
        result = result + schur_half(halo, local, schur, j, 0)
        energies[j - 1 : j] = column_sum(local[j * nf : (j + 1) * nf] * result)
        inner[here] += result


def schur_image(
    halo, image, outer, inner, near, far, weight, message, schur, turned_high, turned_low, local, product, quadratic, base
):
    nf = halo.nf
    complete_local(halo, outer, inner, near, far, weight, message, local)
    project(halo, local, turned_high, turned_low, base)
    faces, energy = schur_faces(halo, local, schur)
    for e, face in enumerate(faces):
        product[e * nf : (e + 1) * nf] = face
    quadratic[0:1] = energy
    quadratic[1:2] = column_sum(image[...] * local[nf:])


def placed(half, crossed_half):
    me = lax.axis_index(AXIS)
    order = half_order()
    count = half.shape[0] // len(order)
    for flip, blocks in ((0, half), (1, crossed_half)):
        for k, place in enumerate(order):
            yield me ^ (place ^ flip), blocks, k * count, (k + 1) * count


def coarse_shares(ncf, results):
    shares = [results[0][:ncf]]
    for before, after in zip(results[:-1], results[1:]):
        shares.append(before[ncf:] + after[:ncf])
    return shares + [results[-1][ncf:]]


def coarse_products(ncf, x, base, gram):
    results, energy = [], 0.0
    for j in range(len(x) - 1):
        here = slice(2 * j * ncf, 2 * (j + 1) * ncf)
        pair = jnp.concatenate([x[j], x[j + 1]], axis=0)
        change = split_dot(split(gram[here, : 2 * ncf]), pair)
        energy = energy + column_sum(pair * (2.0 * base[here] + change))
        results.append(base[here] + change)
    return results, energy


def add_basis(nf, x, basis_high, basis_low, faces):
    faces = list(faces)
    for j in range(len(x) - 1):
        here = slice(2 * j * nf, 2 * (j + 1) * nf)
        pair = jnp.concatenate([x[j], x[j + 1]], axis=0)
        change = split_dot((basis_high[here], basis_low[here]), pair)
        faces[j] = faces[j] + change[:nf]
        faces[j + 1] = faces[j + 1] + change[nf:]
    return faces


def coarse_load(
    halo, load, outer, inner, near, far, weight, message, turned_high, turned_low, half, crossed_half, inverse, coarse, gram,
    local, shares_rounded, shares, solution, sums, base, gathered,
):
    ncf, nf = halo.ncf, halo.nf
    subs = weight.shape[0]
    complete_local(halo, outer, inner, near, far, weight, message, local)
    project(halo, local, turned_high, turned_low, base)
    for place, blocks, start, stop in placed(half, crossed_half):
        gathered[pl.ds(pl.multiple_of(place * subs * ncf, subs * ncf), subs * ncf)] = blocks[start:stop]
    everything = gathered[...]
    own = dot(inverse[...], everything)
    x = [dot(halo.inverse(message), everything)] + [own[j * ncf : (j + 1) * ncf] for j in range(subs)]
    results, energy = coarse_products(ncf, x, base, gram)
    for e, share in enumerate(coarse_shares(ncf, results)):
        shares[e * ncf : (e + 1) * ncf] = share
        solution[e * ncf : (e + 1) * ncf] = x[e]
    shares_rounded[...] = shares[...].astype(BF16)
    sums[0:1] = column_sum(load[...] * local[nf:]) + column_sum(coarse[...] * own)
    sums[1:2] = energy


def coarse_image(
    halo, half, crossed_half, inverse, message, shares, base, gram, quadratic, sums_in, energies, sums, solution, gathered
):
    ncf = halo.ncf
    subs = inverse.shape[0] // ncf
    total = gathered.shape[0]
    for place, blocks, start, stop in placed(half, crossed_half):
        gathered[pl.ds(pl.multiple_of(place * subs * ncf, subs * ncf), subs * ncf)] = blocks[start + ncf : stop].astype(F32)
    for place, blocks, start, stop in placed(half, crossed_half):
        before = pl.multiple_of(lax.rem(place * subs * ncf + (total - ncf), total), ncf)
        gathered[pl.ds(before, ncf)] += blocks[start : start + ncf].astype(F32)
    everything = gathered[...]
    own = split_dot(inverse[...], everything)
    x = [split_dot(halo.inverse(message), everything)] + [own[j * ncf : (j + 1) * ncf] for j in range(subs)]
    _, energy = coarse_products(ncf, x, base, gram)
    for e in range(subs + 1):
        solution[e * ncf : (e + 1) * ncf] = x[e]
    sums[0:1] = sums_in[0:1]
    sums[1:2] = sums_in[1:2] + column_sum(energies[...])
    sums[2:3] = quadratic[1:2] + column_sum(shares[...] * solution[...])
    sums[3:4] = quadratic[0:1] + energy


def complete(
    halo, z_local, z_coarse, y_local, y_coarse, rows, basis_high, basis_low, product, z, y, part, back
):
    ncf, nf = halo.ncf, halo.nf
    subs = rows.shape[0] // ncf
    x = [rows_of(y_coarse, e, ncf) for e in range(subs + 1)]
    faces = add_basis(nf, x, basis_high, basis_low, [rows_of(product, e, nf) for e in range(subs + 1)])
    for e in range(1, subs + 1):
        part[(e - 1) * nf : e * nf] = faces[e]
    back[...] = faces[0].astype(BF16)
    for j in range(subs):
        here, beside = slice(j * nf, (j + 1) * nf), slice((j + 1) * nf, (j + 2) * nf)
        for local, coarse, whole in ((z_local, z_coarse, z), (y_local, y_coarse, y)):
            whole[here] = local[beside] + split_dot(rows_of(rows, j, ncf), rows_of(coarse, j + 1, ncf), dot_tn)


def combine(halo, sums, load, z, y, image, part, from_next, solution, residual):
    nf = halo.nf
    a, b, c, d = (sums[k : k + 1] for k in range(4))
    step = a / b
    grow = step * (c / b)
    next_step = (grow - 1.0) / ((d - c * (c / b)) * (step / b))
    s = step + next_step * grow
    t = step * next_step
    solution[...] = s * z[...] - t * y[...]
    last = load.shape[0] - nf
    residual[:last] = load[:last] - s * image[:last] + t * part[:last]
    residual[last:] = load[last:] - s * image[last:] + t * (part[last:] + from_next[...].astype(F32))


def shards(right_side, face_weight, schur, neumann, constraint, coarse_inverse):
    subs, nf = face_weight.shape
    ncf = constraint.shape[0] // subs
    nco = coarse_inverse.shape[1]
    columns = right_side.shape[1]
    halo = Halo(nf, ncf, nco, columns)
    bind = lambda kernel: functools.partial(kernel, halo)
    faces, own = ((subs + 1) * nf, columns), (subs * nf, columns)
    coarse_own, local_rows = (subs * ncf, columns), 2 * subs * ncf
    products = [(faces, F32), (faces, F32), ((8, columns), F32), ((local_rows, columns), F32)]
    semaphores = lambda count: [pltpu.SemaphoreType.DMA((count,))]
    described = lambda array: (array.shape, array.dtype)
    outside = lambda array: pltpu.with_memory_space_constraint(array, pltpu.HBM)
    steps = bits()
    early, late = steps[:-2], steps[-2:-1]

    load, rows, weight, inverse, coarse_rounded, coarse = stage(
        bind(prepare),
        [described(right_side), described(constraint), described(face_weight), described(coarse_inverse)]
        + [(coarse_own, BF16), (coarse_own, F32)],
        *map(outside, (right_side, constraint, face_weight, coarse_inverse)), scratch=semaphores(subs + 3), fetched=4,
    )
    (message,) = stage(
        bind(halo_message), [((halo.height, columns), BF16)], load, weight, rows, inverse,
        scratch=[pltpu.VMEM((halo.weight_count, columns), F32)],
    )
    half = gather_half(coarse_rounded, early[:1])
    tied = after(tuple(map(outside, (neumann, schur))), message)
    neumann, schur = stage(
        bind(fetch), [described(array) for array in tied], *tied, scratch=semaphores(2), fetched=2
    )
    message = shifted(message, 1)
    outside_faces = [((2 * nf, columns), F32)] + 2 * [((nf, columns), BF16)]
    inside_faces = [(((subs - 1) * nf, columns), F32)]
    outer, near, far = stage(bind(load_outer), outside_faces, load, weight, message, neumann)
    (inner,) = stage(bind(load_inner), inside_faces, load, weight, after(message, far), neumann)
    half = gather_half(half, early[1:], far)
    far, near = far_block(far), crossed(near, 1)
    long, wide = ((2 * subs * nf, 2 * ncf), BF16), ((local_rows, 2 * nf), BF16)
    basis_high, basis_low, turned_high, turned_low, gram = stage(
        bind(static_basis), [long, long, wide, wide, ((local_rows, LANES), F32)], schur, after(message, inner), rows
    )
    half = gather_half(half, late, gram)
    crossed_half = crossed(half, 1)
    share_rows, sum_rows = ((subs + 1) * ncf, columns), ((8, columns), F32)
    z_local, shares_rounded, shares, z_coarse, sums = stage(
        bind(coarse_load), [(faces, F32), (share_rows, BF16), (share_rows, F32), (share_rows, F32), sum_rows],
        load, outer, inner, near, far, weight, message, turned_high, turned_low, half, crossed_half, inverse, coarse, gram,
        scratch=[pltpu.VMEM((local_rows, columns), F32), pltpu.VMEM((nco, columns), BF16)],
    )
    outer, near, far, sums = stage(
        bind(schur_outer), outside_faces + [sum_rows], z_local, schur, basis_high, basis_low, z_coarse, sums
    )
    inner, energies = stage(
        bind(schur_inner), inside_faces + [((subs - 1, columns), F32)], z_local, schur, basis_high, basis_low, z_coarse
    )
    half = gather_half(shares_rounded, early[:1], inner)
    far, near = far_block(far), crossed(near, 1)
    operands = outer, inner, near, far, weight, message, neumann
    outer, near, far = stage(bind(image_outer), outside_faces, *operands)
    image, inner = stage(bind(image_inner), [(own, F32)] + inside_faces, after(operands[0], far), *operands[1:])
    half = gather_half(half, early[1:], far)
    far, near = far_block(far), crossed(near, 1)
    half = gather_half(half, late, near, far, inner)
    crossed_half = crossed(half, 1)
    outer = after(outer, half)
    y_local, product, quadratic, base = stage(
        bind(schur_image), products, image, outer, inner, near, far, weight, message, schur, turned_high, turned_low
    )
    sums, y_coarse = stage(
        bind(coarse_image), [((4, columns), F32), (share_rows, F32)],
        half, crossed_half, inverse, message, shares, base, gram, quadratic, sums, energies,
        scratch=[pltpu.VMEM((nco, columns), F32)],
    )
    z, y, part, back = stage(
        bind(complete), [(own, F32), (own, F32), (own, F32), ((nf, columns), BF16)],
        z_local, z_coarse, y_local, y_coarse, rows, basis_high, basis_low, product,
    )
    for k, bit in enumerate(steps):
        sums = sums + after(crossed(sums, bit), y)
        if k == len(early) - 1:
            back = shifted(after(back, sums), -1)
    return stage(bind(combine), [(own, F32), (own, F32)], sums, load, z, y, image, part, back)


def solution(mesh):
    specs = P(("parts", AXIS), None)
    return jax.shard_map(shards, mesh=mesh, in_specs=(specs,) * 6, out_specs=(specs, specs), check_vma=False)
```

```python
import functools

import jax
import jax.numpy as jnp
from jax import lax
from jax.experimental import pallas as pl
from jax.experimental.pallas import tpu as pltpu
from jax.sharding import PartitionSpec as P

AXIS = "sub"
BF16 = jnp.bfloat16
F32 = jnp.float32
LANES = 128
VMEM_BYTES = 20 * 2**20


def shifted(block, distance):
    n = lax.axis_size(AXIS)
    return lax.ppermute(block, AXIS, [((i - distance) % n, i) for i in range(n)])


def crossed(block, bit):
    return lax.ppermute(block, AXIS, [(i, i ^ bit) for i in range(lax.axis_size(AXIS))])


def far_block(block):
    n = lax.axis_size(AXIS)
    return lax.ppermute(block, AXIS, [(i, (i + (1 if i % 2 else -1)) % n) for i in range(n)])


def bits():
    order = [1 << k for k in reversed(range(lax.axis_size(AXIS).bit_length() - 1))]
    return order[:-3] + order[-2:-1] + order[-3:-2] + order[-1:]


def after(value, *others):
    return lax.optimization_barrier((value, others))[0]


def gather_half(block, steps, *others):
    for bit in steps:
        block = jnp.concatenate([block, after(crossed(block, bit), *others)], axis=0)
    return block


def half_order():
    order = [0]
    for bit in bits()[:-1]:
        order += [place ^ bit for place in order]
    return order


def dot(a, b):
    return jnp.dot(a, b, preferred_element_type=F32)


def dot_nt(a, b):
    return lax.dot_general(a, b, (((1,), (1,)), ((), ())), preferred_element_type=F32)


def dot_tn(a, b):
    return lax.dot_general(a, b, (((0,), (0,)), ((), ())), preferred_element_type=F32)


def split(x):
    high = x.astype(BF16)
    return high, (x - high.astype(F32)).astype(BF16)


def split_dot(a, b, contract=dot):
    high, low = split(b)
    if isinstance(a, tuple):
        return contract(a[0], high) + contract(a[0], low) + contract(a[1], high)
    return contract(a, high) + contract(a, low)


def column_sum(x):
    return jnp.sum(x, axis=0, keepdims=True)


def rows_of(ref, index, count):
    return ref[index * count : (index + 1) * count]


def column_of(row):
    return jnp.broadcast_to(row, (8, row.shape[1])).T[:, :1]


def parts_of(row):
    high = row.astype(BF16).astype(F32)
    middle = (row - high).astype(BF16).astype(F32)
    return high, middle, row - high - middle


class Halo:
    def __init__(self, nf, ncf, nco, columns):
        self.nf, self.ncf, self.columns = nf, ncf, columns
        self.folds = nf // columns
        self.at_inverse = nf + ncf * self.folds
        self.at_weight = self.at_inverse + ncf * (nco // columns)
        self.weight_count = -(-3 * self.folds // 16) * 16
        self.height = self.at_weight + self.weight_count

    def unfolded(self, message, start, stop):
        return jnp.concatenate([message[k : k + self.ncf] for k in range(start, stop, self.ncf)], axis=1)

    def fold(self, message, block, start):
        ncf, columns = self.ncf, self.columns
        for k in range(block.shape[1] // columns):
            message[start + k * ncf : start + (k + 1) * ncf] = block[:, k * columns : (k + 1) * columns]

    def rows(self, message):
        return self.unfolded(message, self.nf, self.at_inverse)

    def inverse(self, message):
        return self.unfolded(message, self.at_inverse, self.at_weight)

    def weight(self, message):
        got = message[self.at_weight : self.height].astype(F32)
        f = self.folds
        row = [sum(got[k * f + i : k * f + i + 1] for k in range(3)) for i in range(f)]
        return jnp.concatenate([column_of(piece) for piece in row], axis=0)


def all_rows(halo, message, rows):
    ncf = halo.ncf
    return [halo.rows(message)] + [rows_of(rows, j, ncf) for j in range(rows.shape[0] // ncf)]


def is_odd():
    return lax.rem(lax.axis_index(AXIS), 2) == 1


def send(first, second, near, far):
    first, second, odd = first.astype(BF16), second.astype(BF16), is_odd()
    near[...] = jnp.where(odd, first, second)
    far[...] = jnp.where(odd, second, first)


def received(near, far):
    near, far, odd = near[...].astype(F32), far[...].astype(F32), is_odd()
    return jnp.where(odd, far, near), jnp.where(odd, near, far)


def all_weights(halo, message, weight):
    return [halo.weight(message)] + [column_of(weight[j : j + 1]) for j in range(weight.shape[0])]


def stage(kernel, shapes, *operands, scratch=(), fetched=0):
    out = [jax.ShapeDtypeStruct(shape, dtype) for shape, dtype in shapes]
    params = pltpu.CompilerParams(vmem_limit_bytes=VMEM_BYTES)
    spaces = [pltpu.HBM] * fetched + [pltpu.VMEM] * (len(operands) - fetched)
    call = pl.pallas_call(
        kernel,
        out_shape=out,
        in_specs=[pl.BlockSpec(memory_space=space) for space in spaces],
        scratch_shapes=list(scratch),
        compiler_params=params,
        name=kernel.func.__name__,
    )
    return call(*operands)


def prepare(
    halo, load, rows, weight, inverse, load_here, rows_here, weight_here, inverse_here, coarse_rounded, coarse, done
):
    ncf, nf = halo.ncf, halo.nf
    subs = load.shape[0] // nf
    copies = [pltpu.make_async_copy(rows, rows_here, done.at[subs])]
    copies += [
        pltpu.make_async_copy(rows_of(load.at, j, nf), rows_of(load_here.at, j, nf), done.at[j]) for j in range(subs)
    ]
    copies.append(pltpu.make_async_copy(weight, weight_here, done.at[subs + 1]))
    copies.append(pltpu.make_async_copy(inverse, inverse_here, done.at[subs + 2]))
    for copy in copies:
        copy.start()
    copies[0].wait()
    for j in range(subs):
        copies[1 + j].wait()
        coarse[j * ncf : (j + 1) * ncf] = dot(rows_of(rows_here, j, ncf), rows_of(load_here, j, nf).astype(BF16))
    coarse_rounded[...] = coarse[...].astype(BF16)
    copies[-2].wait()
    copies[-1].wait()


def halo_message(halo, load, weight, rows, inverse, message, pieces):
    ncf, nf, columns, folds = halo.ncf, halo.nf, halo.columns, halo.folds
    last = weight[weight.shape[0] - 1 :]
    message[:nf] = ((1.0 - column_of(last)) * load[load.shape[0] - nf :]).astype(BF16)
    halo.fold(message, rows[rows.shape[0] - ncf :], nf)
    halo.fold(message, inverse[inverse.shape[0] - ncf :], halo.at_inverse)
    pieces[...] = jnp.zeros_like(pieces)
    for k, values in enumerate(parts_of(last)):
        for i in range(folds):
            pieces[k * folds + i : k * folds + i + 1] = values[:, i * columns : (i + 1) * columns]
    message[halo.at_weight :] = pieces[...].astype(BF16)


def fetch(halo, neumann, schur, neumann_here, schur_here, done):
    pairs = ((neumann, neumann_here), (schur, schur_here))
    copies = [pltpu.make_async_copy(source, here, done.at[k]) for k, (source, here) in enumerate(pairs)]
    for copy in copies:
        copy.start()
    for copy in copies:
        copy.wait()


def neumann_half(neumann, left, right, j, half, nf):
    start = (2 * j + half) * nf
    return dot(neumann[start : start + nf], jnp.concatenate([left[j](), right[j]()], axis=0))


def neumann_outer(left, right, neumann, outer, near, far):
    nf, last = near.shape[0], len(left) - 1
    first = neumann_half(neumann, left, right, 0, 0, nf)
    second = neumann_half(neumann, left, right, last, 1, nf)
    outer[:nf], outer[nf:] = first, second
    send(first, second, near, far)


def neumann_inner(left, right, weights, neumann, inner, nf):
    for j in range(1, len(left)):
        before = neumann_half(neumann, left, right, j - 1, 1, nf)
        after_it = neumann_half(neumann, left, right, j, 0, nf)
        inner[(j - 1) * nf : j * nf] = weights(j) * before + (1.0 - weights(j)) * after_it


def face_of(outer, inner, e, nf):
    if e == 0:
        return outer[:nf]
    if e * nf > inner.shape[0]:
        return outer[nf:]
    return inner[(e - 1) * nf : e * nf]


def load_sides(halo, load, weight, message):
    subs, nf = weight.shape
    own = lambda e: column_of(weight[e - 1 : e])
    left = [lambda: message[:nf]]
    left += [lambda j=j: ((1.0 - own(j)) * rows_of(load, j - 1, nf)).astype(BF16) for j in range(1, subs)]
    right = [lambda j=j: (own(j + 1) * rows_of(load, j, nf)).astype(BF16) for j in range(subs)]
    return left, right, own


def load_outer(halo, load, weight, message, neumann, outer, near, far):
    left, right, _ = load_sides(halo, load, weight, message)
    neumann_outer(left, right, neumann, outer, near, far)


def load_inner(halo, load, weight, message, neumann, inner):
    left, right, own = load_sides(halo, load, weight, message)
    neumann_inner(left, right, own, neumann, inner, halo.nf)


def image_sides(halo, outer, inner, near, far, weight, message):
    subs, nf = weight.shape
    own = lambda e: column_of(weight[e - 1 : e]) if e else halo.weight(message)
    from_next, from_previous = received(near, far)
    face = lambda e: face_of(outer, inner, e, nf) + (from_previous if e == 0 else from_next if e == subs else 0.0)
    left = [lambda j=j: ((1.0 - own(j)) * face(j)).astype(BF16) for j in range(subs)]
    right = [lambda j=j: (own(j + 1) * face(j + 1)).astype(BF16) for j in range(subs)]
    return left, right, own, face


def image_outer(halo, outer_in, inner_in, near_in, far_in, weight, message, neumann, outer, near, far):
    left, right, _, _ = image_sides(halo, outer_in, inner_in, near_in, far_in, weight, message)
    neumann_outer(left, right, neumann, outer, near, far)


def image_inner(halo, outer_in, inner_in, near_in, far_in, weight, message, neumann, image, inner):
    nf = halo.nf
    left, right, own, face = image_sides(halo, outer_in, inner_in, near_in, far_in, weight, message)
    for e in range(1, len(left) + 1):
        image[(e - 1) * nf : e * nf] = face(e)
    neumann_inner(left, right, own, neumann, inner, nf)


def static_basis(halo, schur, message, rows, basis_high, basis_low, turned_high, turned_low, gram):
    ncf, nf = halo.ncf, halo.nf
    blocks = all_rows(halo, message, rows)
    gram[...] = jnp.zeros_like(gram)
    for j in range(len(blocks) - 1):
        matrix, pair = rows_of(schur, j, 2 * nf), blocks[j : j + 2]
        basis = jnp.concatenate([dot_nt(matrix[:, k * nf : (k + 1) * nf], pair[k]) for k in range(2)], axis=1)
        long, wide = slice(2 * j * nf, 2 * (j + 1) * nf), slice(2 * j * ncf, 2 * (j + 1) * ncf)
        basis_high[long], basis_low[long] = split(basis)
        turned = split(basis.T)
        turned_high[wide], turned_low[wide] = turned
        for k in range(2):
            half = slice(k * nf, (k + 1) * nf)
            gram[wide, k * ncf : (k + 1) * ncf] = dot_nt(turned[0][:, half], pair[k]) + dot_nt(turned[1][:, half], pair[k])


def complete_local(halo, outer, inner, near, far, weight, message, local):
    subs, nf = weight.shape
    weights = all_weights(halo, message, weight)
    from_next, from_previous = received(near, far)
    local[:nf] = (1.0 - weights[0]) * outer[:nf] + weights[0] * from_previous
    for e in range(1, subs):
        local[e * nf : (e + 1) * nf] = face_of(outer, inner, e, nf)
    local[subs * nf :] = weights[subs] * outer[nf:] + (1.0 - weights[subs]) * from_next


def project(halo, local, turned_high, turned_low, base):
    ncf, nf = halo.ncf, halo.nf
    for j in range(base.shape[0] // (2 * ncf)):
        here = slice(2 * j * ncf, 2 * (j + 1) * ncf)
        base[here] = split_dot((turned_high[here], turned_low[here]), local[j * nf : (j + 2) * nf])


def schur_faces(halo, local, schur):
    nf, columns = halo.nf, halo.columns
    faces, energy = [], 0.0
    for j in range(schur.shape[0] // (2 * nf)):
        vector = local[j * nf : (j + 2) * nf]
        both = dot(rows_of(schur, j, 2 * nf), jnp.concatenate(split(vector), axis=1))
        result = both[:, :columns] + both[:, columns:]
        energy = energy + column_sum(vector * result)
        faces[j:] = [result[:nf] if j == 0 else faces[j] + result[:nf], result[nf:]]
    return faces, energy


def schur_half(halo, local, schur, j, half):
    nf, columns = halo.nf, halo.columns
    start = (2 * j + half) * nf
    both = dot(schur[start : start + nf], jnp.concatenate(split(local[j * nf : (j + 2) * nf]), axis=1))
    return both[:, :columns] + both[:, columns:]


def basis_half(halo, basis_high, basis_low, solution, j, half):
    ncf, nf = halo.ncf, halo.nf
    here = slice((2 * j + half) * nf, (2 * j + half + 1) * nf)
    return split_dot((basis_high[here], basis_low[here]), solution[j * ncf : (j + 2) * ncf])


def schur_outer(halo, local, schur, basis_high, basis_low, solution, sums_in, outer, near, far, sums):
    nf = halo.nf
    last = schur.shape[0] // (2 * nf) - 1
    energy = sums_in[1:2]
    for here, face, j, half in ((slice(0, nf), 0, 0, 0), (slice(nf, 2 * nf), last + 1, last, 1)):
        outer[here] = basis_half(halo, basis_high, basis_low, solution, j, half)
        result = schur_half(halo, local, schur, j, half)
        energy = energy + column_sum(local[face * nf : (face + 1) * nf] * result)
        outer[here] += result
    send(outer[:nf], outer[nf:], near, far)
    sums[0:1] = sums_in[0:1]
    sums[1:2] = energy


def schur_inner(halo, local, schur, basis_high, basis_low, solution, inner, energies):
    nf = halo.nf
    for j in range(1, schur.shape[0] // (2 * nf)):
        here = slice((j - 1) * nf, j * nf)
        inner[here] = basis_half(halo, basis_high, basis_low, solution, j - 1, 1)
        inner[here] += basis_half(halo, basis_high, basis_low, solution, j, 0)
        result = schur_half(halo, local, schur, j - 1, 1)
        result = result + schur_half(halo, local, schur, j, 0)
        energies[j - 1 : j] = column_sum(local[j * nf : (j + 1) * nf] * result)
        inner[here] += result


def schur_image(
    halo, image, outer, inner, near, far, weight, message, schur, turned_high, turned_low, local, product, quadratic, base
):
    nf = halo.nf
    complete_local(halo, outer, inner, near, far, weight, message, local)
    project(halo, local, turned_high, turned_low, base)
    faces, energy = schur_faces(halo, local, schur)
    for e, face in enumerate(faces):
        product[e * nf : (e + 1) * nf] = face
    quadratic[0:1] = energy
    quadratic[1:2] = column_sum(image[...] * local[nf:])


def placed(half, crossed_half):
    me = lax.axis_index(AXIS)
    order = half_order()
    count = half.shape[0] // len(order)
    for flip, blocks in ((0, half), (1, crossed_half)):
        for k, place in enumerate(order):
            yield me ^ (place ^ flip), blocks, k * count, (k + 1) * count


def coarse_shares(ncf, results):
    shares = [results[0][:ncf]]
    for before, after in zip(results[:-1], results[1:]):
        shares.append(before[ncf:] + after[:ncf])
    return shares + [results[-1][ncf:]]


def coarse_products(ncf, x, base, gram):
    results, energy = [], 0.0
    for j in range(len(x) - 1):
        here = slice(2 * j * ncf, 2 * (j + 1) * ncf)
        pair = jnp.concatenate([x[j], x[j + 1]], axis=0)
        change = split_dot(split(gram[here, : 2 * ncf]), pair)
        energy = energy + column_sum(pair * (2.0 * base[here] + change))
        results.append(base[here] + change)
    return results, energy


def add_basis(nf, x, basis_high, basis_low, faces):
    faces = list(faces)
    for j in range(len(x) - 1):
        here = slice(2 * j * nf, 2 * (j + 1) * nf)
        pair = jnp.concatenate([x[j], x[j + 1]], axis=0)
        change = split_dot((basis_high[here], basis_low[here]), pair)
        faces[j] = faces[j] + change[:nf]
        faces[j + 1] = faces[j + 1] + change[nf:]
    return faces


def coarse_load(
    halo, load, outer, inner, near, far, weight, message, turned_high, turned_low, half, crossed_half, inverse, coarse, gram,
    local, shares_rounded, shares, solution, sums, base, gathered,
):
    ncf, nf = halo.ncf, halo.nf
    subs = weight.shape[0]
    complete_local(halo, outer, inner, near, far, weight, message, local)
    project(halo, local, turned_high, turned_low, base)
    for place, blocks, start, stop in placed(half, crossed_half):
        gathered[pl.ds(pl.multiple_of(place * subs * ncf, subs * ncf), subs * ncf)] = blocks[start:stop]
    everything = gathered[...]
    own = dot(inverse[...], everything)
    x = [dot(halo.inverse(message), everything)] + [own[j * ncf : (j + 1) * ncf] for j in range(subs)]
    results, energy = coarse_products(ncf, x, base, gram)
    for e, share in enumerate(coarse_shares(ncf, results)):
        shares[e * ncf : (e + 1) * ncf] = share
        solution[e * ncf : (e + 1) * ncf] = x[e]
    shares_rounded[...] = shares[...].astype(BF16)
    sums[0:1] = column_sum(load[...] * local[nf:]) + column_sum(coarse[...] * own)
    sums[1:2] = energy


def coarse_image(
    halo, half, crossed_half, inverse, message, shares, base, gram, quadratic, sums_in, energies, sums, solution, gathered
):
    ncf = halo.ncf
    subs = inverse.shape[0] // ncf
    total = gathered.shape[0]
    for place, blocks, start, stop in placed(half, crossed_half):
        gathered[pl.ds(pl.multiple_of(place * subs * ncf, subs * ncf), subs * ncf)] = blocks[start + ncf : stop].astype(F32)
    for place, blocks, start, stop in placed(half, crossed_half):
        before = pl.multiple_of(lax.rem(place * subs * ncf + (total - ncf), total), ncf)
        gathered[pl.ds(before, ncf)] += blocks[start : start + ncf].astype(F32)
    everything = gathered[...]
    own = split_dot(inverse[...], everything)
    x = [split_dot(halo.inverse(message), everything)] + [own[j * ncf : (j + 1) * ncf] for j in range(subs)]
    _, energy = coarse_products(ncf, x, base, gram)
    for e in range(subs + 1):
        solution[e * ncf : (e + 1) * ncf] = x[e]
    sums[0:1] = sums_in[0:1]
    sums[1:2] = sums_in[1:2] + column_sum(energies[...])
    sums[2:3] = quadratic[1:2] + column_sum(shares[...] * solution[...])
    sums[3:4] = quadratic[0:1] + energy


def complete(
    halo, z_local, z_coarse, y_local, y_coarse, rows, basis_high, basis_low, product, z, y, part, back
):
    ncf, nf = halo.ncf, halo.nf
    subs = rows.shape[0] // ncf
    x = [rows_of(y_coarse, e, ncf) for e in range(subs + 1)]
    faces = add_basis(nf, x, basis_high, basis_low, [rows_of(product, e, nf) for e in range(subs + 1)])
    for e in range(1, subs + 1):
        part[(e - 1) * nf : e * nf] = faces[e]
    back[...] = faces[0].astype(BF16)
    for j in range(subs):
        here, beside = slice(j * nf, (j + 1) * nf), slice((j + 1) * nf, (j + 2) * nf)
        for local, coarse, whole in ((z_local, z_coarse, z), (y_local, y_coarse, y)):
            whole[here] = local[beside] + split_dot(rows_of(rows, j, ncf), rows_of(coarse, j + 1, ncf), dot_tn)


def combine(halo, sums, load, z, y, image, part, from_next, solution, residual):
    nf = halo.nf
    a, b, c, d = (sums[k : k + 1] for k in range(4))
    step = a / b
    grow = step * (c / b)
    next_step = (grow - 1.0) / ((d - c * (c / b)) * (step / b))
    s = step + next_step * grow
    t = step * next_step
    solution[...] = s * z[...] - t * y[...]
    last = load.shape[0] - nf
    residual[:last] = load[:last] - s * image[:last] + t * part[:last]
    residual[last:] = load[last:] - s * image[last:] + t * (part[last:] + from_next[...].astype(F32))


def shards(right_side, face_weight, schur, neumann, constraint, coarse_inverse):
    subs, nf = face_weight.shape
    ncf = constraint.shape[0] // subs
    nco = coarse_inverse.shape[1]
    columns = right_side.shape[1]
    halo = Halo(nf, ncf, nco, columns)
    bind = lambda kernel: functools.partial(kernel, halo)
    faces, own = ((subs + 1) * nf, columns), (subs * nf, columns)
    coarse_own, local_rows = (subs * ncf, columns), 2 * subs * ncf
    products = [(faces, F32), (faces, F32), ((8, columns), F32), ((local_rows, columns), F32)]
    semaphores = lambda count: [pltpu.SemaphoreType.DMA((count,))]
    described = lambda array: (array.shape, array.dtype)
    outside = lambda array: pltpu.with_memory_space_constraint(array, pltpu.HBM)
    steps = bits()
    early, late = steps[:-2], steps[-2:-1]

    load, rows, weight, inverse, coarse_rounded, coarse = stage(
        bind(prepare),
        [described(right_side), described(constraint), described(face_weight), described(coarse_inverse)]
        + [(coarse_own, BF16), (coarse_own, F32)],
        *map(outside, (right_side, constraint, face_weight, coarse_inverse)), scratch=semaphores(subs + 3), fetched=4,
    )
    (message,) = stage(
        bind(halo_message), [((halo.height, columns), BF16)], load, weight, rows, inverse,
        scratch=[pltpu.VMEM((halo.weight_count, columns), F32)],
    )
    tied = after(tuple(map(outside, (neumann, schur))), message)
    neumann, schur = stage(
        bind(fetch), [described(array) for array in tied], *tied, scratch=semaphores(2), fetched=2
    )
    message = shifted(message, 1)
    half = gather_half(coarse_rounded, early[:1], neumann)
    outside_faces = [((2 * nf, columns), F32)] + 2 * [((nf, columns), BF16)]
    inside_faces = [(((subs - 1) * nf, columns), F32)]
    outer, near, far = stage(bind(load_outer), outside_faces, load, weight, message, neumann)
    (inner,) = stage(bind(load_inner), inside_faces, load, weight, after(message, far), neumann)
    half = gather_half(half, early[1:], far)
    far, near = far_block(far), crossed(near, 1)
    long, wide = ((2 * subs * nf, 2 * ncf), BF16), ((local_rows, 2 * nf), BF16)
    basis_high, basis_low, turned_high, turned_low, gram = stage(
        bind(static_basis), [long, long, wide, wide, ((local_rows, LANES), F32)], schur, after(message, inner), rows
    )
    half = gather_half(half, late, gram)
    crossed_half = crossed(half, 1)
    share_rows, sum_rows = ((subs + 1) * ncf, columns), ((8, columns), F32)
    z_local, shares_rounded, shares, z_coarse, sums = stage(
        bind(coarse_load), [(faces, F32), (share_rows, BF16), (share_rows, F32), (share_rows, F32), sum_rows],
        load, outer, inner, near, far, weight, message, turned_high, turned_low, half, crossed_half, inverse, coarse, gram,
        scratch=[pltpu.VMEM((local_rows, columns), F32), pltpu.VMEM((nco, columns), BF16)],
    )
    outer, near, far, sums = stage(
        bind(schur_outer), outside_faces + [sum_rows], z_local, schur, basis_high, basis_low, z_coarse, sums
    )
    half = gather_half(shares_rounded, early[:1], far)
    inner, energies = stage(
        bind(schur_inner), inside_faces + [((subs - 1, columns), F32)], after(z_local, half), schur, basis_high, basis_low, z_coarse
    )
    far, near = far_block(far), crossed(near, 1)
    operands = outer, inner, near, far, weight, message, neumann
    outer, near, far = stage(bind(image_outer), outside_faces, *operands)
    image, inner = stage(bind(image_inner), [(own, F32)] + inside_faces, after(operands[0], far), *operands[1:])
    half = gather_half(half, early[1:], far)
    far, near = far_block(far), crossed(near, 1)
    half = gather_half(half, late, near, far, inner)
    crossed_half = crossed(half, 1)
    outer = after(outer, half)
    y_local, product, quadratic, base = stage(
        bind(schur_image), products, image, outer, inner, near, far, weight, message, schur, turned_high, turned_low
    )
    sums, y_coarse = stage(
        bind(coarse_image), [((4, columns), F32), (share_rows, F32)],
        half, crossed_half, inverse, message, shares, base, gram, quadratic, sums, energies,
        scratch=[pltpu.VMEM((nco, columns), F32)],
    )
    z, y, part, back = stage(
        bind(complete), [(own, F32), (own, F32), (own, F32), ((nf, columns), BF16)],
        z_local, z_coarse, y_local, y_coarse, rows, basis_high, basis_low, product,
    )
    for k, bit in enumerate(steps):
        sums = sums + after(crossed(sums, bit), y)
        if k == len(early) - 1:
            back = shifted(after(back, sums), -1)
    return stage(bind(combine), [(own, F32), (own, F32)], sums, load, z, y, image, part, back)


def solution(mesh):
    specs = P(("parts", AXIS), None)
    return jax.shard_map(shards, mesh=mesh, in_specs=(specs,) * 6, out_specs=(specs, specs), check_vma=False)
```

```python
import functools

import jax
import jax.numpy as jnp
from jax import lax
from jax.experimental import pallas as pl
from jax.experimental.pallas import tpu as pltpu
from jax.sharding import PartitionSpec as P

AXIS = "sub"
BF16 = jnp.bfloat16
F32 = jnp.float32
LANES = 128
VMEM_BYTES = 20 * 2**20


def shifted(block, distance):
    n = lax.axis_size(AXIS)
    return lax.ppermute(block, AXIS, [((i - distance) % n, i) for i in range(n)])


def crossed(block, bit):
    return lax.ppermute(block, AXIS, [(i, i ^ bit) for i in range(lax.axis_size(AXIS))])


def far_block(block):
    n = lax.axis_size(AXIS)
    return lax.ppermute(block, AXIS, [(i, (i + (1 if i % 2 else -1)) % n) for i in range(n)])


def bits():
    order = [1 << k for k in reversed(range(lax.axis_size(AXIS).bit_length() - 1))]
    return order[:-3] + order[-2:-1] + order[-3:-2] + order[-1:]


def after(value, *others):
    return lax.optimization_barrier((value, others))[0]


def gather_half(block, steps, *others):
    for bit in steps:
        block = jnp.concatenate([block, after(crossed(block, bit), *others)], axis=0)
    return block


def half_order():
    order = [0]
    for bit in bits()[:-1]:
        order += [place ^ bit for place in order]
    return order


def dot(a, b):
    return jnp.dot(a, b, preferred_element_type=F32)


def dot_nt(a, b):
    return lax.dot_general(a, b, (((1,), (1,)), ((), ())), preferred_element_type=F32)


def dot_tn(a, b):
    return lax.dot_general(a, b, (((0,), (0,)), ((), ())), preferred_element_type=F32)


def split(x):
    high = x.astype(BF16)
    return high, (x - high.astype(F32)).astype(BF16)


def split_dot(a, b, contract=dot):
    high, low = split(b)
    if isinstance(a, tuple):
        return contract(a[0], high) + contract(a[0], low) + contract(a[1], high)
    return contract(a, high) + contract(a, low)


def column_sum(x):
    return jnp.sum(x, axis=0, keepdims=True)


def rows_of(ref, index, count):
    return ref[index * count : (index + 1) * count]


def column_of(row):
    return jnp.broadcast_to(row, (8, row.shape[1])).T[:, :1]


def parts_of(row):
    high = row.astype(BF16).astype(F32)
    middle = (row - high).astype(BF16).astype(F32)
    return high, middle, row - high - middle


class Halo:
    def __init__(self, nf, ncf, nco, columns):
        self.nf, self.ncf, self.columns = nf, ncf, columns
        self.folds = nf // columns
        self.at_inverse = nf + ncf * self.folds
        self.at_weight = self.at_inverse + ncf * (nco // columns)
        self.weight_count = -(-3 * self.folds // 16) * 16
        self.height = self.at_weight + self.weight_count

    def unfolded(self, message, start, stop):
        return jnp.concatenate([message[k : k + self.ncf] for k in range(start, stop, self.ncf)], axis=1)

    def fold(self, message, block, start):
        ncf, columns = self.ncf, self.columns
        for k in range(block.shape[1] // columns):
            message[start + k * ncf : start + (k + 1) * ncf] = block[:, k * columns : (k + 1) * columns]

    def rows(self, message):
        return self.unfolded(message, self.nf, self.at_inverse)

    def inverse(self, message):
        return self.unfolded(message, self.at_inverse, self.at_weight)

    def weight(self, message):
        got = message[self.at_weight : self.height].astype(F32)
        f = self.folds
        row = [sum(got[k * f + i : k * f + i + 1] for k in range(3)) for i in range(f)]
        return jnp.concatenate([column_of(piece) for piece in row], axis=0)


def all_rows(halo, message, rows):
    ncf = halo.ncf
    return [halo.rows(message)] + [rows_of(rows, j, ncf) for j in range(rows.shape[0] // ncf)]


def is_odd():
    return lax.rem(lax.axis_index(AXIS), 2) == 1


def send(first, second, near, far):
    first, second, odd = first.astype(BF16), second.astype(BF16), is_odd()
    near[...] = jnp.where(odd, first, second)
    far[...] = jnp.where(odd, second, first)


def received(near, far):
    near, far, odd = near[...].astype(F32), far[...].astype(F32), is_odd()
    return jnp.where(odd, far, near), jnp.where(odd, near, far)


def all_weights(halo, message, weight):
    return [halo.weight(message)] + [column_of(weight[j : j + 1]) for j in range(weight.shape[0])]


def stage(kernel, shapes, *operands, scratch=(), fetched=0):
    out = [jax.ShapeDtypeStruct(shape, dtype) for shape, dtype in shapes]
    params = pltpu.CompilerParams(vmem_limit_bytes=VMEM_BYTES)
    spaces = [pltpu.HBM] * fetched + [pltpu.VMEM] * (len(operands) - fetched)
    call = pl.pallas_call(
        kernel,
        out_shape=out,
        in_specs=[pl.BlockSpec(memory_space=space) for space in spaces],
        scratch_shapes=list(scratch),
        compiler_params=params,
        name=kernel.func.__name__,
    )
    return call(*operands)


def prepare(
    halo, load, rows, weight, inverse, load_here, rows_here, weight_here, inverse_here, coarse_rounded, coarse, done
):
    ncf, nf = halo.ncf, halo.nf
    subs = load.shape[0] // nf
    copies = [pltpu.make_async_copy(rows, rows_here, done.at[subs])]
    copies += [
        pltpu.make_async_copy(rows_of(load.at, j, nf), rows_of(load_here.at, j, nf), done.at[j]) for j in range(subs)
    ]
    copies.append(pltpu.make_async_copy(weight, weight_here, done.at[subs + 1]))
    copies.append(pltpu.make_async_copy(inverse, inverse_here, done.at[subs + 2]))
    for copy in copies:
        copy.start()
    copies[0].wait()
    for j in range(subs):
        copies[1 + j].wait()
        coarse[j * ncf : (j + 1) * ncf] = dot(rows_of(rows_here, j, ncf), rows_of(load_here, j, nf).astype(BF16))
    coarse_rounded[...] = coarse[...].astype(BF16)
    copies[-2].wait()
    copies[-1].wait()


def halo_message(halo, load, weight, rows, inverse, message, pieces):
    ncf, nf, columns, folds = halo.ncf, halo.nf, halo.columns, halo.folds
    last = weight[weight.shape[0] - 1 :]
    message[:nf] = ((1.0 - column_of(last)) * load[load.shape[0] - nf :]).astype(BF16)
    halo.fold(message, rows[rows.shape[0] - ncf :], nf)
    halo.fold(message, inverse[inverse.shape[0] - ncf :], halo.at_inverse)
    pieces[...] = jnp.zeros_like(pieces)
    for k, values in enumerate(parts_of(last)):
        for i in range(folds):
            pieces[k * folds + i : k * folds + i + 1] = values[:, i * columns : (i + 1) * columns]
    message[halo.at_weight :] = pieces[...].astype(BF16)


def fetch(halo, neumann, schur, neumann_here, schur_here, done):
    pairs = ((neumann, neumann_here), (schur, schur_here))
    copies = [pltpu.make_async_copy(source, here, done.at[k]) for k, (source, here) in enumerate(pairs)]
    for copy in copies:
        copy.start()
    for copy in copies:
        copy.wait()


def neumann_half(neumann, left, right, j, half, nf):
    start = (2 * j + half) * nf
    return dot(neumann[start : start + nf], jnp.concatenate([left[j](), right[j]()], axis=0))


def neumann_outer(left, right, neumann, outer, near, far):
    nf, last = near.shape[0], len(left) - 1
    first = neumann_half(neumann, left, right, 0, 0, nf)
    second = neumann_half(neumann, left, right, last, 1, nf)
    outer[:nf], outer[nf:] = first, second
    send(first, second, near, far)


def neumann_inner(left, right, weights, neumann, inner, nf):
    for j in range(1, len(left)):
        before = neumann_half(neumann, left, right, j - 1, 1, nf)
        after_it = neumann_half(neumann, left, right, j, 0, nf)
        inner[(j - 1) * nf : j * nf] = weights(j) * before + (1.0 - weights(j)) * after_it


def face_of(outer, inner, e, nf):
    if e == 0:
        return outer[:nf]
    if e * nf > inner.shape[0]:
        return outer[nf:]
    return inner[(e - 1) * nf : e * nf]


def load_sides(halo, load, weight, message):
    subs, nf = weight.shape
    own = lambda e: column_of(weight[e - 1 : e])
    left = [lambda: message[:nf]]
    left += [lambda j=j: ((1.0 - own(j)) * rows_of(load, j - 1, nf)).astype(BF16) for j in range(1, subs)]
    right = [lambda j=j: (own(j + 1) * rows_of(load, j, nf)).astype(BF16) for j in range(subs)]
    return left, right, own


def load_outer(halo, load, weight, message, neumann, outer, near, far):
    left, right, _ = load_sides(halo, load, weight, message)
    neumann_outer(left, right, neumann, outer, near, far)


def load_inner(halo, load, weight, message, neumann, inner):
    left, right, own = load_sides(halo, load, weight, message)
    neumann_inner(left, right, own, neumann, inner, halo.nf)


def image_sides(halo, outer, inner, near, far, weight, message):
    subs, nf = weight.shape
    own = lambda e: column_of(weight[e - 1 : e]) if e else halo.weight(message)
    from_next, from_previous = received(near, far)
    face = lambda e: face_of(outer, inner, e, nf) + (from_previous if e == 0 else from_next if e == subs else 0.0)
    left = [lambda j=j: ((1.0 - own(j)) * face(j)).astype(BF16) for j in range(subs)]
    right = [lambda j=j: (own(j + 1) * face(j + 1)).astype(BF16) for j in range(subs)]
    return left, right, own, face


def image_outer(halo, outer_in, inner_in, near_in, far_in, weight, message, neumann, outer, near, far):
    left, right, _, _ = image_sides(halo, outer_in, inner_in, near_in, far_in, weight, message)
    neumann_outer(left, right, neumann, outer, near, far)


def image_inner(halo, outer_in, inner_in, near_in, far_in, weight, message, neumann, image, inner):
    nf = halo.nf
    left, right, own, face = image_sides(halo, outer_in, inner_in, near_in, far_in, weight, message)
    for e in range(1, len(left) + 1):
        image[(e - 1) * nf : e * nf] = face(e)
    neumann_inner(left, right, own, neumann, inner, nf)


def static_basis(halo, schur, message, rows, basis_high, basis_low, turned_high, turned_low, gram):
    ncf, nf = halo.ncf, halo.nf
    blocks = all_rows(halo, message, rows)
    gram[...] = jnp.zeros_like(gram)
    for j in range(len(blocks) - 1):
        matrix, pair = rows_of(schur, j, 2 * nf), blocks[j : j + 2]
        basis = jnp.concatenate([dot_nt(matrix[:, k * nf : (k + 1) * nf], pair[k]) for k in range(2)], axis=1)
        long, wide = slice(2 * j * nf, 2 * (j + 1) * nf), slice(2 * j * ncf, 2 * (j + 1) * ncf)
        basis_high[long], basis_low[long] = split(basis)
        turned = split(basis.T)
        turned_high[wide], turned_low[wide] = turned
        for k in range(2):
            half = slice(k * nf, (k + 1) * nf)
            gram[wide, k * ncf : (k + 1) * ncf] = dot_nt(turned[0][:, half], pair[k]) + dot_nt(turned[1][:, half], pair[k])


def complete_local(halo, outer, inner, near, far, weight, message, local):
    subs, nf = weight.shape
    weights = all_weights(halo, message, weight)
    from_next, from_previous = received(near, far)
    local[:nf] = (1.0 - weights[0]) * outer[:nf] + weights[0] * from_previous
    for e in range(1, subs):
        local[e * nf : (e + 1) * nf] = face_of(outer, inner, e, nf)
    local[subs * nf :] = weights[subs] * outer[nf:] + (1.0 - weights[subs]) * from_next


def project(halo, local, turned_high, turned_low, base):
    ncf, nf = halo.ncf, halo.nf
    for j in range(base.shape[0] // (2 * ncf)):
        here = slice(2 * j * ncf, 2 * (j + 1) * ncf)
        base[here] = split_dot((turned_high[here], turned_low[here]), local[j * nf : (j + 2) * nf])


def schur_faces(halo, local, schur):
    nf, columns = halo.nf, halo.columns
    faces, energy = [], 0.0
    for j in range(schur.shape[0] // (2 * nf)):
        vector = local[j * nf : (j + 2) * nf]
        both = dot(rows_of(schur, j, 2 * nf), jnp.concatenate(split(vector), axis=1))
        result = both[:, :columns] + both[:, columns:]
        energy = energy + column_sum(vector * result)
        faces[j:] = [result[:nf] if j == 0 else faces[j] + result[:nf], result[nf:]]
    return faces, energy


def schur_half(halo, local, schur, j, half):
    nf, columns = halo.nf, halo.columns
    start = (2 * j + half) * nf
    both = dot(schur[start : start + nf], jnp.concatenate(split(local[j * nf : (j + 2) * nf]), axis=1))
    return both[:, :columns] + both[:, columns:]


def basis_half(halo, basis_high, basis_low, solution, j, half):
    ncf, nf = halo.ncf, halo.nf
    here = slice((2 * j + half) * nf, (2 * j + half + 1) * nf)
    return split_dot((basis_high[here], basis_low[here]), solution[j * ncf : (j + 2) * ncf])


def schur_outer(halo, local, schur, basis_high, basis_low, solution, sums_in, outer, near, far, sums):
    nf = halo.nf
    last = schur.shape[0] // (2 * nf) - 1
    energy = sums_in[1:2]
    for here, face, j, half in ((slice(0, nf), 0, 0, 0), (slice(nf, 2 * nf), last + 1, last, 1)):
        outer[here] = basis_half(halo, basis_high, basis_low, solution, j, half)
        result = schur_half(halo, local, schur, j, half)
        energy = energy + column_sum(local[face * nf : (face + 1) * nf] * result)
        outer[here] += result
    send(outer[:nf], outer[nf:], near, far)
    sums[0:1] = sums_in[0:1]
    sums[1:2] = energy


def schur_inner(halo, local, schur, basis_high, basis_low, solution, inner, energies):
    nf = halo.nf
    for j in range(1, schur.shape[0] // (2 * nf)):
        here = slice((j - 1) * nf, j * nf)
        inner[here] = basis_half(halo, basis_high, basis_low, solution, j - 1, 1)
        inner[here] += basis_half(halo, basis_high, basis_low, solution, j, 0)
        result = schur_half(halo, local, schur, j - 1, 1)
        result = result + schur_half(halo, local, schur, j, 0)
        energies[j - 1 : j] = column_sum(local[j * nf : (j + 1) * nf] * result)
        inner[here] += result


def schur_image(
    halo, image, outer, inner, near, far, weight, message, schur, turned_high, turned_low, local, product, quadratic, base
):
    nf = halo.nf
    complete_local(halo, outer, inner, near, far, weight, message, local)
    project(halo, local, turned_high, turned_low, base)
    faces, energy = schur_faces(halo, local, schur)
    for e, face in enumerate(faces):
        product[e * nf : (e + 1) * nf] = face
    quadratic[0:1] = energy
    quadratic[1:2] = column_sum(image[...] * local[nf:])


def placed(half, crossed_half):
    me = lax.axis_index(AXIS)
    order = half_order()
    count = half.shape[0] // len(order)
    for flip, blocks in ((0, half), (1, crossed_half)):
        for k, place in enumerate(order):
            yield me ^ (place ^ flip), blocks, k * count, (k + 1) * count


def coarse_shares(ncf, results):
    shares = [results[0][:ncf]]
    for before, after in zip(results[:-1], results[1:]):
        shares.append(before[ncf:] + after[:ncf])
    return shares + [results[-1][ncf:]]


def coarse_products(ncf, x, base, gram):
    results, energy = [], 0.0
    for j in range(len(x) - 1):
        here = slice(2 * j * ncf, 2 * (j + 1) * ncf)
        pair = jnp.concatenate([x[j], x[j + 1]], axis=0)
        change = split_dot(split(gram[here, : 2 * ncf]), pair)
        energy = energy + column_sum(pair * (2.0 * base[here] + change))
        results.append(base[here] + change)
    return results, energy


def add_basis(nf, x, basis_high, basis_low, faces):
    faces = list(faces)
    for j in range(len(x) - 1):
        here = slice(2 * j * nf, 2 * (j + 1) * nf)
        pair = jnp.concatenate([x[j], x[j + 1]], axis=0)
        change = split_dot((basis_high[here], basis_low[here]), pair)
        faces[j] = faces[j] + change[:nf]
        faces[j + 1] = faces[j + 1] + change[nf:]
    return faces


def coarse_load(
    halo, load, outer, inner, near, far, weight, message, turned_high, turned_low, half, crossed_half, inverse, coarse, gram,
    local, shares_rounded, shares, solution, sums, base, gathered,
):
    ncf, nf = halo.ncf, halo.nf
    subs = weight.shape[0]
    complete_local(halo, outer, inner, near, far, weight, message, local)
    project(halo, local, turned_high, turned_low, base)
    for place, blocks, start, stop in placed(half, crossed_half):
        gathered[pl.ds(pl.multiple_of(place * subs * ncf, subs * ncf), subs * ncf)] = blocks[start:stop]
    everything = gathered[...]
    own = dot(inverse[...], everything)
    x = [dot(halo.inverse(message), everything)] + [own[j * ncf : (j + 1) * ncf] for j in range(subs)]
    results, energy = coarse_products(ncf, x, base, gram)
    for e, share in enumerate(coarse_shares(ncf, results)):
        shares[e * ncf : (e + 1) * ncf] = share
        solution[e * ncf : (e + 1) * ncf] = x[e]
    shares_rounded[...] = shares[...].astype(BF16)
    sums[0:1] = column_sum(load[...] * local[nf:]) + column_sum(coarse[...] * own)
    sums[1:2] = energy


def coarse_image(
    halo, half, crossed_half, inverse, message, shares, base, gram, quadratic, sums_in, energies, sums, solution, gathered
):
    ncf = halo.ncf
    subs = inverse.shape[0] // ncf
    total = gathered.shape[0]
    for place, blocks, start, stop in placed(half, crossed_half):
        gathered[pl.ds(pl.multiple_of(place * subs * ncf, subs * ncf), subs * ncf)] = blocks[start + ncf : stop].astype(F32)
    for place, blocks, start, stop in placed(half, crossed_half):
        before = pl.multiple_of(lax.rem(place * subs * ncf + (total - ncf), total), ncf)
        gathered[pl.ds(before, ncf)] += blocks[start : start + ncf].astype(F32)
    everything = gathered[...]
    own = split_dot(inverse[...], everything)
    x = [split_dot(halo.inverse(message), everything)] + [own[j * ncf : (j + 1) * ncf] for j in range(subs)]
    _, energy = coarse_products(ncf, x, base, gram)
    for e in range(subs + 1):
        solution[e * ncf : (e + 1) * ncf] = x[e]
    sums[0:1] = sums_in[0:1]
    sums[1:2] = sums_in[1:2] + column_sum(energies[...])
    sums[2:3] = quadratic[1:2] + column_sum(shares[...] * solution[...])
    sums[3:4] = quadratic[0:1] + energy


def complete(
    halo, z_local, z_coarse, y_local, y_coarse, rows, basis_high, basis_low, product, z, y, part, back
):
    ncf, nf = halo.ncf, halo.nf
    subs = rows.shape[0] // ncf
    x = [rows_of(y_coarse, e, ncf) for e in range(subs + 1)]
    faces = add_basis(nf, x, basis_high, basis_low, [rows_of(product, e, nf) for e in range(subs + 1)])
    for e in range(1, subs + 1):
        part[(e - 1) * nf : e * nf] = faces[e]
    back[...] = faces[0].astype(BF16)
    for j in range(subs):
        here, beside = slice(j * nf, (j + 1) * nf), slice((j + 1) * nf, (j + 2) * nf)
        for local, coarse, whole in ((z_local, z_coarse, z), (y_local, y_coarse, y)):
            whole[here] = local[beside] + split_dot(rows_of(rows, j, ncf), rows_of(coarse, j + 1, ncf), dot_tn)


def combine(halo, sums, load, z, y, image, part, from_next, solution, residual):
    nf = halo.nf
    a, b, c, d = (sums[k : k + 1] for k in range(4))
    step = a / b
    grow = step * (c / b)
    next_step = (grow - 1.0) / ((d - c * (c / b)) * (step / b))
    s = step + next_step * grow
    t = step * next_step
    solution[...] = s * z[...] - t * y[...]
    last = load.shape[0] - nf
    residual[:last] = load[:last] - s * image[:last] + t * part[:last]
    residual[last:] = load[last:] - s * image[last:] + t * (part[last:] + from_next[...].astype(F32))


def shards(right_side, face_weight, schur, neumann, constraint, coarse_inverse):
    subs, nf = face_weight.shape
    ncf = constraint.shape[0] // subs
    nco = coarse_inverse.shape[1]
    columns = right_side.shape[1]
    halo = Halo(nf, ncf, nco, columns)
    bind = lambda kernel: functools.partial(kernel, halo)
    faces, own = ((subs + 1) * nf, columns), (subs * nf, columns)
    coarse_own, local_rows = (subs * ncf, columns), 2 * subs * ncf
    products = [(faces, F32), (faces, F32), ((8, columns), F32), ((local_rows, columns), F32)]
    semaphores = lambda count: [pltpu.SemaphoreType.DMA((count,))]
    described = lambda array: (array.shape, array.dtype)
    outside = lambda array: pltpu.with_memory_space_constraint(array, pltpu.HBM)
    steps = bits()
    early, late = steps[:-2], steps[-2:-1]

    load, rows, weight, inverse, coarse_rounded, coarse = stage(
        bind(prepare),
        [described(right_side), described(constraint), described(face_weight), described(coarse_inverse)]
        + [(coarse_own, BF16), (coarse_own, F32)],
        *map(outside, (right_side, constraint, face_weight, coarse_inverse)), scratch=semaphores(subs + 3), fetched=4,
    )
    (message,) = stage(
        bind(halo_message), [((halo.height, columns), BF16)], load, weight, rows, inverse,
        scratch=[pltpu.VMEM((halo.weight_count, columns), F32)],
    )
    tied = after(tuple(map(outside, (neumann, schur))), message)
    neumann, schur = stage(
        bind(fetch), [described(array) for array in tied], *tied, scratch=semaphores(2), fetched=2
    )
    message = shifted(message, 1)
    half = gather_half(coarse_rounded, early[:1], neumann)
    outside_faces = [((2 * nf, columns), F32)] + 2 * [((nf, columns), BF16)]
    inside_faces = [(((subs - 1) * nf, columns), F32)]
    outer, near, far = stage(bind(load_outer), outside_faces, load, weight, message, neumann)
    (inner,) = stage(bind(load_inner), inside_faces, load, weight, after(message, far), neumann)
    half = gather_half(half, early[1:], far)
    far, near = far_block(far), crossed(near, 1)
    long, wide = ((2 * subs * nf, 2 * ncf), BF16), ((local_rows, 2 * nf), BF16)
    basis_high, basis_low, turned_high, turned_low, gram = stage(
        bind(static_basis), [long, long, wide, wide, ((local_rows, LANES), F32)], schur, after(message, inner), rows
    )
    half = gather_half(half, late, gram)
    crossed_half = crossed(half, 1)
    share_rows, sum_rows = ((subs + 1) * ncf, columns), ((8, columns), F32)
    z_local, shares_rounded, shares, z_coarse, sums = stage(
        bind(coarse_load), [(faces, F32), (share_rows, BF16), (share_rows, F32), (share_rows, F32), sum_rows],
        load, outer, inner, near, far, weight, message, turned_high, turned_low, half, crossed_half, inverse, coarse, gram,
        scratch=[pltpu.VMEM((local_rows, columns), F32), pltpu.VMEM((nco, columns), BF16)],
    )
    outer, near, far, sums = stage(
        bind(schur_outer), outside_faces + [sum_rows], z_local, schur, basis_high, basis_low, z_coarse, sums
    )
    inner, energies = stage(
        bind(schur_inner), inside_faces + [((subs - 1, columns), F32)], z_local, schur, basis_high, basis_low, z_coarse
    )
    half = gather_half(shares_rounded, early[:1], inner)
    far, near = far_block(far), crossed(near, 1)
    operands = outer, inner, near, far, weight, message, neumann
    outer, near, far = stage(bind(image_outer), outside_faces, *operands)
    image, inner = stage(bind(image_inner), [(own, F32)] + inside_faces, after(operands[0], far), *operands[1:])
    half = gather_half(half, early[1:], far)
    far, near = far_block(far), crossed(near, 1)
    half = gather_half(half, late, near, far, inner)
    crossed_half = crossed(half, 1)
    outer = after(outer, half)
    y_local, product, quadratic, base = stage(
        bind(schur_image), products, image, outer, inner, near, far, weight, message, schur, turned_high, turned_low
    )
    sums, y_coarse = stage(
        bind(coarse_image), [((4, columns), F32), (share_rows, F32)],
        half, crossed_half, inverse, message, shares, base, gram, quadratic, sums, energies,
        scratch=[pltpu.VMEM((nco, columns), F32)],
    )
    z, y, part, back = stage(
        bind(complete), [(own, F32), (own, F32), (own, F32), ((nf, columns), BF16)],
        z_local, z_coarse, y_local, y_coarse, rows, basis_high, basis_low, product,
    )
    for k, bit in enumerate(early + steps[-1:] + late):
        sums = sums + after(crossed(sums, bit), y)
        if k == len(early) - 1:
            back = shifted(after(back, sums), -1)
    return stage(bind(combine), [(own, F32), (own, F32)], sums, load, z, y, image, part, back)


def solution(mesh):
    specs = P(("parts", AXIS), None)
    return jax.shard_map(shards, mesh=mesh, in_specs=(specs,) * 6, out_specs=(specs, specs), check_vma=False)
```

```python
import functools

import jax
import jax.numpy as jnp
from jax import lax
from jax.experimental import pallas as pl
from jax.experimental.pallas import tpu as pltpu
from jax.sharding import PartitionSpec as P

AXIS = "sub"
BF16 = jnp.bfloat16
F32 = jnp.float32
LANES = 128
VMEM_BYTES = 20 * 2**20


def shifted(block, distance):
    n = lax.axis_size(AXIS)
    return lax.ppermute(block, AXIS, [((i - distance) % n, i) for i in range(n)])


def crossed(block, bit):
    return lax.ppermute(block, AXIS, [(i, i ^ bit) for i in range(lax.axis_size(AXIS))])


def far_block(block):
    n = lax.axis_size(AXIS)
    return lax.ppermute(block, AXIS, [(i, (i + (1 if i % 2 else -1)) % n) for i in range(n)])


def bits():
    order = [1 << k for k in reversed(range(lax.axis_size(AXIS).bit_length() - 1))]
    return order[:-3] + order[-2:-1] + order[-3:-2] + order[-1:]


def after(value, *others):
    return lax.optimization_barrier((value, others))[0]


def gather_half(block, steps, *others):
    for bit in steps:
        block = jnp.concatenate([block, after(crossed(block, bit), *others)], axis=0)
    return block


def half_order():
    order = [0]
    for bit in bits()[:-1]:
        order += [place ^ bit for place in order]
    return order


def dot(a, b):
    return jnp.dot(a, b, preferred_element_type=F32)


def dot_nt(a, b):
    return lax.dot_general(a, b, (((1,), (1,)), ((), ())), preferred_element_type=F32)


def dot_tn(a, b):
    return lax.dot_general(a, b, (((0,), (0,)), ((), ())), preferred_element_type=F32)


def split(x):
    high = x.astype(BF16)
    return high, (x - high.astype(F32)).astype(BF16)


def split_dot(a, b, contract=dot):
    high, low = split(b)
    if isinstance(a, tuple):
        return contract(a[0], high) + contract(a[0], low) + contract(a[1], high)
    return contract(a, high) + contract(a, low)


def column_sum(x):
    return jnp.sum(x, axis=0, keepdims=True)


def rows_of(ref, index, count):
    return ref[index * count : (index + 1) * count]


def column_of(row):
    return jnp.broadcast_to(row, (8, row.shape[1])).T[:, :1]


def parts_of(row):
    high = row.astype(BF16).astype(F32)
    middle = (row - high).astype(BF16).astype(F32)
    return high, middle, row - high - middle


class Halo:
    def __init__(self, nf, ncf, nco, columns):
        self.nf, self.ncf, self.columns = nf, ncf, columns
        self.folds = nf // columns
        self.at_inverse = nf + ncf * self.folds
        self.at_weight = self.at_inverse + ncf * (nco // columns)
        self.weight_count = -(-3 * self.folds // 16) * 16
        self.height = self.at_weight + self.weight_count

    def unfolded(self, message, start, stop):
        return jnp.concatenate([message[k : k + self.ncf] for k in range(start, stop, self.ncf)], axis=1)

    def fold(self, message, block, start):
        ncf, columns = self.ncf, self.columns
        for k in range(block.shape[1] // columns):
            message[start + k * ncf : start + (k + 1) * ncf] = block[:, k * columns : (k + 1) * columns]

    def rows(self, message):
        return self.unfolded(message, self.nf, self.at_inverse)

    def inverse(self, message):
        return self.unfolded(message, self.at_inverse, self.at_weight)

    def weight(self, message):
        got = message[self.at_weight : self.height].astype(F32)
        f = self.folds
        row = [sum(got[k * f + i : k * f + i + 1] for k in range(3)) for i in range(f)]
        return jnp.concatenate([column_of(piece) for piece in row], axis=0)


def all_rows(halo, message, rows):
    ncf = halo.ncf
    return [halo.rows(message)] + [rows_of(rows, j, ncf) for j in range(rows.shape[0] // ncf)]


def is_odd():
    return lax.rem(lax.axis_index(AXIS), 2) == 1


def send(first, second, near, far):
    first, second, odd = first.astype(BF16), second.astype(BF16), is_odd()
    near[...] = jnp.where(odd, first, second)
    far[...] = jnp.where(odd, second, first)


def received(near, far):
    near, far, odd = near[...].astype(F32), far[...].astype(F32), is_odd()
    return jnp.where(odd, far, near), jnp.where(odd, near, far)


def all_weights(halo, message, weight):
    return [halo.weight(message)] + [column_of(weight[j : j + 1]) for j in range(weight.shape[0])]


def stage(kernel, shapes, *operands, scratch=(), fetched=0, outputs=pltpu.VMEM):
    out = [jax.ShapeDtypeStruct(shape, dtype) for shape, dtype in shapes]
    params = pltpu.CompilerParams(vmem_limit_bytes=VMEM_BYTES)
    spaces = [pltpu.HBM] * fetched + [pltpu.VMEM] * (len(operands) - fetched)
    call = pl.pallas_call(
        kernel,
        out_shape=out,
        out_specs=[pl.BlockSpec(memory_space=outputs)] * len(out),
        in_specs=[pl.BlockSpec(memory_space=space) for space in spaces],
        scratch_shapes=list(scratch),
        compiler_params=params,
        name=kernel.func.__name__,
    )
    return call(*operands)


def prepare(
    halo, load, rows, weight, inverse, load_here, rows_here, weight_here, inverse_here, coarse_rounded, coarse, done
):
    ncf, nf = halo.ncf, halo.nf
    subs = load.shape[0] // nf
    copies = [pltpu.make_async_copy(rows, rows_here, done.at[subs])]
    copies += [
        pltpu.make_async_copy(rows_of(load.at, j, nf), rows_of(load_here.at, j, nf), done.at[j]) for j in range(subs)
    ]
    copies.append(pltpu.make_async_copy(weight, weight_here, done.at[subs + 1]))
    copies.append(pltpu.make_async_copy(inverse, inverse_here, done.at[subs + 2]))
    for copy in copies:
        copy.start()
    copies[0].wait()
    for j in range(subs):
        copies[1 + j].wait()
        coarse[j * ncf : (j + 1) * ncf] = dot(rows_of(rows_here, j, ncf), rows_of(load_here, j, nf).astype(BF16))
    coarse_rounded[...] = coarse[...].astype(BF16)
    copies[-2].wait()
    copies[-1].wait()


def halo_message(halo, load, weight, rows, inverse, message, pieces):
    ncf, nf, columns, folds = halo.ncf, halo.nf, halo.columns, halo.folds
    last = weight[weight.shape[0] - 1 :]
    message[:nf] = ((1.0 - column_of(last)) * load[load.shape[0] - nf :]).astype(BF16)
    halo.fold(message, rows[rows.shape[0] - ncf :], nf)
    halo.fold(message, inverse[inverse.shape[0] - ncf :], halo.at_inverse)
    pieces[...] = jnp.zeros_like(pieces)
    for k, values in enumerate(parts_of(last)):
        for i in range(folds):
            pieces[k * folds + i : k * folds + i + 1] = values[:, i * columns : (i + 1) * columns]
    message[halo.at_weight :] = pieces[...].astype(BF16)


def fetch(halo, neumann, schur, neumann_here, schur_here, done):
    pairs = ((neumann, neumann_here), (schur, schur_here))
    copies = [pltpu.make_async_copy(source, here, done.at[k]) for k, (source, here) in enumerate(pairs)]
    for copy in copies:
        copy.start()
    for copy in copies:
        copy.wait()


def neumann_half(neumann, left, right, j, half, nf):
    start = (2 * j + half) * nf
    return dot(neumann[start : start + nf], jnp.concatenate([left[j](), right[j]()], axis=0))


def neumann_outer(left, right, neumann, outer, near, far):
    nf, last = near.shape[0], len(left) - 1
    first = neumann_half(neumann, left, right, 0, 0, nf)
    second = neumann_half(neumann, left, right, last, 1, nf)
    outer[:nf], outer[nf:] = first, second
    send(first, second, near, far)


def neumann_inner(left, right, weights, neumann, inner, nf):
    for j in range(1, len(left)):
        before = neumann_half(neumann, left, right, j - 1, 1, nf)
        after_it = neumann_half(neumann, left, right, j, 0, nf)
        inner[(j - 1) * nf : j * nf] = weights(j) * before + (1.0 - weights(j)) * after_it


def face_of(outer, inner, e, nf):
    if e == 0:
        return outer[:nf]
    if e * nf > inner.shape[0]:
        return outer[nf:]
    return inner[(e - 1) * nf : e * nf]


def load_sides(halo, load, weight, message):
    subs, nf = weight.shape
    own = lambda e: column_of(weight[e - 1 : e])
    left = [lambda: message[:nf]]
    left += [lambda j=j: ((1.0 - own(j)) * rows_of(load, j - 1, nf)).astype(BF16) for j in range(1, subs)]
    right = [lambda j=j: (own(j + 1) * rows_of(load, j, nf)).astype(BF16) for j in range(subs)]
    return left, right, own


def load_outer(halo, load, weight, message, neumann, outer, near, far):
    left, right, _ = load_sides(halo, load, weight, message)
    neumann_outer(left, right, neumann, outer, near, far)


def load_inner(halo, load, weight, message, neumann, inner):
    left, right, own = load_sides(halo, load, weight, message)
    neumann_inner(left, right, own, neumann, inner, halo.nf)


def image_sides(halo, outer, inner, near, far, weight, message):
    subs, nf = weight.shape
    own = lambda e: column_of(weight[e - 1 : e]) if e else halo.weight(message)
    from_next, from_previous = received(near, far)
    face = lambda e: face_of(outer, inner, e, nf) + (from_previous if e == 0 else from_next if e == subs else 0.0)
    left = [lambda j=j: ((1.0 - own(j)) * face(j)).astype(BF16) for j in range(subs)]
    right = [lambda j=j: (own(j + 1) * face(j + 1)).astype(BF16) for j in range(subs)]
    return left, right, own, face


def image_outer(halo, outer_in, inner_in, near_in, far_in, weight, message, neumann, outer, near, far):
    left, right, _, _ = image_sides(halo, outer_in, inner_in, near_in, far_in, weight, message)
    neumann_outer(left, right, neumann, outer, near, far)


def image_inner(halo, outer_in, inner_in, near_in, far_in, weight, message, neumann, image, inner):
    nf = halo.nf
    left, right, own, face = image_sides(halo, outer_in, inner_in, near_in, far_in, weight, message)
    for e in range(1, len(left) + 1):
        image[(e - 1) * nf : e * nf] = face(e)
    neumann_inner(left, right, own, neumann, inner, nf)


def static_basis(halo, schur, message, rows, basis_high, basis_low, turned_high, turned_low, gram):
    ncf, nf = halo.ncf, halo.nf
    blocks = all_rows(halo, message, rows)
    gram[...] = jnp.zeros_like(gram)
    for j in range(len(blocks) - 1):
        matrix, pair = rows_of(schur, j, 2 * nf), blocks[j : j + 2]
        basis = jnp.concatenate([dot_nt(matrix[:, k * nf : (k + 1) * nf], pair[k]) for k in range(2)], axis=1)
        long, wide = slice(2 * j * nf, 2 * (j + 1) * nf), slice(2 * j * ncf, 2 * (j + 1) * ncf)
        basis_high[long], basis_low[long] = split(basis)
        turned = split(basis.T)
        turned_high[wide], turned_low[wide] = turned
        for k in range(2):
            half = slice(k * nf, (k + 1) * nf)
            gram[wide, k * ncf : (k + 1) * ncf] = dot_nt(turned[0][:, half], pair[k]) + dot_nt(turned[1][:, half], pair[k])


def complete_local(halo, outer, inner, near, far, weight, message, local):
    subs, nf = weight.shape
    weights = all_weights(halo, message, weight)
    from_next, from_previous = received(near, far)
    local[:nf] = (1.0 - weights[0]) * outer[:nf] + weights[0] * from_previous
    for e in range(1, subs):
        local[e * nf : (e + 1) * nf] = face_of(outer, inner, e, nf)
    local[subs * nf :] = weights[subs] * outer[nf:] + (1.0 - weights[subs]) * from_next


def project(halo, local, turned_high, turned_low, base):
    ncf, nf = halo.ncf, halo.nf
    for j in range(base.shape[0] // (2 * ncf)):
        here = slice(2 * j * ncf, 2 * (j + 1) * ncf)
        base[here] = split_dot((turned_high[here], turned_low[here]), local[j * nf : (j + 2) * nf])


def schur_faces(halo, local, schur):
    nf, columns = halo.nf, halo.columns
    faces, energy = [], 0.0
    for j in range(schur.shape[0] // (2 * nf)):
        vector = local[j * nf : (j + 2) * nf]
        both = dot(rows_of(schur, j, 2 * nf), jnp.concatenate(split(vector), axis=1))
        result = both[:, :columns] + both[:, columns:]
        energy = energy + column_sum(vector * result)
        faces[j:] = [result[:nf] if j == 0 else faces[j] + result[:nf], result[nf:]]
    return faces, energy


def schur_half(halo, local, schur, j, half):
    nf, columns = halo.nf, halo.columns
    start = (2 * j + half) * nf
    both = dot(schur[start : start + nf], jnp.concatenate(split(local[j * nf : (j + 2) * nf]), axis=1))
    return both[:, :columns] + both[:, columns:]


def basis_half(halo, basis_high, basis_low, solution, j, half):
    ncf, nf = halo.ncf, halo.nf
    here = slice((2 * j + half) * nf, (2 * j + half + 1) * nf)
    return split_dot((basis_high[here], basis_low[here]), solution[j * ncf : (j + 2) * ncf])


def schur_outer(halo, local, schur, basis_high, basis_low, solution, sums_in, outer, near, far, sums):
    nf = halo.nf
    last = schur.shape[0] // (2 * nf) - 1
    energy = sums_in[1:2]
    for here, face, j, half in ((slice(0, nf), 0, 0, 0), (slice(nf, 2 * nf), last + 1, last, 1)):
        outer[here] = basis_half(halo, basis_high, basis_low, solution, j, half)
        result = schur_half(halo, local, schur, j, half)
        energy = energy + column_sum(local[face * nf : (face + 1) * nf] * result)
        outer[here] += result
    send(outer[:nf], outer[nf:], near, far)
    sums[0:1] = sums_in[0:1]
    sums[1:2] = energy


def schur_inner(halo, local, schur, basis_high, basis_low, solution, inner, energies):
    nf = halo.nf
    for j in range(1, schur.shape[0] // (2 * nf)):
        here = slice((j - 1) * nf, j * nf)
        inner[here] = basis_half(halo, basis_high, basis_low, solution, j - 1, 1)
        inner[here] += basis_half(halo, basis_high, basis_low, solution, j, 0)
        result = schur_half(halo, local, schur, j - 1, 1)
        result = result + schur_half(halo, local, schur, j, 0)
        energies[j - 1 : j] = column_sum(local[j * nf : (j + 1) * nf] * result)
        inner[here] += result


def schur_image(
    halo, image, outer, inner, near, far, weight, message, schur, turned_high, turned_low, local, product, quadratic, base
):
    nf = halo.nf
    complete_local(halo, outer, inner, near, far, weight, message, local)
    project(halo, local, turned_high, turned_low, base)
    faces, energy = schur_faces(halo, local, schur)
    for e, face in enumerate(faces):
        product[e * nf : (e + 1) * nf] = face
    quadratic[0:1] = energy
    quadratic[1:2] = column_sum(image[...] * local[nf:])


def placed(half, crossed_half):
    me = lax.axis_index(AXIS)
    order = half_order()
    count = half.shape[0] // len(order)
    for flip, blocks in ((0, half), (1, crossed_half)):
        for k, place in enumerate(order):
            yield me ^ (place ^ flip), blocks, k * count, (k + 1) * count


def coarse_shares(ncf, results):
    shares = [results[0][:ncf]]
    for before, after in zip(results[:-1], results[1:]):
        shares.append(before[ncf:] + after[:ncf])
    return shares + [results[-1][ncf:]]


def coarse_products(ncf, x, base, gram):
    results, energy = [], 0.0
    for j in range(len(x) - 1):
        here = slice(2 * j * ncf, 2 * (j + 1) * ncf)
        pair = jnp.concatenate([x[j], x[j + 1]], axis=0)
        change = split_dot(split(gram[here, : 2 * ncf]), pair)
        energy = energy + column_sum(pair * (2.0 * base[here] + change))
        results.append(base[here] + change)
    return results, energy


def add_basis(nf, x, basis_high, basis_low, faces):
    faces = list(faces)
    for j in range(len(x) - 1):
        here = slice(2 * j * nf, 2 * (j + 1) * nf)
        pair = jnp.concatenate([x[j], x[j + 1]], axis=0)
        change = split_dot((basis_high[here], basis_low[here]), pair)
        faces[j] = faces[j] + change[:nf]
        faces[j + 1] = faces[j + 1] + change[nf:]
    return faces


def coarse_load(
    halo, load, outer, inner, near, far, weight, message, turned_high, turned_low, half, crossed_half, inverse, coarse, gram,
    local, shares_rounded, shares, solution, sums, base, gathered,
):
    ncf, nf = halo.ncf, halo.nf
    subs = weight.shape[0]
    complete_local(halo, outer, inner, near, far, weight, message, local)
    project(halo, local, turned_high, turned_low, base)
    for place, blocks, start, stop in placed(half, crossed_half):
        gathered[pl.ds(pl.multiple_of(place * subs * ncf, subs * ncf), subs * ncf)] = blocks[start:stop]
    everything = gathered[...]
    own = dot(inverse[...], everything)
    x = [dot(halo.inverse(message), everything)] + [own[j * ncf : (j + 1) * ncf] for j in range(subs)]
    results, energy = coarse_products(ncf, x, base, gram)
    for e, share in enumerate(coarse_shares(ncf, results)):
        shares[e * ncf : (e + 1) * ncf] = share
        solution[e * ncf : (e + 1) * ncf] = x[e]
    shares_rounded[...] = shares[...].astype(BF16)
    sums[0:1] = column_sum(load[...] * local[nf:]) + column_sum(coarse[...] * own)
    sums[1:2] = energy


def coarse_image(
    halo, half, crossed_half, inverse, message, shares, base, gram, quadratic, sums_in, energies, sums, solution, gathered
):
    ncf = halo.ncf
    subs = inverse.shape[0] // ncf
    total = gathered.shape[0]
    for place, blocks, start, stop in placed(half, crossed_half):
        gathered[pl.ds(pl.multiple_of(place * subs * ncf, subs * ncf), subs * ncf)] = blocks[start + ncf : stop].astype(F32)
    for place, blocks, start, stop in placed(half, crossed_half):
        before = pl.multiple_of(lax.rem(place * subs * ncf + (total - ncf), total), ncf)
        gathered[pl.ds(before, ncf)] += blocks[start : start + ncf].astype(F32)
    everything = gathered[...]
    own = split_dot(inverse[...], everything)
    x = [split_dot(halo.inverse(message), everything)] + [own[j * ncf : (j + 1) * ncf] for j in range(subs)]
    _, energy = coarse_products(ncf, x, base, gram)
    for e in range(subs + 1):
        solution[e * ncf : (e + 1) * ncf] = x[e]
    sums[0:1] = sums_in[0:1]
    sums[1:2] = sums_in[1:2] + column_sum(energies[...])
    sums[2:3] = quadratic[1:2] + column_sum(shares[...] * solution[...])
    sums[3:4] = quadratic[0:1] + energy


def complete(
    halo, z_local, z_coarse, y_local, y_coarse, rows, basis_high, basis_low, product, z, y, part, back
):
    ncf, nf = halo.ncf, halo.nf
    subs = rows.shape[0] // ncf
    x = [rows_of(y_coarse, e, ncf) for e in range(subs + 1)]
    faces = add_basis(nf, x, basis_high, basis_low, [rows_of(product, e, nf) for e in range(subs + 1)])
    for e in range(1, subs + 1):
        part[(e - 1) * nf : e * nf] = faces[e]
    back[...] = faces[0].astype(BF16)
    for j in range(subs):
        here, beside = slice(j * nf, (j + 1) * nf), slice((j + 1) * nf, (j + 2) * nf)
        for local, coarse, whole in ((z_local, z_coarse, z), (y_local, y_coarse, y)):
            whole[here] = local[beside] + split_dot(rows_of(rows, j, ncf), rows_of(coarse, j + 1, ncf), dot_tn)


def combine(halo, sums, load, z, y, image, part, from_next, solution, residual, solution_here, residual_here, done):
    nf = halo.nf
    subs = load.shape[0] // nf
    a, b, c, d = (sums[k : k + 1] for k in range(4))
    step = a / b
    grow = step * (c / b)
    next_step = (grow - 1.0) / ((d - c * (c / b)) * (step / b))
    s = step + next_step * grow
    t = step * next_step
    copies = []

    def copy_out(here, source, target):
        copies.append(pltpu.make_async_copy(source.at[here], target.at[here], done.at[len(copies)]))
        copies[-1].start()

    for j in range(subs):
        here = slice(j * nf, (j + 1) * nf)
        solution_here[here] = s * z[here] - t * y[here]
        copy_out(pl.ds(j * nf, nf), solution_here, solution)
        last = part[here] + from_next[...].astype(F32) if j == subs - 1 else part[here]
        residual_here[here] = load[here] - s * image[here] + t * last
        copy_out(pl.ds(j * nf, nf), residual_here, residual)
    for copy in copies:
        copy.wait()


def shards(right_side, face_weight, schur, neumann, constraint, coarse_inverse):
    subs, nf = face_weight.shape
    ncf = constraint.shape[0] // subs
    nco = coarse_inverse.shape[1]
    columns = right_side.shape[1]
    halo = Halo(nf, ncf, nco, columns)
    bind = lambda kernel: functools.partial(kernel, halo)
    faces, own = ((subs + 1) * nf, columns), (subs * nf, columns)
    coarse_own, local_rows = (subs * ncf, columns), 2 * subs * ncf
    products = [(faces, F32), (faces, F32), ((8, columns), F32), ((local_rows, columns), F32)]
    semaphores = lambda count: [pltpu.SemaphoreType.DMA((count,))]
    described = lambda array: (array.shape, array.dtype)
    outside = lambda array: pltpu.with_memory_space_constraint(array, pltpu.HBM)
    steps = bits()
    early, late = steps[:-2], steps[-2:-1]

    load, rows, weight, inverse, coarse_rounded, coarse = stage(
        bind(prepare),
        [described(right_side), described(constraint), described(face_weight), described(coarse_inverse)]
        + [(coarse_own, BF16), (coarse_own, F32)],
        *map(outside, (right_side, constraint, face_weight, coarse_inverse)), scratch=semaphores(subs + 3), fetched=4,
    )
    (message,) = stage(
        bind(halo_message), [((halo.height, columns), BF16)], load, weight, rows, inverse,
        scratch=[pltpu.VMEM((halo.weight_count, columns), F32)],
    )
    tied = after(tuple(map(outside, (neumann, schur))), message)
    neumann, schur = stage(
        bind(fetch), [described(array) for array in tied], *tied, scratch=semaphores(2), fetched=2
    )
    message = shifted(message, 1)
    half = gather_half(coarse_rounded, early[:1], neumann)
    outside_faces = [((2 * nf, columns), F32)] + 2 * [((nf, columns), BF16)]
    inside_faces = [(((subs - 1) * nf, columns), F32)]
    outer, near, far = stage(bind(load_outer), outside_faces, load, weight, message, neumann)
    (inner,) = stage(bind(load_inner), inside_faces, load, weight, after(message, far), neumann)
    half = gather_half(half, early[1:], far)
    far, near = far_block(far), crossed(near, 1)
    long, wide = ((2 * subs * nf, 2 * ncf), BF16), ((local_rows, 2 * nf), BF16)
    basis_high, basis_low, turned_high, turned_low, gram = stage(
        bind(static_basis), [long, long, wide, wide, ((local_rows, LANES), F32)], schur, after(message, inner), rows
    )
    half = gather_half(half, late, gram)
    crossed_half = crossed(half, 1)
    share_rows, sum_rows = ((subs + 1) * ncf, columns), ((8, columns), F32)
    z_local, shares_rounded, shares, z_coarse, sums = stage(
        bind(coarse_load), [(faces, F32), (share_rows, BF16), (share_rows, F32), (share_rows, F32), sum_rows],
        load, outer, inner, near, far, weight, message, turned_high, turned_low, half, crossed_half, inverse, coarse, gram,
        scratch=[pltpu.VMEM((local_rows, columns), F32), pltpu.VMEM((nco, columns), BF16)],
    )
    outer, near, far, sums = stage(
        bind(schur_outer), outside_faces + [sum_rows], z_local, schur, basis_high, basis_low, z_coarse, sums
    )
    inner, energies = stage(
        bind(schur_inner), inside_faces + [((subs - 1, columns), F32)], z_local, schur, basis_high, basis_low, z_coarse
    )
    half = gather_half(shares_rounded, early[:1], inner)
    far, near = far_block(far), crossed(near, 1)
    operands = outer, inner, near, far, weight, message, neumann
    outer, near, far = stage(bind(image_outer), outside_faces, *operands)
    image, inner = stage(bind(image_inner), [(own, F32)] + inside_faces, after(operands[0], far), *operands[1:])
    half = gather_half(half, early[1:], far)
    far, near = far_block(far), crossed(near, 1)
    half = gather_half(half, late, near, far, inner)
    crossed_half = crossed(half, 1)
    outer = after(outer, half)
    y_local, product, quadratic, base = stage(
        bind(schur_image), products, image, outer, inner, near, far, weight, message, schur, turned_high, turned_low
    )
    sums, y_coarse = stage(
        bind(coarse_image), [((4, columns), F32), (share_rows, F32)],
        half, crossed_half, inverse, message, shares, base, gram, quadratic, sums, energies,
        scratch=[pltpu.VMEM((nco, columns), F32)],
    )
    z, y, part, back = stage(
        bind(complete), [(own, F32), (own, F32), (own, F32), ((nf, columns), BF16)],
        z_local, z_coarse, y_local, y_coarse, rows, basis_high, basis_low, product,
    )
    for k, bit in enumerate(early[:1] + steps[-1:] + early[1:] + late):
        sums = sums + after(crossed(sums, bit), y)
        if k == 0:
            back = shifted(after(back, sums), -1)
    return stage(
        bind(combine), [(own, F32), (own, F32)], sums, load, z, y, image, part, back,
        scratch=[pltpu.VMEM(own, F32)] * 2 + semaphores(2 * subs), outputs=pltpu.HBM,
    )


def solution(mesh):
    specs = P(("parts", AXIS), None)
    return jax.shard_map(shards, mesh=mesh, in_specs=(specs,) * 6, out_specs=(specs, specs), check_vma=False)
```

```python
import functools

import jax
import jax.numpy as jnp
from jax import lax
from jax.experimental import pallas as pl
from jax.experimental.pallas import tpu as pltpu
from jax.sharding import PartitionSpec as P

AXIS = "sub"
BF16 = jnp.bfloat16
F32 = jnp.float32
LANES = 128
VMEM_BYTES = 20 * 2**20


def shifted(block, distance):
    n = lax.axis_size(AXIS)
    return lax.ppermute(block, AXIS, [((i - distance) % n, i) for i in range(n)])


def crossed(block, bit):
    return lax.ppermute(block, AXIS, [(i, i ^ bit) for i in range(lax.axis_size(AXIS))])


def far_block(block):
    n = lax.axis_size(AXIS)
    return lax.ppermute(block, AXIS, [(i, (i + (1 if i % 2 else -1)) % n) for i in range(n)])


def bits():
    order = [1 << k for k in reversed(range(lax.axis_size(AXIS).bit_length() - 1))]
    return order[:-3] + order[-2:-1] + order[-3:-2] + order[-1:]


def after(value, *others):
    return lax.optimization_barrier((value, others))[0]


def gather_half(block, steps, *others):
    for bit in steps:
        block = jnp.concatenate([block, after(crossed(block, bit), *others)], axis=0)
    return block


def half_order():
    order = [0]
    for bit in bits()[:-1]:
        order += [place ^ bit for place in order]
    return order


def dot(a, b):
    return jnp.dot(a, b, preferred_element_type=F32)


def dot_nt(a, b):
    return lax.dot_general(a, b, (((1,), (1,)), ((), ())), preferred_element_type=F32)


def dot_tn(a, b):
    return lax.dot_general(a, b, (((0,), (0,)), ((), ())), preferred_element_type=F32)


def split(x):
    high = x.astype(BF16)
    return high, (x - high.astype(F32)).astype(BF16)


def split_dot(a, b, contract=dot):
    high, low = split(b)
    if isinstance(a, tuple):
        return contract(a[0], high) + contract(a[0], low) + contract(a[1], high)
    return contract(a, high) + contract(a, low)


def column_sum(x):
    return jnp.sum(x, axis=0, keepdims=True)


def rows_of(ref, index, count):
    return ref[index * count : (index + 1) * count]


def column_of(row):
    return jnp.broadcast_to(row, (8, row.shape[1])).T[:, :1]


def parts_of(row):
    high = row.astype(BF16).astype(F32)
    middle = (row - high).astype(BF16).astype(F32)
    return high, middle, row - high - middle


class Halo:
    def __init__(self, nf, ncf, nco, columns):
        self.nf, self.ncf, self.columns = nf, ncf, columns
        self.folds = nf // columns
        self.at_inverse = nf + ncf * self.folds
        self.at_weight = self.at_inverse + ncf * (nco // columns)
        self.weight_count = -(-3 * self.folds // 16) * 16
        self.height = self.at_weight + self.weight_count

    def unfolded(self, message, start, stop):
        return jnp.concatenate([message[k : k + self.ncf] for k in range(start, stop, self.ncf)], axis=1)

    def fold(self, message, block, start):
        ncf, columns = self.ncf, self.columns
        for k in range(block.shape[1] // columns):
            message[start + k * ncf : start + (k + 1) * ncf] = block[:, k * columns : (k + 1) * columns]

    def rows(self, message):
        return self.unfolded(message, self.nf, self.at_inverse)

    def inverse(self, message):
        return self.unfolded(message, self.at_inverse, self.at_weight)

    def weight(self, message):
        got = message[self.at_weight : self.height].astype(F32)
        f = self.folds
        row = [sum(got[k * f + i : k * f + i + 1] for k in range(3)) for i in range(f)]
        return jnp.concatenate([column_of(piece) for piece in row], axis=0)


def all_rows(halo, message, rows):
    ncf = halo.ncf
    return [halo.rows(message)] + [rows_of(rows, j, ncf) for j in range(rows.shape[0] // ncf)]


def is_odd():
    return lax.rem(lax.axis_index(AXIS), 2) == 1


def send(first, second, near, far):
    first, second, odd = first.astype(BF16), second.astype(BF16), is_odd()
    near[...] = jnp.where(odd, first, second)
    far[...] = jnp.where(odd, second, first)


def received(near, far):
    near, far, odd = near[...].astype(F32), far[...].astype(F32), is_odd()
    return jnp.where(odd, far, near), jnp.where(odd, near, far)


def all_weights(halo, message, weight):
    return [halo.weight(message)] + [column_of(weight[j : j + 1]) for j in range(weight.shape[0])]


def stage(kernel, shapes, *operands, scratch=(), fetched=0, outputs=pltpu.VMEM):
    out = [jax.ShapeDtypeStruct(shape, dtype) for shape, dtype in shapes]
    params = pltpu.CompilerParams(vmem_limit_bytes=VMEM_BYTES)
    spaces = [pltpu.HBM] * fetched + [pltpu.VMEM] * (len(operands) - fetched)
    call = pl.pallas_call(
        kernel,
        out_shape=out,
        out_specs=[pl.BlockSpec(memory_space=outputs)] * len(out),
        in_specs=[pl.BlockSpec(memory_space=space) for space in spaces],
        scratch_shapes=list(scratch),
        compiler_params=params,
        name=kernel.func.__name__,
    )
    return call(*operands)


def prepare(
    halo, load, rows, weight, inverse, load_here, rows_here, weight_here, inverse_here, coarse_rounded, coarse, done
):
    ncf, nf = halo.ncf, halo.nf
    subs = load.shape[0] // nf
    copies = [pltpu.make_async_copy(rows, rows_here, done.at[subs])]
    copies += [
        pltpu.make_async_copy(rows_of(load.at, j, nf), rows_of(load_here.at, j, nf), done.at[j]) for j in range(subs)
    ]
    copies.append(pltpu.make_async_copy(weight, weight_here, done.at[subs + 1]))
    copies.append(pltpu.make_async_copy(inverse, inverse_here, done.at[subs + 2]))
    for copy in copies:
        copy.start()
    copies[0].wait()
    for j in range(subs):
        copies[1 + j].wait()
        coarse[j * ncf : (j + 1) * ncf] = dot(rows_of(rows_here, j, ncf), rows_of(load_here, j, nf).astype(BF16))
    coarse_rounded[...] = coarse[...].astype(BF16)
    copies[-2].wait()
    copies[-1].wait()


def halo_message(halo, load, weight, rows, inverse, message, pieces):
    ncf, nf, columns, folds = halo.ncf, halo.nf, halo.columns, halo.folds
    last = weight[weight.shape[0] - 1 :]
    message[:nf] = ((1.0 - column_of(last)) * load[load.shape[0] - nf :]).astype(BF16)
    halo.fold(message, rows[rows.shape[0] - ncf :], nf)
    halo.fold(message, inverse[inverse.shape[0] - ncf :], halo.at_inverse)
    pieces[...] = jnp.zeros_like(pieces)
    for k, values in enumerate(parts_of(last)):
        for i in range(folds):
            pieces[k * folds + i : k * folds + i + 1] = values[:, i * columns : (i + 1) * columns]
    message[halo.at_weight :] = pieces[...].astype(BF16)


def fetch(halo, neumann, schur, neumann_here, schur_here, done):
    pairs = ((neumann, neumann_here), (schur, schur_here))
    copies = [pltpu.make_async_copy(source, here, done.at[k]) for k, (source, here) in enumerate(pairs)]
    for copy in copies:
        copy.start()
    for copy in copies:
        copy.wait()


def neumann_half(neumann, left, right, j, half, nf):
    start = (2 * j + half) * nf
    return dot(neumann[start : start + nf], jnp.concatenate([left[j](), right[j]()], axis=0))


def neumann_outer(left, right, neumann, outer, near, far):
    nf, last = near.shape[0], len(left) - 1
    first = neumann_half(neumann, left, right, 0, 0, nf)
    second = neumann_half(neumann, left, right, last, 1, nf)
    outer[:nf], outer[nf:] = first, second
    send(first, second, near, far)


def neumann_inner(left, right, weights, neumann, inner, nf):
    for j in range(1, len(left)):
        before = neumann_half(neumann, left, right, j - 1, 1, nf)
        after_it = neumann_half(neumann, left, right, j, 0, nf)
        inner[(j - 1) * nf : j * nf] = weights(j) * before + (1.0 - weights(j)) * after_it


def face_of(outer, inner, e, nf):
    if e == 0:
        return outer[:nf]
    if e * nf > inner.shape[0]:
        return outer[nf:]
    return inner[(e - 1) * nf : e * nf]


def load_sides(halo, load, weight, message):
    subs, nf = weight.shape
    own = lambda e: column_of(weight[e - 1 : e])
    left = [lambda: message[:nf]]
    left += [lambda j=j: ((1.0 - own(j)) * rows_of(load, j - 1, nf)).astype(BF16) for j in range(1, subs)]
    right = [lambda j=j: (own(j + 1) * rows_of(load, j, nf)).astype(BF16) for j in range(subs)]
    return left, right, own


def load_outer(halo, load, weight, message, neumann, outer, near, far):
    left, right, _ = load_sides(halo, load, weight, message)
    neumann_outer(left, right, neumann, outer, near, far)


def load_inner(halo, load, weight, message, neumann, inner):
    left, right, own = load_sides(halo, load, weight, message)
    neumann_inner(left, right, own, neumann, inner, halo.nf)


def image_sides(halo, outer, inner, near, far, weight, message):
    subs, nf = weight.shape
    own = lambda e: column_of(weight[e - 1 : e]) if e else halo.weight(message)
    from_next, from_previous = received(near, far)
    face = lambda e: face_of(outer, inner, e, nf) + (from_previous if e == 0 else from_next if e == subs else 0.0)
    left = [lambda j=j: ((1.0 - own(j)) * face(j)).astype(BF16) for j in range(subs)]
    right = [lambda j=j: (own(j + 1) * face(j + 1)).astype(BF16) for j in range(subs)]
    return left, right, own, face


def image_outer(halo, outer_in, inner_in, near_in, far_in, weight, message, neumann, outer, near, far):
    left, right, _, _ = image_sides(halo, outer_in, inner_in, near_in, far_in, weight, message)
    neumann_outer(left, right, neumann, outer, near, far)


def image_inner(halo, outer_in, inner_in, near_in, far_in, weight, message, neumann, image, inner):
    nf = halo.nf
    left, right, own, face = image_sides(halo, outer_in, inner_in, near_in, far_in, weight, message)
    for e in range(1, len(left) + 1):
        image[(e - 1) * nf : e * nf] = face(e)
    neumann_inner(left, right, own, neumann, inner, nf)


def static_basis(halo, schur, message, rows, basis_high, basis_low, turned_high, turned_low, gram):
    ncf, nf = halo.ncf, halo.nf
    blocks = all_rows(halo, message, rows)
    gram[...] = jnp.zeros_like(gram)
    for j in range(len(blocks) - 1):
        matrix, pair = rows_of(schur, j, 2 * nf), blocks[j : j + 2]
        basis = jnp.concatenate([dot_nt(matrix[:, k * nf : (k + 1) * nf], pair[k]) for k in range(2)], axis=1)
        long, wide = slice(2 * j * nf, 2 * (j + 1) * nf), slice(2 * j * ncf, 2 * (j + 1) * ncf)
        basis_high[long], basis_low[long] = split(basis)
        turned = split(basis.T)
        turned_high[wide], turned_low[wide] = turned
        for k in range(2):
            half = slice(k * nf, (k + 1) * nf)
            gram[wide, k * ncf : (k + 1) * ncf] = dot_nt(turned[0][:, half], pair[k]) + dot_nt(turned[1][:, half], pair[k])


def complete_local(halo, outer, inner, near, far, weight, message, local):
    subs, nf = weight.shape
    weights = all_weights(halo, message, weight)
    from_next, from_previous = received(near, far)
    local[:nf] = (1.0 - weights[0]) * outer[:nf] + weights[0] * from_previous
    for e in range(1, subs):
        local[e * nf : (e + 1) * nf] = face_of(outer, inner, e, nf)
    local[subs * nf :] = weights[subs] * outer[nf:] + (1.0 - weights[subs]) * from_next


def project(halo, local, turned_high, turned_low, base):
    ncf, nf = halo.ncf, halo.nf
    for j in range(base.shape[0] // (2 * ncf)):
        here = slice(2 * j * ncf, 2 * (j + 1) * ncf)
        base[here] = split_dot((turned_high[here], turned_low[here]), local[j * nf : (j + 2) * nf])


def schur_faces(halo, local, schur):
    nf, columns = halo.nf, halo.columns
    faces, energy = [], 0.0
    for j in range(schur.shape[0] // (2 * nf)):
        vector = local[j * nf : (j + 2) * nf]
        both = dot(rows_of(schur, j, 2 * nf), jnp.concatenate(split(vector), axis=1))
        result = both[:, :columns] + both[:, columns:]
        energy = energy + column_sum(vector * result)
        faces[j:] = [result[:nf] if j == 0 else faces[j] + result[:nf], result[nf:]]
    return faces, energy


def schur_half(halo, local, schur, j, half):
    nf, columns = halo.nf, halo.columns
    start = (2 * j + half) * nf
    both = dot(schur[start : start + nf], jnp.concatenate(split(local[j * nf : (j + 2) * nf]), axis=1))
    return both[:, :columns] + both[:, columns:]


def basis_half(halo, basis_high, basis_low, solution, j, half):
    ncf, nf = halo.ncf, halo.nf
    here = slice((2 * j + half) * nf, (2 * j + half + 1) * nf)
    return split_dot((basis_high[here], basis_low[here]), solution[j * ncf : (j + 2) * ncf])


def schur_outer(halo, local, schur, basis_high, basis_low, solution, sums_in, outer, near, far, sums):
    nf = halo.nf
    last = schur.shape[0] // (2 * nf) - 1
    energy = sums_in[1:2]
    for here, face, j, half in ((slice(0, nf), 0, 0, 0), (slice(nf, 2 * nf), last + 1, last, 1)):
        outer[here] = basis_half(halo, basis_high, basis_low, solution, j, half)
        result = schur_half(halo, local, schur, j, half)
        energy = energy + column_sum(local[face * nf : (face + 1) * nf] * result)
        outer[here] += result
    send(outer[:nf], outer[nf:], near, far)
    sums[0:1] = sums_in[0:1]
    sums[1:2] = energy


def schur_inner(halo, local, schur, basis_high, basis_low, solution, inner, energies):
    nf = halo.nf
    for j in range(1, schur.shape[0] // (2 * nf)):
        here = slice((j - 1) * nf, j * nf)
        inner[here] = basis_half(halo, basis_high, basis_low, solution, j - 1, 1)
        inner[here] += basis_half(halo, basis_high, basis_low, solution, j, 0)
        result = schur_half(halo, local, schur, j - 1, 1)
        result = result + schur_half(halo, local, schur, j, 0)
        energies[j - 1 : j] = column_sum(local[j * nf : (j + 1) * nf] * result)
        inner[here] += result


def schur_image(
    halo, image, outer, inner, near, far, weight, message, schur, turned_high, turned_low, local, product, quadratic, base
):
    nf = halo.nf
    complete_local(halo, outer, inner, near, far, weight, message, local)
    project(halo, local, turned_high, turned_low, base)
    faces, energy = schur_faces(halo, local, schur)
    for e, face in enumerate(faces):
        product[e * nf : (e + 1) * nf] = face
    quadratic[0:1] = energy
    quadratic[1:2] = column_sum(image[...] * local[nf:])


def placed(half, crossed_half):
    me = lax.axis_index(AXIS)
    order = half_order()
    count = half.shape[0] // len(order)
    for flip, blocks in ((0, half), (1, crossed_half)):
        for k, place in enumerate(order):
            yield me ^ (place ^ flip), blocks, k * count, (k + 1) * count


def coarse_shares(ncf, results):
    shares = [results[0][:ncf]]
    for before, after in zip(results[:-1], results[1:]):
        shares.append(before[ncf:] + after[:ncf])
    return shares + [results[-1][ncf:]]


def coarse_products(ncf, x, base, gram):
    results, energy = [], 0.0
    for j in range(len(x) - 1):
        here = slice(2 * j * ncf, 2 * (j + 1) * ncf)
        pair = jnp.concatenate([x[j], x[j + 1]], axis=0)
        change = split_dot(split(gram[here, : 2 * ncf]), pair)
        energy = energy + column_sum(pair * (2.0 * base[here] + change))
        results.append(base[here] + change)
    return results, energy


def add_basis(nf, x, basis_high, basis_low, faces):
    faces = list(faces)
    for j in range(len(x) - 1):
        here = slice(2 * j * nf, 2 * (j + 1) * nf)
        pair = jnp.concatenate([x[j], x[j + 1]], axis=0)
        change = split_dot((basis_high[here], basis_low[here]), pair)
        faces[j] = faces[j] + change[:nf]
        faces[j + 1] = faces[j + 1] + change[nf:]
    return faces


def coarse_load(
    halo, load, outer, inner, near, far, weight, message, turned_high, turned_low, half, crossed_half, inverse, coarse, gram,
    local, shares_rounded, shares, solution, sums, base, gathered,
):
    ncf, nf = halo.ncf, halo.nf
    subs = weight.shape[0]
    complete_local(halo, outer, inner, near, far, weight, message, local)
    project(halo, local, turned_high, turned_low, base)
    for place, blocks, start, stop in placed(half, crossed_half):
        gathered[pl.ds(pl.multiple_of(place * subs * ncf, subs * ncf), subs * ncf)] = blocks[start:stop]
    everything = gathered[...]
    own = dot(inverse[...], everything)
    x = [dot(halo.inverse(message), everything)] + [own[j * ncf : (j + 1) * ncf] for j in range(subs)]
    results, energy = coarse_products(ncf, x, base, gram)
    for e, share in enumerate(coarse_shares(ncf, results)):
        shares[e * ncf : (e + 1) * ncf] = share
        solution[e * ncf : (e + 1) * ncf] = x[e]
    shares_rounded[...] = shares[...].astype(BF16)
    sums[0:1] = column_sum(load[...] * local[nf:]) + column_sum(coarse[...] * own)
    sums[1:2] = energy


def coarse_image(
    halo, half, crossed_half, inverse, message, shares, base, gram, quadratic, sums_in, energies, sums, solution, gathered
):
    ncf = halo.ncf
    subs = inverse.shape[0] // ncf
    total = gathered.shape[0]
    for place, blocks, start, stop in placed(half, crossed_half):
        gathered[pl.ds(pl.multiple_of(place * subs * ncf, subs * ncf), subs * ncf)] = blocks[start + ncf : stop].astype(F32)
    for place, blocks, start, stop in placed(half, crossed_half):
        before = pl.multiple_of(lax.rem(place * subs * ncf + (total - ncf), total), ncf)
        gathered[pl.ds(before, ncf)] += blocks[start : start + ncf].astype(F32)
    everything = gathered[...]
    own = split_dot(inverse[...], everything)
    x = [split_dot(halo.inverse(message), everything)] + [own[j * ncf : (j + 1) * ncf] for j in range(subs)]
    _, energy = coarse_products(ncf, x, base, gram)
    for e in range(subs + 1):
        solution[e * ncf : (e + 1) * ncf] = x[e]
    sums[0:1] = sums_in[0:1]
    sums[1:2] = sums_in[1:2] + column_sum(energies[...])
    sums[2:3] = quadratic[1:2] + column_sum(shares[...] * solution[...])
    sums[3:4] = quadratic[0:1] + energy


def complete(
    halo, z_local, z_coarse, y_local, y_coarse, rows, basis_high, basis_low, product, z, y, part, back
):
    ncf, nf = halo.ncf, halo.nf
    subs = rows.shape[0] // ncf
    x = [rows_of(y_coarse, e, ncf) for e in range(subs + 1)]
    faces = add_basis(nf, x, basis_high, basis_low, [rows_of(product, e, nf) for e in range(subs + 1)])
    for e in range(1, subs + 1):
        part[(e - 1) * nf : e * nf] = faces[e]
    back[...] = faces[0].astype(BF16)
    for j in range(subs):
        here, beside = slice(j * nf, (j + 1) * nf), slice((j + 1) * nf, (j + 2) * nf)
        for local, coarse, whole in ((z_local, z_coarse, z), (y_local, y_coarse, y)):
            whole[here] = local[beside] + split_dot(rows_of(rows, j, ncf), rows_of(coarse, j + 1, ncf), dot_tn)


def combine(halo, sums, load, z, y, image, part, from_next, solution, residual, solution_here, residual_here, done):
    nf = halo.nf
    subs = load.shape[0] // nf
    a, b, c, d = (sums[k : k + 1] for k in range(4))
    step = a / b
    grow = step * (c / b)
    next_step = (grow - 1.0) / ((d - c * (c / b)) * (step / b))
    s = step + next_step * grow
    t = step * next_step
    copies = []

    def copy_out(here, source, target):
        copies.append(pltpu.make_async_copy(source.at[here], target.at[here], done.at[len(copies)]))
        copies[-1].start()

    for j in range(subs):
        here = slice(j * nf, (j + 1) * nf)
        solution_here[here] = s * z[here] - t * y[here]
        copy_out(pl.ds(j * nf, nf), solution_here, solution)
        last = part[here] + from_next[...].astype(F32) if j == subs - 1 else part[here]
        residual_here[here] = load[here] - s * image[here] + t * last
        copy_out(pl.ds(j * nf, nf), residual_here, residual)
    for copy in copies:
        copy.wait()


def shards(right_side, face_weight, schur, neumann, constraint, coarse_inverse):
    subs, nf = face_weight.shape
    ncf = constraint.shape[0] // subs
    nco = coarse_inverse.shape[1]
    columns = right_side.shape[1]
    halo = Halo(nf, ncf, nco, columns)
    bind = lambda kernel: functools.partial(kernel, halo)
    faces, own = ((subs + 1) * nf, columns), (subs * nf, columns)
    coarse_own, local_rows = (subs * ncf, columns), 2 * subs * ncf
    products = [(faces, F32), (faces, F32), ((8, columns), F32), ((local_rows, columns), F32)]
    semaphores = lambda count: [pltpu.SemaphoreType.DMA((count,))]
    described = lambda array: (array.shape, array.dtype)
    outside = lambda array: pltpu.with_memory_space_constraint(array, pltpu.HBM)
    steps = bits()
    early, late = steps[:-2], steps[-2:-1]

    load, rows, weight, inverse, coarse_rounded, coarse = stage(
        bind(prepare),
        [described(right_side), described(constraint), described(face_weight), described(coarse_inverse)]
        + [(coarse_own, BF16), (coarse_own, F32)],
        *map(outside, (right_side, constraint, face_weight, coarse_inverse)), scratch=semaphores(subs + 3), fetched=4,
    )
    (message,) = stage(
        bind(halo_message), [((halo.height, columns), BF16)], load, weight, rows, inverse,
        scratch=[pltpu.VMEM((halo.weight_count, columns), F32)],
    )
    tied = after(tuple(map(outside, (neumann, schur))), message)
    neumann, schur = stage(
        bind(fetch), [described(array) for array in tied], *tied, scratch=semaphores(2), fetched=2
    )
    message = shifted(message, 1)
    half = gather_half(coarse_rounded, early[:1], neumann)
    outside_faces = [((2 * nf, columns), F32)] + 2 * [((nf, columns), BF16)]
    inside_faces = [(((subs - 1) * nf, columns), F32)]
    outer, near, far = stage(bind(load_outer), outside_faces, load, weight, message, neumann)
    (inner,) = stage(bind(load_inner), inside_faces, load, weight, after(message, far), neumann)
    half = gather_half(half, early[1:], far)
    far, near = far_block(far), crossed(near, 1)
    long, wide = ((2 * subs * nf, 2 * ncf), BF16), ((local_rows, 2 * nf), BF16)
    basis_high, basis_low, turned_high, turned_low, gram = stage(
        bind(static_basis), [long, long, wide, wide, ((local_rows, LANES), F32)], schur, after(message, inner), rows
    )
    half = gather_half(half, late, gram)
    crossed_half = crossed(half, 1)
    share_rows, sum_rows = ((subs + 1) * ncf, columns), ((8, columns), F32)
    z_local, shares_rounded, shares, z_coarse, sums = stage(
        bind(coarse_load), [(faces, F32), (share_rows, BF16), (share_rows, F32), (share_rows, F32), sum_rows],
        load, outer, inner, near, far, weight, message, turned_high, turned_low, half, crossed_half, inverse, coarse, gram,
        scratch=[pltpu.VMEM((local_rows, columns), F32), pltpu.VMEM((nco, columns), BF16)],
    )
    outer, near, far, sums = stage(
        bind(schur_outer), outside_faces + [sum_rows], z_local, schur, basis_high, basis_low, z_coarse, sums
    )
    half = gather_half(shares_rounded, early[:1], far)
    inner, energies = stage(
        bind(schur_inner), inside_faces + [((subs - 1, columns), F32)], after(z_local, half), schur, basis_high, basis_low, z_coarse
    )
    far, near = far_block(far), crossed(after(near, half), 1)
    operands = outer, inner, near, far, weight, message, neumann
    outer, near, far = stage(bind(image_outer), outside_faces, *operands)
    image, inner = stage(bind(image_inner), [(own, F32)] + inside_faces, after(operands[0], far), *operands[1:])
    half = gather_half(half, early[1:], far)
    far, near = far_block(far), crossed(near, 1)
    half = gather_half(half, late, near, far, inner)
    crossed_half = crossed(half, 1)
    outer = after(outer, half)
    y_local, product, quadratic, base = stage(
        bind(schur_image), products, image, outer, inner, near, far, weight, message, schur, turned_high, turned_low
    )
    sums, y_coarse = stage(
        bind(coarse_image), [((4, columns), F32), (share_rows, F32)],
        half, crossed_half, inverse, message, shares, base, gram, quadratic, sums, energies,
        scratch=[pltpu.VMEM((nco, columns), F32)],
    )
    z, y, part, back = stage(
        bind(complete), [(own, F32), (own, F32), (own, F32), ((nf, columns), BF16)],
        z_local, z_coarse, y_local, y_coarse, rows, basis_high, basis_low, product,
    )
    for k, bit in enumerate(early + steps[-1:] + late):
        sums = sums + after(crossed(sums, bit), y)
        if k == len(early) - 1:
            back = shifted(after(back, sums), -1)
    return stage(
        bind(combine), [(own, F32), (own, F32)], sums, load, z, y, image, part, back,
        scratch=[pltpu.VMEM(own, F32)] * 2 + semaphores(2 * subs), outputs=pltpu.HBM,
    )


def solution(mesh):
    specs = P(("parts", AXIS), None)
    return jax.shard_map(shards, mesh=mesh, in_specs=(specs,) * 6, out_specs=(specs, specs), check_vma=False)
```

```python
import functools

import jax
import jax.numpy as jnp
from jax import lax
from jax.experimental import pallas as pl
from jax.experimental.pallas import tpu as pltpu
from jax.sharding import PartitionSpec as P

AXIS = "sub"
BF16 = jnp.bfloat16
F32 = jnp.float32
LANES = 128
VMEM_BYTES = 20 * 2**20


def shifted(block, distance):
    n = lax.axis_size(AXIS)
    return lax.ppermute(block, AXIS, [((i - distance) % n, i) for i in range(n)])


def crossed(block, bit):
    return lax.ppermute(block, AXIS, [(i, i ^ bit) for i in range(lax.axis_size(AXIS))])


def far_block(block):
    n = lax.axis_size(AXIS)
    return lax.ppermute(block, AXIS, [(i, (i + (1 if i % 2 else -1)) % n) for i in range(n)])


def bits():
    order = [1 << k for k in reversed(range(lax.axis_size(AXIS).bit_length() - 1))]
    return order[:-3] + order[-2:-1] + order[-3:-2] + order[-1:]


def after(value, *others):
    return lax.optimization_barrier((value, others))[0]


def gather_half(block, steps, *others):
    for bit in steps:
        block = jnp.concatenate([block, after(crossed(block, bit), *others)], axis=0)
    return block


def half_order():
    order = [0]
    for bit in bits()[:-1]:
        order += [place ^ bit for place in order]
    return order


def dot(a, b):
    return jnp.dot(a, b, preferred_element_type=F32)


def dot_nt(a, b):
    return lax.dot_general(a, b, (((1,), (1,)), ((), ())), preferred_element_type=F32)


def dot_tn(a, b):
    return lax.dot_general(a, b, (((0,), (0,)), ((), ())), preferred_element_type=F32)


def split(x):
    high = x.astype(BF16)
    return high, (x - high.astype(F32)).astype(BF16)


def split_dot(a, b, contract=dot):
    high, low = split(b)
    if isinstance(a, tuple):
        return contract(a[0], high) + contract(a[0], low) + contract(a[1], high)
    return contract(a, high) + contract(a, low)


def column_sum(x):
    return jnp.sum(x, axis=0, keepdims=True)


def rows_of(ref, index, count):
    return ref[index * count : (index + 1) * count]


def column_of(row):
    return jnp.broadcast_to(row, (8, row.shape[1])).T[:, :1]


def parts_of(row):
    high = row.astype(BF16).astype(F32)
    middle = (row - high).astype(BF16).astype(F32)
    return high, middle, row - high - middle


class Halo:
    def __init__(self, nf, ncf, nco, columns):
        self.nf, self.ncf, self.columns = nf, ncf, columns
        self.folds = nf // columns
        self.at_inverse = nf + ncf * self.folds
        self.at_weight = self.at_inverse + ncf * (nco // columns)
        self.weight_count = -(-3 * self.folds // 16) * 16
        self.height = self.at_weight + self.weight_count

    def unfolded(self, message, start, stop):
        return jnp.concatenate([message[k : k + self.ncf] for k in range(start, stop, self.ncf)], axis=1)

    def fold(self, message, block, start):
        ncf, columns = self.ncf, self.columns
        for k in range(block.shape[1] // columns):
            message[start + k * ncf : start + (k + 1) * ncf] = block[:, k * columns : (k + 1) * columns]

    def rows(self, message):
        return self.unfolded(message, self.nf, self.at_inverse)

    def inverse(self, message):
        return self.unfolded(message, self.at_inverse, self.at_weight)

    def weight(self, message):
        got = message[self.at_weight : self.height].astype(F32)
        f = self.folds
        row = [sum(got[k * f + i : k * f + i + 1] for k in range(3)) for i in range(f)]
        return jnp.concatenate([column_of(piece) for piece in row], axis=0)


def all_rows(halo, message, rows):
    ncf = halo.ncf
    return [halo.rows(message)] + [rows_of(rows, j, ncf) for j in range(rows.shape[0] // ncf)]


def is_odd():
    return lax.rem(lax.axis_index(AXIS), 2) == 1


def send(first, second, near, far):
    first, second, odd = first.astype(BF16), second.astype(BF16), is_odd()
    near[...] = jnp.where(odd, first, second)
    far[...] = jnp.where(odd, second, first)


def received(near, far):
    near, far, odd = near[...].astype(F32), far[...].astype(F32), is_odd()
    return jnp.where(odd, far, near), jnp.where(odd, near, far)


def all_weights(halo, message, weight):
    return [halo.weight(message)] + [column_of(weight[j : j + 1]) for j in range(weight.shape[0])]


def stage(kernel, shapes, *operands, scratch=(), fetched=0, outputs=pltpu.VMEM):
    out = [jax.ShapeDtypeStruct(shape, dtype) for shape, dtype in shapes]
    params = pltpu.CompilerParams(vmem_limit_bytes=VMEM_BYTES)
    spaces = [pltpu.HBM] * fetched + [pltpu.VMEM] * (len(operands) - fetched)
    call = pl.pallas_call(
        kernel,
        out_shape=out,
        out_specs=[pl.BlockSpec(memory_space=outputs)] * len(out),
        in_specs=[pl.BlockSpec(memory_space=space) for space in spaces],
        scratch_shapes=list(scratch),
        compiler_params=params,
        name=kernel.func.__name__,
    )
    return call(*operands)


def prepare(
    halo, load, rows, weight, inverse, load_here, rows_here, weight_here, inverse_here, coarse_rounded, coarse, done
):
    ncf, nf = halo.ncf, halo.nf
    subs = load.shape[0] // nf
    copies = [pltpu.make_async_copy(rows, rows_here, done.at[subs])]
    copies += [
        pltpu.make_async_copy(rows_of(load.at, j, nf), rows_of(load_here.at, j, nf), done.at[j]) for j in range(subs)
    ]
    copies.append(pltpu.make_async_copy(weight, weight_here, done.at[subs + 1]))
    copies.append(pltpu.make_async_copy(inverse, inverse_here, done.at[subs + 2]))
    for copy in copies:
        copy.start()
    copies[0].wait()
    for j in range(subs):
        copies[1 + j].wait()
        coarse[j * ncf : (j + 1) * ncf] = dot(rows_of(rows_here, j, ncf), rows_of(load_here, j, nf).astype(BF16))
    coarse_rounded[...] = coarse[...].astype(BF16)
    copies[-2].wait()
    copies[-1].wait()


def halo_message(halo, load, weight, rows, inverse, message, pieces):
    ncf, nf, columns, folds = halo.ncf, halo.nf, halo.columns, halo.folds
    last = weight[weight.shape[0] - 1 :]
    message[:nf] = ((1.0 - column_of(last)) * load[load.shape[0] - nf :]).astype(BF16)
    halo.fold(message, rows[rows.shape[0] - ncf :], nf)
    halo.fold(message, inverse[inverse.shape[0] - ncf :], halo.at_inverse)
    pieces[...] = jnp.zeros_like(pieces)
    for k, values in enumerate(parts_of(last)):
        for i in range(folds):
            pieces[k * folds + i : k * folds + i + 1] = values[:, i * columns : (i + 1) * columns]
    message[halo.at_weight :] = pieces[...].astype(BF16)


def fetch(halo, neumann, schur, neumann_here, schur_here, done):
    pairs = ((neumann, neumann_here), (schur, schur_here))
    copies = [pltpu.make_async_copy(source, here, done.at[k]) for k, (source, here) in enumerate(pairs)]
    for copy in copies:
        copy.start()
    for copy in copies:
        copy.wait()


def neumann_half(neumann, left, right, j, half, nf):
    start = (2 * j + half) * nf
    return dot(neumann[start : start + nf], jnp.concatenate([left[j](), right[j]()], axis=0))


def neumann_outer(left, right, neumann, outer, near, far):
    nf, last = near.shape[0], len(left) - 1
    first = neumann_half(neumann, left, right, 0, 0, nf)
    second = neumann_half(neumann, left, right, last, 1, nf)
    outer[:nf], outer[nf:] = first, second
    send(first, second, near, far)


def neumann_inner(left, right, weights, neumann, inner, nf):
    for j in range(1, len(left)):
        before = neumann_half(neumann, left, right, j - 1, 1, nf)
        after_it = neumann_half(neumann, left, right, j, 0, nf)
        inner[(j - 1) * nf : j * nf] = weights(j) * before + (1.0 - weights(j)) * after_it


def face_of(outer, inner, e, nf):
    if e == 0:
        return outer[:nf]
    if e * nf > inner.shape[0]:
        return outer[nf:]
    return inner[(e - 1) * nf : e * nf]


def load_sides(halo, load, weight, message):
    subs, nf = weight.shape
    own = lambda e: column_of(weight[e - 1 : e])
    left = [lambda: message[:nf]]
    left += [lambda j=j: ((1.0 - own(j)) * rows_of(load, j - 1, nf)).astype(BF16) for j in range(1, subs)]
    right = [lambda j=j: (own(j + 1) * rows_of(load, j, nf)).astype(BF16) for j in range(subs)]
    return left, right, own


def load_outer(halo, load, weight, message, neumann, outer, near, far):
    left, right, _ = load_sides(halo, load, weight, message)
    neumann_outer(left, right, neumann, outer, near, far)


def load_inner(halo, load, weight, message, neumann, inner):
    left, right, own = load_sides(halo, load, weight, message)
    neumann_inner(left, right, own, neumann, inner, halo.nf)


def image_sides(halo, outer, inner, near, far, weight, message):
    subs, nf = weight.shape
    own = lambda e: column_of(weight[e - 1 : e]) if e else halo.weight(message)
    from_next, from_previous = received(near, far)
    face = lambda e: face_of(outer, inner, e, nf) + (from_previous if e == 0 else from_next if e == subs else 0.0)
    left = [lambda j=j: ((1.0 - own(j)) * face(j)).astype(BF16) for j in range(subs)]
    right = [lambda j=j: (own(j + 1) * face(j + 1)).astype(BF16) for j in range(subs)]
    return left, right, own, face


def image_outer(halo, outer_in, inner_in, near_in, far_in, weight, message, neumann, outer, near, far):
    left, right, _, _ = image_sides(halo, outer_in, inner_in, near_in, far_in, weight, message)
    neumann_outer(left, right, neumann, outer, near, far)


def image_inner(halo, outer_in, inner_in, near_in, far_in, weight, message, neumann, image, inner):
    nf = halo.nf
    left, right, own, face = image_sides(halo, outer_in, inner_in, near_in, far_in, weight, message)
    for e in range(1, len(left) + 1):
        image[(e - 1) * nf : e * nf] = face(e)
    neumann_inner(left, right, own, neumann, inner, nf)


def static_basis(halo, schur, message, rows, basis_high, basis_low, turned_high, turned_low, gram):
    ncf, nf = halo.ncf, halo.nf
    blocks = all_rows(halo, message, rows)
    gram[...] = jnp.zeros_like(gram)
    for j in range(len(blocks) - 1):
        matrix, pair = rows_of(schur, j, 2 * nf), blocks[j : j + 2]
        basis = jnp.concatenate([dot_nt(matrix[:, k * nf : (k + 1) * nf], pair[k]) for k in range(2)], axis=1)
        long, wide = slice(2 * j * nf, 2 * (j + 1) * nf), slice(2 * j * ncf, 2 * (j + 1) * ncf)
        basis_high[long], basis_low[long] = split(basis)
        turned = split(basis.T)
        turned_high[wide], turned_low[wide] = turned
        for k in range(2):
            half = slice(k * nf, (k + 1) * nf)
            gram[wide, k * ncf : (k + 1) * ncf] = dot_nt(turned[0][:, half], pair[k]) + dot_nt(turned[1][:, half], pair[k])


def complete_local(halo, outer, inner, near, far, weight, message, local):
    subs, nf = weight.shape
    weights = all_weights(halo, message, weight)
    from_next, from_previous = received(near, far)
    local[:nf] = (1.0 - weights[0]) * outer[:nf] + weights[0] * from_previous
    for e in range(1, subs):
        local[e * nf : (e + 1) * nf] = face_of(outer, inner, e, nf)
    local[subs * nf :] = weights[subs] * outer[nf:] + (1.0 - weights[subs]) * from_next


def project(halo, local, turned_high, turned_low, base):
    ncf, nf = halo.ncf, halo.nf
    for j in range(base.shape[0] // (2 * ncf)):
        here = slice(2 * j * ncf, 2 * (j + 1) * ncf)
        base[here] = split_dot((turned_high[here], turned_low[here]), local[j * nf : (j + 2) * nf])


def schur_faces(halo, local, schur):
    nf, columns = halo.nf, halo.columns
    faces, energy = [], 0.0
    for j in range(schur.shape[0] // (2 * nf)):
        vector = local[j * nf : (j + 2) * nf]
        both = dot(rows_of(schur, j, 2 * nf), jnp.concatenate(split(vector), axis=1))
        result = both[:, :columns] + both[:, columns:]
        energy = energy + column_sum(vector * result)
        faces[j:] = [result[:nf] if j == 0 else faces[j] + result[:nf], result[nf:]]
    return faces, energy


def schur_half(halo, local, schur, j, half):
    nf, columns = halo.nf, halo.columns
    start = (2 * j + half) * nf
    both = dot(schur[start : start + nf], jnp.concatenate(split(local[j * nf : (j + 2) * nf]), axis=1))
    return both[:, :columns] + both[:, columns:]


def basis_half(halo, basis_high, basis_low, solution, j, half):
    ncf, nf = halo.ncf, halo.nf
    here = slice((2 * j + half) * nf, (2 * j + half + 1) * nf)
    return split_dot((basis_high[here], basis_low[here]), solution[j * ncf : (j + 2) * ncf])


def schur_outer(halo, local, schur, basis_high, basis_low, solution, sums_in, outer, near, far, sums):
    nf = halo.nf
    last = schur.shape[0] // (2 * nf) - 1
    energy = sums_in[1:2]
    for here, face, j, half in ((slice(0, nf), 0, 0, 0), (slice(nf, 2 * nf), last + 1, last, 1)):
        outer[here] = basis_half(halo, basis_high, basis_low, solution, j, half)
        result = schur_half(halo, local, schur, j, half)
        energy = energy + column_sum(local[face * nf : (face + 1) * nf] * result)
        outer[here] += result
    send(outer[:nf], outer[nf:], near, far)
    sums[0:1] = sums_in[0:1]
    sums[1:2] = energy


def schur_inner(halo, local, schur, basis_high, basis_low, solution, inner, energies):
    nf = halo.nf
    for j in range(1, schur.shape[0] // (2 * nf)):
        here = slice((j - 1) * nf, j * nf)
        inner[here] = basis_half(halo, basis_high, basis_low, solution, j - 1, 1)
        inner[here] += basis_half(halo, basis_high, basis_low, solution, j, 0)
        result = schur_half(halo, local, schur, j - 1, 1)
        result = result + schur_half(halo, local, schur, j, 0)
        energies[j - 1 : j] = column_sum(local[j * nf : (j + 1) * nf] * result)
        inner[here] += result


def schur_image(
    halo, image, outer, inner, near, far, weight, message, schur, turned_high, turned_low, local, product, quadratic, base
):
    nf = halo.nf
    complete_local(halo, outer, inner, near, far, weight, message, local)
    project(halo, local, turned_high, turned_low, base)
    faces, energy = schur_faces(halo, local, schur)
    for e, face in enumerate(faces):
        product[e * nf : (e + 1) * nf] = face
    quadratic[0:1] = energy
    quadratic[1:2] = column_sum(image[...] * local[nf:])


def placed(half, crossed_half):
    me = lax.axis_index(AXIS)
    order = half_order()
    count = half.shape[0] // len(order)
    for flip, blocks in ((0, half), (1, crossed_half)):
        for k, place in enumerate(order):
            yield me ^ (place ^ flip), blocks, k * count, (k + 1) * count


def coarse_shares(ncf, results):
    shares = [results[0][:ncf]]
    for before, after in zip(results[:-1], results[1:]):
        shares.append(before[ncf:] + after[:ncf])
    return shares + [results[-1][ncf:]]


def coarse_products(ncf, x, base, gram):
    results, energy = [], 0.0
    for j in range(len(x) - 1):
        here = slice(2 * j * ncf, 2 * (j + 1) * ncf)
        pair = jnp.concatenate([x[j], x[j + 1]], axis=0)
        change = split_dot(split(gram[here, : 2 * ncf]), pair)
        energy = energy + column_sum(pair * (2.0 * base[here] + change))
        results.append(base[here] + change)
    return results, energy


def add_basis(nf, x, basis_high, basis_low, faces):
    faces = list(faces)
    for j in range(len(x) - 1):
        here = slice(2 * j * nf, 2 * (j + 1) * nf)
        pair = jnp.concatenate([x[j], x[j + 1]], axis=0)
        change = split_dot((basis_high[here], basis_low[here]), pair)
        faces[j] = faces[j] + change[:nf]
        faces[j + 1] = faces[j + 1] + change[nf:]
    return faces


def coarse_load(
    halo, load, outer, inner, near, far, weight, message, turned_high, turned_low, half, crossed_half, inverse, coarse, gram,
    local, shares_rounded, shares, solution, sums, base, gathered,
):
    ncf, nf = halo.ncf, halo.nf
    subs = weight.shape[0]
    complete_local(halo, outer, inner, near, far, weight, message, local)
    project(halo, local, turned_high, turned_low, base)
    for place, blocks, start, stop in placed(half, crossed_half):
        gathered[pl.ds(pl.multiple_of(place * subs * ncf, subs * ncf), subs * ncf)] = blocks[start:stop]
    everything = gathered[...]
    own = dot(inverse[...], everything)
    x = [dot(halo.inverse(message), everything)] + [own[j * ncf : (j + 1) * ncf] for j in range(subs)]
    results, energy = coarse_products(ncf, x, base, gram)
    for e, share in enumerate(coarse_shares(ncf, results)):
        shares[e * ncf : (e + 1) * ncf] = share
        solution[e * ncf : (e + 1) * ncf] = x[e]
    shares_rounded[...] = shares[...].astype(BF16)
    sums[0:1] = column_sum(load[...] * local[nf:]) + column_sum(coarse[...] * own)
    sums[1:2] = energy


def coarse_image(
    halo, half, crossed_half, inverse, message, shares, base, gram, quadratic, sums_in, energies, sums, solution, gathered
):
    ncf = halo.ncf
    subs = inverse.shape[0] // ncf
    total = gathered.shape[0]
    for place, blocks, start, stop in placed(half, crossed_half):
        gathered[pl.ds(pl.multiple_of(place * subs * ncf, subs * ncf), subs * ncf)] = blocks[start + ncf : stop].astype(F32)
    for place, blocks, start, stop in placed(half, crossed_half):
        before = pl.multiple_of(lax.rem(place * subs * ncf + (total - ncf), total), ncf)
        gathered[pl.ds(before, ncf)] += blocks[start : start + ncf].astype(F32)
    everything = gathered[...]
    own = split_dot(inverse[...], everything)
    x = [split_dot(halo.inverse(message), everything)] + [own[j * ncf : (j + 1) * ncf] for j in range(subs)]
    _, energy = coarse_products(ncf, x, base, gram)
    for e in range(subs + 1):
        solution[e * ncf : (e + 1) * ncf] = x[e]
    sums[0:1] = sums_in[0:1]
    sums[1:2] = sums_in[1:2] + column_sum(energies[...])
    sums[2:3] = quadratic[1:2] + column_sum(shares[...] * solution[...])
    sums[3:4] = quadratic[0:1] + energy


def complete(
    halo, z_local, z_coarse, y_local, y_coarse, rows, basis_high, basis_low, product, z, y, part, back
):
    ncf, nf = halo.ncf, halo.nf
    subs = rows.shape[0] // ncf
    x = [rows_of(y_coarse, e, ncf) for e in range(subs + 1)]
    faces = add_basis(nf, x, basis_high, basis_low, [rows_of(product, e, nf) for e in range(subs + 1)])
    for e in range(1, subs + 1):
        part[(e - 1) * nf : e * nf] = faces[e]
    back[...] = faces[0].astype(BF16)
    for j in range(subs):
        here, beside = slice(j * nf, (j + 1) * nf), slice((j + 1) * nf, (j + 2) * nf)
        for local, coarse, whole in ((z_local, z_coarse, z), (y_local, y_coarse, y)):
            whole[here] = local[beside] + split_dot(rows_of(rows, j, ncf), rows_of(coarse, j + 1, ncf), dot_tn)


def combine(halo, sums, load, z, y, image, part, from_next, solution, residual, solution_here, residual_here, done):
    nf = halo.nf
    subs = load.shape[0] // nf
    a, b, c, d = (sums[k : k + 1] for k in range(4))
    step = a / b
    grow = step * (c / b)
    next_step = (grow - 1.0) / ((d - c * (c / b)) * (step / b))
    s = step + next_step * grow
    t = step * next_step
    copies = []

    def copy_out(here, source, target):
        copies.append(pltpu.make_async_copy(source.at[here], target.at[here], done.at[len(copies)]))
        copies[-1].start()

    for j in range(subs):
        here = slice(j * nf, (j + 1) * nf)
        solution_here[here] = s * z[here] - t * y[here]
        copy_out(pl.ds(j * nf, nf), solution_here, solution)
        last = part[here] + from_next[...].astype(F32) if j == subs - 1 else part[here]
        residual_here[here] = load[here] - s * image[here] + t * last
        copy_out(pl.ds(j * nf, nf), residual_here, residual)
    for copy in copies:
        copy.wait()


def shards(right_side, face_weight, schur, neumann, constraint, coarse_inverse):
    subs, nf = face_weight.shape
    ncf = constraint.shape[0] // subs
    nco = coarse_inverse.shape[1]
    columns = right_side.shape[1]
    halo = Halo(nf, ncf, nco, columns)
    bind = lambda kernel: functools.partial(kernel, halo)
    faces, own = ((subs + 1) * nf, columns), (subs * nf, columns)
    coarse_own, local_rows = (subs * ncf, columns), 2 * subs * ncf
    products = [(faces, F32), (faces, F32), ((8, columns), F32), ((local_rows, columns), F32)]
    semaphores = lambda count: [pltpu.SemaphoreType.DMA((count,))]
    described = lambda array: (array.shape, array.dtype)
    outside = lambda array: pltpu.with_memory_space_constraint(array, pltpu.HBM)
    steps = bits()
    early, late = steps[:-2], steps[-2:-1]

    load, rows, weight, inverse, coarse_rounded, coarse = stage(
        bind(prepare),
        [described(right_side), described(constraint), described(face_weight), described(coarse_inverse)]
        + [(coarse_own, BF16), (coarse_own, F32)],
        *map(outside, (right_side, constraint, face_weight, coarse_inverse)), scratch=semaphores(subs + 3), fetched=4,
    )
    (message,) = stage(
        bind(halo_message), [((halo.height, columns), BF16)], load, weight, rows, inverse,
        scratch=[pltpu.VMEM((halo.weight_count, columns), F32)],
    )
    tied = after(tuple(map(outside, (neumann, schur))), message)
    neumann, schur = stage(
        bind(fetch), [described(array) for array in tied], *tied, scratch=semaphores(2), fetched=2
    )
    message = shifted(message, 1)
    half = gather_half(coarse_rounded, early[:1], neumann)
    outside_faces = [((2 * nf, columns), F32)] + 2 * [((nf, columns), BF16)]
    inside_faces = [(((subs - 1) * nf, columns), F32)]
    outer, near, far = stage(bind(load_outer), outside_faces, load, weight, message, neumann)
    (inner,) = stage(bind(load_inner), inside_faces, load, weight, after(message, far), neumann)
    half = gather_half(half, early[1:], far)
    far, near = far_block(far), crossed(near, 1)
    long, wide = ((2 * subs * nf, 2 * ncf), BF16), ((local_rows, 2 * nf), BF16)
    basis_high, basis_low, turned_high, turned_low, gram = stage(
        bind(static_basis), [long, long, wide, wide, ((local_rows, LANES), F32)], schur, after(message, inner), rows
    )
    half = gather_half(half, late, gram)
    crossed_half = crossed(half, 1)
    share_rows, sum_rows = ((subs + 1) * ncf, columns), ((8, columns), F32)
    z_local, shares_rounded, shares, z_coarse, sums = stage(
        bind(coarse_load), [(faces, F32), (share_rows, BF16), (share_rows, F32), (share_rows, F32), sum_rows],
        load, outer, inner, near, far, weight, message, turned_high, turned_low, half, crossed_half, inverse, coarse, gram,
        scratch=[pltpu.VMEM((local_rows, columns), F32), pltpu.VMEM((nco, columns), BF16)],
    )
    outer, near, far, sums = stage(
        bind(schur_outer), outside_faces + [sum_rows], z_local, schur, basis_high, basis_low, z_coarse, sums
    )
    inner, energies = stage(
        bind(schur_inner), inside_faces + [((subs - 1, columns), F32)], z_local, schur, basis_high, basis_low, z_coarse
    )
    half = gather_half(shares_rounded, early[:1], inner)
    far, near = far_block(far), crossed(near, 1)
    operands = outer, inner, near, far, weight, message, neumann
    outer, near, far = stage(bind(image_outer), outside_faces, *operands)
    image, inner = stage(bind(image_inner), [(own, F32)] + inside_faces, after(operands[0], far), *operands[1:])
    half = gather_half(half, early[1:], far)
    far, near = far_block(far), crossed(near, 1)
    half = gather_half(half, late, near, far, inner)
    crossed_half = crossed(half, 1)
    outer = after(outer, half)
    y_local, product, quadratic, base = stage(
        bind(schur_image), products, image, outer, inner, near, far, weight, message, schur, turned_high, turned_low
    )
    sums, y_coarse = stage(
        bind(coarse_image), [((4, columns), F32), (share_rows, F32)],
        half, crossed_half, inverse, message, shares, base, gram, quadratic, sums, energies,
        scratch=[pltpu.VMEM((nco, columns), F32)],
    )
    z, y, part, back = stage(
        bind(complete), [(own, F32), (own, F32), (own, F32), ((nf, columns), BF16)],
        z_local, z_coarse, y_local, y_coarse, rows, basis_high, basis_low, product,
    )
    for k, bit in enumerate(early + steps[-1:] + late):
        sums = sums + after(crossed(sums, bit), y)
        if k == len(early) - 1:
            back = shifted(after(back, sums), -1)
    return stage(
        bind(combine), [(own, F32), (own, F32)], sums, load, z, y, image, part, back,
        scratch=[pltpu.VMEM(own, F32)] * 2 + semaphores(2 * subs), outputs=pltpu.HBM,
    )


def solution(mesh):
    specs = P(("parts", AXIS), None)
    return jax.shard_map(shards, mesh=mesh, in_specs=(specs,) * 6, out_specs=(specs, specs), check_vma=False)
```
